32 devices in a mesh: dp: 4 (over z), mp: 8 (over y, x, core).
Axes of the slice: x: 2, y: 2, z: 4, core: 2. Of those that a mesh axis runs over, the one named last changes fastest.
Arguments:
- tokens: bfloat16 [8192, 512], P(('dp', 'mp')), may hold values from -6 to 6
- cotangent: bfloat16 [8192, 512], P(('dp', 'mp')), may hold values from -6 to 6
- carried: float32 [32, 8, 2, 64, 256], P('dp', 'mp'), may hold values from -0.625 to 0.625
- frequencies: float32 [8, 128, 64], replicated, may hold values from -0.625 to 0.625
- vectors: float32 [3, 512], replicated, may hold values from 0.75 to 7, as said below
- vectors_first: float32 [3, 512], replicated, may hold values from -0.0009765625 to 0.0009765625
- vectors_second: float32 [3, 512], replicated, may hold values from 1.3198772e-09 to 2.1118035e-08
- mix_in: float32 [512, 8, 256], P(None, 'mp'), as said below
- mix_in_first: float32 [512, 8, 256], P(None, 'mp'), may hold values from -0.00036621094 to 0.00036621094
- mix_in_second: float32 [512, 8, 256], P(None, 'mp'), may hold values from 1.4665302e-10 to 2.3464484e-09
- mix_out: float32 [512, 512], P('mp'), may hold values from -0.875 to 0.875
- mix_out_first: float32 [512, 512], P('mp'), may hold values from -0.00036621094 to 0.00036621094
- mix_out_second: float32 [512, 512], P('mp'), may hold values from 1.4665302e-10 to 2.3464484e-09
- ffn_up: float32 [512, 2048], P(None, 'mp'), as said below
- ffn_up_first: float32 [512, 2048], P(None, 'mp'), may hold values from -0.00036621094 to 0.00036621094
- ffn_up_second: float32 [512, 2048], P(None, 'mp'), may hold values from 1.4665302e-10 to 2.3464484e-09
- ffn_down: float32 [2048, 512], P('mp'), may hold values from -0.125 to 0.125
- ffn_down_first: float32 [2048, 512], P('mp'), may hold values from -0.00036621094 to 0.00036621094
- ffn_down_second: float32 [2048, 512], P('mp'), may hold values from 1.4665302e-10 to 2.3464484e-09
Outputs:
- block_out: bfloat16 [8192, 512], P(('dp', 'mp'))
- final_carried: float32 [32, 8, 2, 64, 256], P('dp', 'mp')
- token_grad: float32 [8192, 512], P(('dp', 'mp'))
- carried_grad: float32 [32, 8, 2, 64, 256], P('dp', 'mp')
- grad_norm: float32 [], replicated
- vectors_first_new: float32 [3, 512], replicated
- vectors_second_new: float32 [3, 512], replicated
- vectors_new: float32 [3, 512], replicated
- mix_in_first_new: float32 [512, 8, 256], P(None, 'mp')
- mix_in_second_new: float32 [512, 8, 256], P(None, 'mp')
- mix_in_new: float32 [512, 8, 256], P(None, 'mp')
- mix_in_low: bfloat16 [512, 8, 256], P(None, 'mp')
- mix_out_first_new: float32 [512, 512], P('mp')
- mix_out_second_new: float32 [512, 512], P('mp')
- mix_out_new: float32 [512, 512], P('mp')
- mix_out_low: bfloat16 [512, 512], P('mp')
- ffn_up_first_new: float32 [512, 2048], P(None, 'mp')
- ffn_up_second_new: float32 [512, 2048], P(None, 'mp')
- ffn_up_new: float32 [512, 2048], P(None, 'mp')
- ffn_up_low: bfloat16 [512, 2048], P(None, 'mp')
- ffn_down_first_new: float32 [2048, 512], P('mp')
- ffn_down_second_new: float32 [2048, 512], P('mp')
- ffn_down_new: float32 [2048, 512], P('mp')
- ffn_down_low: bfloat16 [2048, 512], P('mp')
The draws below stay inside these ranges and needn't reach their ends.
Inputs may be any that keep to these rules, and one draw needn't show every extreme that they name: `vectors`: rows 0 and 1 are gains near 1; row 2, read as [8, 64], is the gate's bias. `mix_in`: a weight matrix. `ffn_up`: a weight matrix.
All inputs are finite; a program needn't handle non-finite values.
Results may differ from the reference program's by a relative error of at most 0.0095.
Values may be sent and summed in bfloat16 or wider, within the bound.
A program may use at most 128 MiB of HBM per device.

```python
import math
from functools import partial
import jax
import jax.numpy as jnp
from jax import lax

D = 512
HEADS = 8
HD = 64
RF = 128
FF = 2048
SEQ_DEV = 1
LEN = 256
BLOCK = 64
STEP = 10
SEQS = 32
TOKENS = 8192
N_DP = 4
N_MP = 8


def draw_vectors(key, part):
    key = jax.random.fold_in(key, 11)
    gain_key, bias_key = jax.random.split(key)
    gain_rows = jax.random.uniform(gain_key, (2, D), jnp.float32, 0.75, 1.25)
    bias_row = jax.random.uniform(bias_key, (1, D), jnp.float32, 1.0, 7.0)
    return jnp.concatenate([gain_rows, bias_row], axis=0)


def draw_mix_in(key, part):
    key = jax.random.fold_in(key, 23)
    entries = jax.random.normal(key, (D, HEADS, 4, HD), jnp.float32) * D ** (-0.5)
    rising = 1.0 + 2.0 * jnp.arange(HEADS, dtype=jnp.float32) / max(HEADS - 1, 1)
    ones_row = jnp.ones((HEADS,), jnp.float32)
    slot_scale = jnp.stack([ones_row, ones_row, rising, 0.5 * ones_row], axis=1)
    return (entries * slot_scale[None, :, :, None]).reshape(D, HEADS, 4 * HD)


def draw_ffn_up(key, part):
    key = jax.random.fold_in(key, 37)
    rising = 1.0 + 2.0 * jnp.arange(FF, dtype=jnp.float32) / FF
    return jax.random.normal(key, (D, FF), jnp.float32) * D ** (-0.5) * rising[None, :]


def levels(rng, extent, cuts, smallest, largest):
    def one(axis_at, blocks):
        draws = jax.random.uniform(jax.random.fold_in(jax.random.fold_in(rng, 6), axis_at), (blocks,), jnp.float32, smallest / len(cuts), largest / len(cuts))
        return jnp.repeat(jnp.exp(draws), extent[axis_at] // blocks).reshape((-1,) + (1,) * (len(extent) - axis_at - 1))

    gain = one(*cuts[0])
    for cut in cuts[1:]:
        gain = gain * one(*cut)
    return gain


def centred(stream_key, extent, deviation, most, cuts=(), held_as=jnp.bfloat16):
    values = jax.random.normal(stream_key, extent, jnp.float32) * deviation
    if len(cuts) > 0:
        values = levels(stream_key, extent, cuts, -0.22, 0.18) * values
    return jnp.clip(values, min=-most, max=most).astype(held_as)


def setup_inputs(seed: int = 0) -> dict:
    key_of = jax.random.split(jax.random.key(seed), 20)
    tokens = centred(key_of[0], (TOKENS, D), 1.0, 6.0, ((0, 32),))
    cotangent = centred(key_of[1], (TOKENS, D), 1.0, 6.0, ((0, 32),))
    carried = centred(key_of[2], (SEQS, HEADS, 2, HD, 2 * RF), 0.1, 0.625, ((0, 4), (1, 8)), jnp.float32)
    frequencies = centred(key_of[3], (HEADS, RF, HD), 0.1, 0.625, (), jnp.float32)
    vectors = draw_vectors(jax.random.fold_in(key_of[19], 71), 0)
    vectors_first = centred(key_of[5], (3, D), (0.33 * (5 * D * HEADS * HD + 2 * D * FF + 3 * D) ** -0.5), 0.0009765625, (), jnp.float32)
    vectors_second = jnp.clip(jnp.exp(jax.random.uniform(key_of[6], (3, D), jnp.float32, math.log(1.3198772075284637e-09), math.log(2.111803532045542e-08))), 1.3198772075284637e-09, 2.111803532045542e-08)
    mix_in = draw_mix_in(jax.random.fold_in(key_of[19], 71), 0)
    mix_in_first = centred(key_of[8], (D, HEADS, 4 * HD), (0.11 * (5 * D * HEADS * HD + 2 * D * FF + 3 * D) ** -0.5), 0.00036621094, ((1, 8),), jnp.float32)
    mix_in_second = jnp.clip(jnp.exp(math.log(2.346448368939491e-09) - 2.7725887 * jax.random.uniform(key_of[9], (D, HEADS, 4 * HD), jnp.float32) ** levels(key_of[9], (D, HEADS, 4 * HD), ((1, 8),), -0.2, 0.2)), 1.466530230587182e-10, 2.346448368939491e-09)
    mix_out = centred(key_of[10], (HEADS * HD, D), (HEADS * HD // 10) ** -0.5, 0.875, ((0, 8),), jnp.float32)
    mix_out_first = centred(key_of[11], (HEADS * HD, D), (0.11 * (5 * D * HEADS * HD + 2 * D * FF + 3 * D) ** -0.5), 0.00036621094, ((0, 8),), jnp.float32)
    mix_out_second = jnp.clip(jnp.exp(math.log(2.346448368939491e-09) - 2.7725887 * jax.random.uniform(key_of[12], (HEADS * HD, D), jnp.float32) ** levels(key_of[12], (HEADS * HD, D), ((0, 8),), -0.2, 0.2)), 1.466530230587182e-10, 2.346448368939491e-09)
    ffn_up = draw_ffn_up(jax.random.fold_in(key_of[19], 71), 0)
    ffn_up_first = centred(key_of[14], (D, FF), (0.11 * (5 * D * HEADS * HD + 2 * D * FF + 3 * D) ** -0.5), 0.00036621094, ((1, 8),), jnp.float32)
    ffn_up_second = jnp.clip(jnp.exp(math.log(2.346448368939491e-09) - 2.7725887 * jax.random.uniform(key_of[15], (D, FF), jnp.float32) ** levels(key_of[15], (D, FF), ((1, 8),), -0.2, 0.2)), 1.466530230587182e-10, 2.346448368939491e-09)
    ffn_down = centred(key_of[16], (FF, D), FF ** -0.5, 0.125, ((0, 8),), jnp.float32)
    ffn_down_first = centred(key_of[17], (FF, D), (0.11 * (5 * D * HEADS * HD + 2 * D * FF + 3 * D) ** -0.5), 0.00036621094, ((0, 8),), jnp.float32)
    ffn_down_second = jnp.clip(jnp.exp(math.log(2.346448368939491e-09) - 2.7725887 * jax.random.uniform(key_of[18], (FF, D), jnp.float32) ** levels(key_of[18], (FF, D), ((0, 8),), -0.2, 0.2)), 1.466530230587182e-10, 2.346448368939491e-09)
    return dict(tokens=tokens, cotangent=cotangent, carried=carried, frequencies=frequencies, vectors=vectors, vectors_first=vectors_first, vectors_second=vectors_second, mix_in=mix_in, mix_in_first=mix_in_first, mix_in_second=mix_in_second, mix_out=mix_out, mix_out_first=mix_out_first, mix_out_second=mix_out_second, ffn_up=ffn_up, ffn_up_first=ffn_up_first, ffn_up_second=ffn_up_second, ffn_down=ffn_down, ffn_down_first=ffn_down_first, ffn_down_second=ffn_down_second)


@jax.custom_vjp
def low(v):
    return lax.optimization_barrier(v.astype(jnp.bfloat16)).astype(jnp.float32)

@jax.custom_vjp
def low_back(v):
    return v

def low_keep(v):
    return (low(v), None)

def low_pass(kept, grad):
    return (grad,)

def back_keep(v):
    return (v, None)

def back_low(kept, grad):
    return (low(grad),)
low.defvjp(low_keep, low_pass)
low_back.defvjp(back_keep, back_low)
highest = lax.Precision.HIGHEST
norm_eps = 1e-06
den_floor = 0.25
clip_bound = 1.0
beta_one = 0.9
beta_two = 0.999
adam_eps = 1e-08
decay_rate = 0.1
rate_matrix = 0.05
rate_vector = 0.6

def features(inputs, frequencies):
    angles = jnp.dot(inputs, frequencies.T, precision=highest)
    return jnp.concatenate([jnp.sin(angles), jnp.cos(angles)], axis=-1) * frequencies.shape[0] ** (-0.5)

def mix_block(carried_in, block_in, frequencies):
    queries, key_rows, value_rows, gate_pre = block_in
    phi_query = features(queries, frequencies)
    phi_key = features(key_rows, frequencies)
    log_keep = -jax.nn.softplus(-gate_pre)
    writes = jax.nn.sigmoid(-gate_pre)
    cumulative = jnp.cumsum(log_keep, axis=0)
    positions = jnp.arange(queries.shape[0])
    causal = (positions[:, None] >= positions[None, :])[:, :, None]
    log_gaps = cumulative[:, None, :] - cumulative[None, :, :]
    decays = jnp.where(causal, jnp.exp(jnp.where(causal, log_gaps, 0.0)), 0.0)
    scores = jnp.dot(phi_query, phi_key.T, precision=highest)
    weights = decays * scores[:, :, None]
    written = writes * value_rows
    numerator = jnp.einsum('tsc,sc->tc', weights, written, precision=highest)
    denominator = jnp.einsum('tsc,sc->tc', weights, writes, precision=highest)
    opening = jnp.exp(cumulative)
    numerator = numerator + opening * jnp.dot(phi_query, carried_in[0].T, precision=highest)
    denominator = denominator + opening * jnp.dot(phi_query, carried_in[1].T, precision=highest)
    output = numerator * lax.rsqrt(denominator * denominator + den_floor)
    remaining = jnp.exp(cumulative[-1][None, :] - cumulative)
    kept_all = jnp.exp(cumulative[-1])[:, None]
    new_sum = kept_all * carried_in[0] + jnp.dot((remaining * written).T, phi_key, precision=highest)
    new_norm = kept_all * carried_in[1] + jnp.dot((remaining * writes).T, phi_key, precision=highest)
    return (jnp.stack([new_sum, new_norm]), output)

def mix_sequence(queries, key_rows, value_rows, gate_pre, frequencies, carried_in):
    block_count = queries.shape[0] // BLOCK

    def split_blocks(whole_seq):
        return whole_seq.reshape(block_count, BLOCK, whole_seq.shape[-1])
    step_fn = jax.checkpoint(partial(mix_block, frequencies=frequencies))
    final_state, outputs = lax.scan(step_fn, carried_in, (split_blocks(queries), split_blocks(key_rows), split_blocks(value_rows), split_blocks(gate_pre)))
    return (outputs.reshape(queries.shape), final_state)

def mixer_all(projected, gate_bias, frequencies, carried_in):
    head_dim = gate_bias.shape[-1]
    pieces = jnp.transpose(projected.reshape(projected.shape[:3] + (4, head_dim)), (3, 0, 2, 1, 4))
    gate_input = pieces[3] + gate_bias[None, :, None, :]
    per_head = jax.vmap(mix_sequence, in_axes=(0, 0, 0, 0, 0, 0))
    per_seq = jax.vmap(per_head, in_axes=(0, 0, 0, 0, None, 0))
    outputs, final_state = per_seq(pieces[0], pieces[1], pieces[2], gate_input, frequencies, carried_in)
    outputs = jnp.transpose(outputs, (0, 2, 1, 3))
    return (outputs.reshape(-1, outputs.shape[2] * head_dim), final_state)

def rms_scale(inputs):
    return lax.rsqrt(lax.optimization_barrier(jnp.mean(inputs * inputs, axis=-1, keepdims=True)) + norm_eps)

def adam_update(param, grad, first, second, rate, decay):
    first_new = beta_one * first + (1.0 - beta_one) * grad
    second_new = beta_two * second + (1.0 - beta_two) * grad * grad
    first_hat = first_new / (1.0 - beta_one ** STEP)
    second_hat = second_new / (1.0 - beta_two ** STEP)
    param_new = param - rate * (first_hat / (jnp.sqrt(second_hat) + adam_eps) + decay * param)
    return (first_new, second_new, param_new)

def reference(tokens, cotangent, carried, frequencies, vectors, vectors_first, vectors_second, mix_in, mix_in_first, mix_in_second, mix_out, mix_out_first, mix_out_second, ffn_up, ffn_up_first, ffn_up_second, ffn_down, ffn_down_first, ffn_down_second):
    group = SEQ_DEV * N_MP
    group_rows = group * LEN
    params = (vectors, mix_in, mix_out, ffn_up, ffn_down)

    def layer(weights_in, residual, carried_in):
        vector_rows, in_mat, out_mat, up_mat, down_mat = weights_in
        normed_first = low(residual * rms_scale(residual) * vector_rows[0])
        projected = low_back(jnp.dot(normed_first, low(in_mat.reshape(D, 4 * HEADS * HD)), precision=highest))
        mixed, final_state = mixer_all(projected.reshape(group, LEN, HEADS, 4 * HD), vector_rows[2].reshape(HEADS, HD), frequencies, carried_in)
        attended = low_back(jnp.dot(low(mixed), low(out_mat), precision=highest))
        middle = residual + attended
        normed_second = low(middle * rms_scale(middle) * vector_rows[1])
        pre_act = low_back(jnp.dot(normed_second, low(up_mat), precision=highest))
        hidden = low(jax.nn.gelu(pre_act, approximate=True))
        return (middle + jnp.dot(hidden, low(down_mat), precision=highest), final_state)

    def one_group(running, inputs):
        group_tokens, group_cot, group_carried = inputs
        (output, final_state), layer_back = jax.vjp(layer, params, group_tokens.astype(jnp.float32), group_carried)
        grad_params, grad_tokens, grad_carried = layer_back((group_cot.astype(jnp.float32), jnp.zeros_like(final_state)))
        running = jax.tree.map(lambda before, update: before + update, running, grad_params)
        return (running, (output.astype(jnp.bfloat16), final_state, grad_tokens, grad_carried))
    zero_sums = jax.tree.map(lambda leaf_in: jnp.zeros(leaf_in.shape, jnp.float32), params)
    state_shape = (N_DP, group, HEADS, 2, HD, 2 * RF)
    totals, stacked = lax.scan(one_group, zero_sums, (tokens.reshape(N_DP, group_rows, D), cotangent.reshape(N_DP, group_rows, D), carried.reshape(state_shape)))
    square_sum = sum((jnp.sum(grad_leaf * grad_leaf) for grad_leaf in totals))
    grad_norm = jnp.sqrt(square_sum)
    factor = clip_bound / jnp.maximum(grad_norm, clip_bound)
    vec_new = adam_update(vectors, totals[0] * factor, vectors_first, vectors_second, rate_vector, 0.0)
    in_new = adam_update(mix_in, totals[1] * factor, mix_in_first, mix_in_second, rate_matrix, decay_rate)
    out_new = adam_update(mix_out, totals[2] * factor, mix_out_first, mix_out_second, rate_matrix, decay_rate)
    up_new = adam_update(ffn_up, totals[3] * factor, ffn_up_first, ffn_up_second, rate_matrix, decay_rate)
    down_new = adam_update(ffn_down, totals[4] * factor, ffn_down_first, ffn_down_second, rate_matrix, decay_rate)
    full_state = (SEQS, HEADS, 2, HD, 2 * RF)
    return (stacked[0].reshape(TOKENS, D), stacked[1].reshape(full_state), stacked[2].reshape(TOKENS, D), stacked[3].reshape(full_state), grad_norm, vec_new[0], vec_new[1], vec_new[2], in_new[0], in_new[1], in_new[2], in_new[2].astype(jnp.bfloat16), out_new[0], out_new[1], out_new[2], out_new[2].astype(jnp.bfloat16), up_new[0], up_new[1], up_new[2], up_new[2].astype(jnp.bfloat16), down_new[0], down_new[1], down_new[2], down_new[2].astype(jnp.bfloat16))
```

```python
import functools

import jax
import jax.numpy as jnp
from jax import lax
from jax.experimental import pallas as pl
from jax.experimental.pallas import tpu as pltpu
from jax.sharding import PartitionSpec as P

STEP = 10
NORM_EPS = 1e-06
DEN_FLOOR = 0.25
CLIP = 1.0
B1 = 0.9
B2 = 0.999
ADAM_EPS = 1e-08
DECAY = 0.1
RATE_MATRIX = 0.05
RATE_VECTOR = 0.6
MESH = pl.DeviceIdType.MESH
F32 = jnp.float32
BF16 = jnp.bfloat16

SIN = (9.99999996e-01, -1.66666578e-01, 8.33304727e-03, -1.98087928e-04, 2.60457914e-06)
COS = (1.0, -4.99999993e-01, 4.16666357e-02, -1.38883546e-03, 2.47598090e-05, -2.60452002e-07)
PI_A, PI_B, PI_C = 3.140625, 0.0009675025939941406, 1.5099579897537296e-07


def mm(a, b):
    return jnp.dot(a, b, preferred_element_type=F32)


def mm_nt(a, b):
    return lax.dot_general(a, b, (((1,), (1,)), ((), ())), preferred_element_type=F32)


def mm_tn(a, b):
    return lax.dot_general(a, b, (((0,), (0,)), ((), ())), preferred_element_type=F32)


def horner(coefs, y):
    acc = jnp.full_like(y, coefs[-1])
    for coef in coefs[-2::-1]:
        acc = acc * y + coef
    return acc


def sincos(x):
    turns = jnp.floor(x * 0.3183098861837907 + 0.5)
    r = ((x - turns * PI_A) - turns * PI_B) - turns * PI_C
    sign = 1.0 - 2.0 * (turns - 2.0 * jnp.floor(turns * 0.5))
    y = r * r
    return sign * (r * horner(SIN, y)), sign * horner(COS, y)


def rms_scale(x):
    return lax.rsqrt(jnp.mean(x * x, axis=-1, keepdims=True) + NORM_EPS)


def norm_back(grad, unit, scale, gain):
    e = grad * gain
    return scale * (e - unit * jnp.mean(e * unit, axis=-1, keepdims=True))


def xor(a, bits):
    out = a
    step = 1
    while step <= bits:
        if bits & step:
            out = out + step - 2 * step * (lax.div(a, step) % 2)
        step *= 2
    return out


def tree_sum(terms):
    terms = list(terms)
    if len(terms) == 1:
        return terms[0]
    half = len(terms) // 2
    return tree_sum(terms[:half]) + tree_sum(terms[half:])


def halves(a):
    return a[:, :128], a[:, 128:]


def pair_cat(a):
    return jnp.concatenate([a, a], axis=1)


def layer_kernel(cfg, *refs):
    names = cfg["names"]
    S = dict(zip(names, refs))
    ndp, nq, T, D = cfg["ndp"], cfg["nq"], cfg["T"], cfg["D"]
    nlev = cfg["nlev"]
    FH = cfg["FH"]
    npair = nq // 2
    rows2 = 2 * T
    me_dp = lax.axis_index("dp")
    m = lax.axis_index("mp")
    c = m % 2
    q = lax.div(m, 2)
    sib = {"mp": q * 2 + (1 - c)}
    ssem, rsem = S["ssem"], S["rsem"]
    sem_of = {}

    def sem(key):
        return sem_of.setdefault(key, len(sem_of))

    def peer(i):
        return {"mp": xor(q, i) * 2 + c}

    def dpeer(k):
        return {"dp": xor(me_dp, k)}

    def copy(key, src, dst, dev):
        k = sem(key)
        return pltpu.make_async_remote_copy(
            src_ref=src, dst_ref=dst, send_sem=ssem.at[k], recv_sem=rsem.at[k],
            device_id=dev, device_id_type=MESH)

    barrier = pltpu.get_barrier_semaphore()
    count = 0
    for r in range(1, 2 * nq):
        pl.semaphore_signal(barrier, inc=1, device_id={"mp": xor(m, r)}, device_id_type=MESH)
        count += 1
    for k in range(1, ndp):
        pl.semaphore_signal(barrier, inc=1, device_id=dpeer(k), device_id_type=MESH)
        count += 1

    XT, XC = S["XT"], S["XC"]
    Win, Wout, Wup, Wdown = S["Win"], S["Wout"], S["Wup"], S["Wdown"]
    tok, cot = S["tok"], S["cot"]
    w_in = S["w_in"]
    Win[0] = jnp.concatenate(
        [w_in[pl.ds(0, D, 2), :], w_in[pl.ds(1, D, 2), :]], axis=1).astype(BF16)
    CS = S["CS"]
    nseq = 2 * nq
    CS[...] = S["carried"][:, 0].astype(BF16)
    pl.semaphore_wait(barrier, count)

    sends = []

    def go(cp):
        cp.start()
        sends.append(cp)
        return cp

    cp_tok = go(copy("tok", tok, XT.at[c], sib))
    cp_in = [None] + [go(copy(("in", i), Win.at[0], Win.at[i], peer(i))) for i in range(1, nq)]
    Cin = S["Cin"]
    cp_car = [None] + [
        go(copy(("car", i), CS.at[pl.ds(2 * xor(q, i), 2)], Cin.at[i], peer(i)))
        for i in range(1, nq)]
    cp_cot = go(copy("cot", cot, XC.at[pl.ds(c * T, T)], sib))
    Wout[0] = S["w_out"][...].astype(BF16)
    Wup[0] = S["w_up"][...].astype(BF16)
    Wdown[0] = S["w_down"][...].astype(BF16)
    cp_out = [None] + [go(copy(("out", i), Wout.at[0], Wout.at[i], peer(i))) for i in range(1, nq)]
    cp_up = [None]
    cp_down = [None]
    for i in range(1, nq):
        cp_up.append(go(copy(("up", i), Wup.at[0], Wup.at[i], peer(i))))
        cp_down.append(go(copy(("down", i), Wdown.at[0], Wdown.at[i], peer(i))))

    XT[c] = tok[...]
    XC[pl.ds(pl.multiple_of(c * T, T), T), :] = cot[...]
    Cin[0] = CS[pl.ds(2 * q, 2)]

    vec = S["vec"]
    gain_a = vec[0:1, :]
    gain_f = vec[1:2, :]
    row_i = lax.broadcasted_iota(jnp.int32, (T, T), 0)
    col_i = lax.broadcasted_iota(jnp.int32, (T, T), 1)
    gap = row_i ^ col_i
    lower = row_i > col_i
    upper = row_i < col_i
    LV, MK, MT, TRI = S["LV"], S["MK"], S["MT"], S["TRI"]
    code = jnp.where(row_i == col_i, 0.0, -1.0)
    MK[0] = jnp.where(row_i == col_i, 1.0, 0.0).astype(BF16)
    MT[0] = jnp.where(row_i == col_i, 1.0, 0.0).astype(BF16)
    for lv in range(nlev):
        h = 1 << lv
        here = (gap >= h) & (gap < 2 * h)
        code = jnp.where(lower & here, float(lv + 1), code)
        MK[lv + 1] = jnp.where(lower & here, 1.0, 0.0).astype(BF16)
        MT[lv + 1] = jnp.where(upper & here, 1.0, 0.0).astype(BF16)
        bit = (row_i & h) != 0
        same = gap < h
        take = same & ((bit & (col_i >= row_i)) | ((~bit) & (col_i < row_i)))
        TRI[:, lv * T:(lv + 1) * T] = jnp.where(take, 1.0, 0.0).astype(BF16)
    TRI[:, nlev * T:(nlev + 1) * T] = jnp.where(col_i >= row_i, 1.0, 0.0).astype(BF16)
    LV[...] = code
    VEC = S["VEC"]
    VEC[...] = jnp.zeros_like(VEC)
    WBH, WBL = S["WBH"], S["WBL"]
    WBH[...] = jnp.zeros_like(WBH)
    WBL[...] = jnp.zeros_like(WBL)
    for i in range(nq):
        freq = S["freq"][2 * xor(q, i) + c]
        high = freq.astype(BF16)
        rest = (freq - high.astype(F32)).astype(BF16)
        WBH[i, 0:64, 0:128] = high
        WBH[i, 64:128, 128:256] = high
        WBL[i, 0:64, 0:128] = rest
        WBL[i, 64:128, 128:256] = rest
    SZ = S["SZ"]
    SZ[...] = jnp.zeros_like(SZ)

    NA = S["NA"]
    cp_tok.wait_recv()
    for s in range(2):
        x = XT[s].astype(F32)
        NA[s * T:(s + 1) * T, :] = (x * rms_scale(x) * gain_a).astype(BF16)

    PH, TV = S["PH"], S["TV"]
    for i in range(nq):
        if i > 0:
            cp_in[i].wait_recv()
        bias = S["bias"][pl.ds(2 * xor(q, i) + c, 1), :]

        def head(s, _, i=i, bias=bias):
            rows = pl.ds(pl.multiple_of(s * T, T), T)
            pr = mm(NA[rows, :], Win[i])
            t0, t1 = halves(pr)
            TV[i, rows, :] = t1 + bias
            high = t0.astype(BF16)
            rest = (t0 - high.astype(F32)).astype(BF16)
            ang = mm(high, WBH[i]) + (mm(rest, WBH[i]) + mm(high, WBL[i]))
            sin, cos = sincos(ang)
            PH[i, rows, 0:128] = sin[:, :128].astype(BF16)
            PH[i, rows, 128:256] = cos[:, :128].astype(BF16)
            PH[i, rows, 256:384] = sin[:, 128:].astype(BF16)
            PH[i, rows, 384:512] = cos[:, 128:].astype(BF16)
            return 0

        lax.fori_loop(0, 2, head, 0)

    lane = lax.broadcasted_iota(jnp.int32, (T, 128), 1)
    first = lane < 64
    row = lax.broadcasted_iota(jnp.int32, (T, 128), 0)
    lane_b = lax.broadcasted_iota(jnp.int32, (T, 256), 1)
    first_b = (lane_b % 128) < 64
    inv_feat = 1.0 / 128.0
    inv_root = 128.0 ** (-0.5)

    def swap(a, h):
        if h < 8:
            return jnp.where((row & h) != 0, pltpu.roll(a, h, 0), pltpu.roll(a, T - h, 0))
        parts = []
        for b in range(T // (2 * h)):
            parts.append(a[(2 * b + 1) * h:(2 * b + 2) * h])
            parts.append(a[2 * b * h:(2 * b + 1) * h])
        return jnp.concatenate(parts, axis=0)

    VV, KK, WW, PP, UU, YY = S["VV"], S["KK"], S["WW"], S["PP"], S["UU"], S["YY"]
    ND, NDL, MX = S["ND"], S["NDL"], S["MX"]
    FS = S["FS"]

    def split_rows(y):
        z = jnp.zeros_like(y)
        return jnp.concatenate([jnp.where(first_b, y, z), jnp.where(first_b, z, y)], axis=0)

    for j in range(npair):
        i0, i1 = 2 * j, 2 * j + 1
        for i in (i0, i1):
            if i > 0:
                cp_car[i].wait_recv()

        def forward(s, _, i0=i0, i1=i1, j=j):
            rows = pl.ds(pl.multiple_of(s * T, T), T)
            for k, i in enumerate((i0, i1)):
                SZ[j, s, k * 64:k * 64 + 64, k * 256:k * 256 + 256] = Cin[i, s, 0]
                SZ[j, s, 128 + k * 64:192 + k * 64, k * 256:k * 256 + 256] = Cin[i, s, 1]
            ta, tb = TV[i0, rows, :], TV[i1, rows, :]
            value = jnp.where(first, ta, pltpu.roll(tb, 64, 1))
            gate = jnp.where(first, pltpu.roll(ta, 64, 1), tb)
            small = jnp.exp(-jnp.abs(gate))
            big = 1.0 / (1.0 + small)
            rest = small * big
            keep = jnp.where(gate >= 0, big, rest)
            write = jnp.where(gate >= 0, rest, big)
            written = write * value
            VV[j, rows, :] = value
            KK[j, rows, :] = keep
            WW[j, rows, :] = write
            scores = [
                (mm_nt(PH[i, rows, 0:256], PH[i, rows, 256:512]) * inv_feat).astype(BF16)
                for i in (i0, i1)]
            total, pre, suf = keep, keep, jnp.ones_like(keep)
            y = jnp.concatenate([written, write], axis=1).astype(BF16)
            left = jnp.concatenate([sc * MK[0] for sc in scores], axis=1)
            acc = mm(left, split_rows(y))
            for lv in range(nlev):
                h = 1 << lv
                if lv > 0:
                    y = jnp.concatenate([suf * written, suf * write], axis=1).astype(BF16)
                YY[j, s, lv] = y
                PP[j, s, lv] = pre.astype(BF16)
                UU[j, s, lv] = suf.astype(BF16)
                left = jnp.concatenate([sc * MK[lv + 1] for sc in scores], axis=1)
                nd = mm(left, split_rows(y)) * pair_cat(pre)
                acc = acc + nd
                NDL[j, s, lv] = nd.astype(BF16)
                other = swap(total, h)
                upper_half = (row & h) != 0
                pre = jnp.where(upper_half, pre * other, pre)
                suf = jnp.where(upper_half, suf, suf * other)
                total = total * other
            PP[j, s, nlev] = pre.astype(BF16)
            phq = jnp.concatenate([PH[i, rows, 0:256] for i in (i0, i1)], axis=1)
            phk = jnp.concatenate([PH[i, rows, 256:512] for i in (i0, i1)], axis=1)
            nd = mm_nt(phq, SZ[j, s]) * (pair_cat(pre) * inv_root)
            NDL[j, s, nlev] = nd.astype(BF16)
            acc = acc + nd
            ND[j, s] = acc
            num, den = halves(acc)
            MX[rows, j * 128:(j + 1) * 128] = (
                num * lax.rsqrt(den * den + DEN_FLOOR)).astype(BF16)
            y = jnp.concatenate([suf * written, suf * write], axis=1).astype(BF16)
            new = mm_tn(y, phk) * inv_root
            last = jnp.transpose(pre[T - 128:, :], (1, 0))[:, 127:128]
            for k, i in enumerate((i0, i1)):
                kept = last[k * 64:k * 64 + 64, :]
                for z in range(2):
                    block = new[z * 128 + k * 64:z * 128 + k * 64 + 64, k * 256:k * 256 + 256]
                    FS[i, s, z] = (kept * Cin[i, s, z].astype(F32) + block).astype(BF16)
            return 0

        lax.fori_loop(0, 2, forward, 0)

    FR = S["FR"]
    cp_fin = [None] + [
        go(copy(("fin", i), FS.at[i], FR.at[pl.ds(2 * q, 2)], peer(i))) for i in range(1, nq)]
    FR[pl.ds(2 * q, 2)] = FS[0]

    AP, AQ, MID, NF = S["AP"], S["AQ"], S["MID"], S["NF"]
    for i in range(1, nq):
        cp_out[i].wait_recv()
    wout = jnp.concatenate([Wout[i] for i in range(nq)], axis=0)
    AP[...] = mm(MX[...], wout)
    cp_att = go(copy("att", AP, AQ, sib))
    cp_att.wait_recv()
    for s in range(2):
        rows = slice(s * T, (s + 1) * T)
        middle = XT[s].astype(F32) + (AP[rows, :] + AQ[rows, :])
        MID[rows, :] = middle
        NF[rows, :] = (middle * rms_scale(middle) * gain_f).astype(BF16)

    FO, DN = AP, S["DN"]
    cp_att.wait_send()
    cp_cot.wait_recv()
    NFT, CT = S["NFT"], XC
    NFT[...] = jnp.transpose(NF[...], (1, 0))
    GUo, GDo, GUs, GDs, GUr, GDr = (S[n] for n in ("GUo", "GDo", "GUs", "GDs", "GUr", "GDr"))
    cp_gu, cp_gd = [None], [None]
    for i in range(nq):
        if i > 0:
            cp_up[i].wait_recv()
            cp_down[i].wait_recv()
        up, down = Wup[i], Wdown[i]
        pre = mm(NF[...], up)
        square = pre * pre
        th = jnp.tanh(0.7978845608028654 * (pre + 0.044715 * pre * square))
        hidden = (0.5 * pre * (1.0 + th)).astype(BF16)
        slope = 0.5 * (1.0 + th) + 0.5 * pre * (1.0 - th * th) * (
            0.7978845608028654 * (1.0 + 0.134145 * square))
        d_pre = (mm_nt(CT[...], down) * slope).astype(BF16)
        fo = mm(hidden, down)
        dn = mm_nt(d_pre, up)
        if i == 0:
            FO[...] = fo
            DN[...] = dn
        else:
            FO[...] += fo
            DN[...] += dn
        gd = mm_tn(hidden, CT[...])
        gu = mm(NFT[...], d_pre)
        if i == 0:
            GUo[...] = gu
            GDo[...] = gd
        else:
            GUs[i - 1] = gu.astype(BF16)
            GDs[i - 1] = gd.astype(BF16)
            cp_gu.append(copy(("gu", i), GUs.at[i - 1], GUr.at[i - 1], peer(i)))
            cp_gd.append(copy(("gd", i), GDs.at[i - 1], GDr.at[i - 1], peer(i)))
            if i == nq - 1:
                continue
            go(cp_gu[i])
            go(cp_gd[i])
    FOR, DNR = S["FOR"], S["DNR"]
    cp_dn = go(copy("dn", DN, DNR, sib))
    cp_fo = go(copy("fo", FO.at[pl.ds((1 - c) * T, T)], FOR, sib))
    go(cp_gu[nq - 1])
    go(cp_gd[nq - 1])
    cp_dn.wait_recv()
    DA, DM, DMI = S["DA"], S["DM"], S["DMI"]
    for s in range(2):
        rows = slice(s * T, (s + 1) * T)
        middle = MID[rows, :]
        scale = rms_scale(middle)
        unit = middle * scale
        grad = DN[rows, :] + DNR[rows, :]
        d_mid = XC[rows, :].astype(F32) + norm_back(grad, unit, scale, gain_f)
        DA[rows, :] = d_mid.astype(BF16)
        gain_grad = jnp.sum(grad * unit, axis=0, keepdims=True)

        @pl.when(c == s)
        def _(gain_grad=gain_grad, d_mid=d_mid):
            DMI[...] = d_mid
            for t in range(D // 128):
                VEC[D // 128 + t:D // 128 + t + 1, :] = gain_grad[:, t * 128:(t + 1) * 128]

    own_rows = pl.ds(pl.multiple_of(c * T, T), T)
    cp_fo.wait_recv()
    S["block_out"][...] = (MID[own_rows, :] + (FO[own_rows, :] + FOR[...])).astype(BF16)
    DM[...] = mm_nt(DA[...], wout)
    GOo, GOs, GOr = S["GOo"], S["GOs"], S["GOr"]
    go_all = mm_tn(MX[...], DA[...])
    GOo[...] = go_all[0:64]
    for i in range(1, nq):
        GOs[i - 1] = go_all[64 * i:64 * i + 64].astype(BF16)
    cp_go = [None] + [
        go(copy(("go", i), GOs.at[i - 1], GOr.at[i - 1], peer(i))) for i in range(1, nq)]

    XL, DPJ, CG = S["XL"], S["DPJ"], S["CG"]
    for j in range(npair):
        i0, i1 = 2 * j, 2 * j + 1

        def backward(s, bias_sum, i0=i0, i1=i1, j=j):
            rows = pl.ds(pl.multiple_of(s * T, T), T)
            dm = DM[rows, j * 128:(j + 1) * 128]
            num, den = halves(ND[j, s])
            r = lax.rsqrt(den * den + DEN_FLOOR)
            d_num = dm * r
            d_den = -(d_num * num) * den * (r * r)
            g = jnp.concatenate([d_num, d_den], axis=1)
            value, keep, write = VV[j, rows, :], KK[j, rows, :], WW[j, rows, :]
            written = write * value
            scores = [
                (mm_nt(PH[i, rows, 256:512], PH[i, rows, 0:256]) * inv_feat).astype(BF16)
                for i in (i0, i1)]
            levels = LV[...]
            z16 = jnp.zeros((T, 256), BF16)
            gb = g.astype(BF16)
            g0, g1 = jnp.where(first_b, gb, z16), jnp.where(first_b, z16, gb)
            left = jnp.concatenate([sc * MT[0] for sc in scores], axis=1)
            ab = mm(left, jnp.concatenate([g0, g1], axis=0))
            y = YY[j, s, 0]
            ds0 = mm_nt(g0, y)
            ds1 = mm_nt(g1, y)
            for lv in range(nlev):
                h = 1 << lv
                pg = (pair_cat(PP[j, s, lv].astype(F32)) * g).astype(BF16)
                g0, g1 = jnp.where(first_b, pg, z16), jnp.where(first_b, z16, pg)
                left = jnp.concatenate([sc * MT[lv + 1] for sc in scores], axis=1)
                part = mm(left, jnp.concatenate([g0, g1], axis=0)) * pair_cat(UU[j, s, lv].astype(F32))
                ab = ab + part
                pa, pb = halves(part)
                from_key = written * pa + write * pb
                oa, ob = halves(g * NDL[j, s, lv].astype(F32))
                XL[lv * T:(lv + 1) * T, :] = jnp.where(
                    (row & h) != 0, oa + ob, from_key).astype(BF16)
                y = YY[j, s, lv]
                hit = levels == float(lv + 1)
                ds0 = jnp.where(hit, mm_nt(g0, y), ds0)
                ds1 = jnp.where(hit, mm_nt(g1, y), ds1)
            causal = levels >= 0.0
            ds0 = jnp.where(causal, ds0, 0.0).astype(BF16)
            ds1 = jnp.where(causal, ds1, 0.0).astype(BF16)
            oa, ob = halves(g * NDL[j, s, nlev].astype(F32))
            XL[nlev * T:, :] = (oa + ob).astype(BF16)
            pg = (pair_cat(PP[j, s, nlev].astype(F32)) * g).astype(BF16)
            phq = jnp.concatenate([PH[i, rows, 0:256] for i in (i0, i1)], axis=1)
            opening = mm(pg, SZ[j, s]) * inv_root
            cg = mm_tn(pg, phq) * inv_root
            for k, i in enumerate((i0, i1)):
                for z in range(2):
                    CG[i, s, z] = cg[z * 128 + k * 64:z * 128 + k * 64 + 64,
                                     k * 256:k * 256 + 256].astype(BF16)
            d_log = mm(TRI[...], XL[...])
            a, b = halves(ab)
            d_value = write * a
            d_write = value * a + b
            d_gate = write * (d_log - keep * d_write)
            tiles = (jnp.where(first, d_value, pltpu.roll(d_gate, 64, 1)),
                     jnp.where(first, pltpu.roll(d_value, 64, 1), d_gate))
            for k, (i, ds) in enumerate(((i0, ds0), (i1, ds1))):
                pq, pk = PH[i, rows, 0:256], PH[i, rows, 256:512]
                dq = mm(ds, pk) * inv_feat + opening[:, k * 256:k * 256 + 256]
                dk = mm_tn(ds, pq) * inv_feat
                pq, pk = pq.astype(F32), pk.astype(F32)
                aq = pq[:, 128:] * dq[:, :128] - pq[:, :128] * dq[:, 128:]
                ak = pk[:, 128:] * dk[:, :128] - pk[:, :128] * dk[:, 128:]
                d_ang = jnp.concatenate([aq, ak], axis=1).astype(BF16)
                DPJ[i, rows, 0:128] = mm_nt(d_ang, WBH[i]).astype(BF16)
                DPJ[i, rows, 128:256] = tiles[k].astype(BF16)
            return bias_sum + jnp.sum(d_gate, axis=0, keepdims=True)

        bias_sum = lax.fori_loop(0, 2, backward, jnp.zeros((1, 128), F32))
        for k, i in enumerate((i0, i1)):
            VEC[pl.ds(2 * D // 128 + 2 * xor(q, i) + c, 1), :] = (
                bias_sum if k else pltpu.roll(bias_sum, 64, 1))

    CR = S["CR"]
    NAT = NFT
    NAT[...] = jnp.transpose(NA[...], (1, 0))
    GIo, GIs, GIr = S["GIo"], S["GIs"], S["GIr"]
    DX = FO
    cp_fo.wait_send()
    cp_gi = [None]
    order = list(range(1, nq)) + [0]
    for i in order:
        gi = mm(NAT[...], DPJ[i])
        if i == 0:
            GIo[...] = gi
        else:
            GIs[i - 1] = gi.astype(BF16)
            cp_gi.append(go(copy(("gi", i), GIs.at[i - 1], GIr.at[i - 1], peer(i))))
    cp_cg = [None] + [
        go(copy(("cg", i), CG.at[i], CR.at[pl.ds(2 * q, 2)], peer(i))) for i in range(1, nq)]
    CR[pl.ds(2 * q, 2)] = CG[0]
    DX[...] = mm_nt(DPJ[0], Win[0])
    for i in range(1, nq):
        DX[...] += mm_nt(DPJ[i], Win[i])
    DXR = S["DXR"]
    cp_dx = go(copy("dx", DX.at[pl.ds((1 - c) * T, T)], DXR, sib))

    ZF, ZM = S["ZF"], S["ZM"]
    LT = D // 128
    for i in range(1, nq):
        cp_gu[i].wait_recv()
        cp_gd[i].wait_recv()
    gu = tree_sum([GUo[...]] + [GUr[i].astype(F32) for i in range(nq - 1)])
    gd = tree_sum([GDo[...]] + [GDr[i].astype(F32) for i in range(nq - 1)])
    for t in range(FH // 128):
        ZF[t * D:(t + 1) * D, :] = gu[:, t * 128:(t + 1) * 128].astype(BF16)
    base = D * (FH // 128)
    for t in range(LT):
        ZF[base + t * FH:base + (t + 1) * FH, :] = gd[:, t * 128:(t + 1) * 128].astype(BF16)

    def reduce_dp(name, Z, R, out):
        piece = Z.shape[0] // ndp
        cps = []
        for k in range(1, ndp):
            cps.append(go(copy(
                (name, "rs", k), Z.at[pl.ds(xor(me_dp, k) * piece, piece)], R.at[k - 1], dpeer(k))))

        def finish():
            mine = pl.ds(pl.multiple_of(me_dp * piece, 16), piece)
            for cp in cps:
                cp.wait_recv()
            total = tree_sum([Z[mine, :].astype(F32)] + [R[k].astype(F32) for k in range(ndp - 1)])
            out[mine, :] = total.astype(BF16)
            return [go(copy((name, "ag", k), out.at[mine], out.at[mine], dpeer(k)))
                    for k in range(1, ndp)]
        return finish

    fin_f = reduce_dp("zf", ZF, S["ZFR"], S["ZFO"])

    cp_dx.wait_recv()
    x = tok[...].astype(F32)
    scale = rms_scale(x)
    unit = x * scale
    grad = DX[own_rows, :] + DXR[...]
    S["token_grad"][...] = DMI[...] + norm_back(grad, unit, scale, gain_a)
    gain_grad = jnp.sum(grad * unit, axis=0, keepdims=True)
    for t in range(LT):
        VEC[t:t + 1, :] = gain_grad[:, t * 128:(t + 1) * 128]
    VR = S["VR"]
    VS = S["VS"]
    cp_v = go(copy("v0", VEC, VR.at[0], sib))
    cp_v.wait_recv()
    VS[0] = VEC[...] + VR[0]
    cp_vs = [go(copy(("v1", i), VS.at[0], VR.at[i], peer(i))) for i in range(1, nq)]

    for i in range(1, nq):
        cp_go[i].wait_recv()
        cp_gi[i].wait_recv()
    gi = tree_sum([GIo[...]] + [GIr[i].astype(F32) for i in range(nq - 1)])
    gout = tree_sum([GOo[...]] + [GOr[i].astype(F32) for i in range(nq - 1)])
    width = gi.shape[1]
    for t in range(width // 128):
        ZM[t * D:(t + 1) * D, :] = gi[:, t * 128:(t + 1) * 128].astype(BF16)
    base = D * (width // 128)
    for t in range(LT):
        ZM[base + t * 64:base + (t + 1) * 64, :] = gout[:, t * 128:(t + 1) * 128].astype(BF16)
    fin_m = reduce_dp("zm", ZM, S["ZMR"], S["ZMO"])
    for cp in cp_vs:
        cp.wait_recv()
    VS[1] = tree_sum([VS[0]] + [VR[i] for i in range(1, nq)])
    cp_vd = [go(copy(("v2", k), VS.at[1], VR.at[nq - 1 + k], dpeer(k))) for k in range(1, ndp)]
    ag_f = fin_f()
    ag_m = fin_m()
    for cp in cp_vd:
        cp.wait_recv()
    vtot = tree_sum([VS[1]] + [VR[nq - 1 + k] for k in range(1, ndp)])
    S["vec_sum"][...] = vtot
    for cp in ag_f + ag_m:
        cp.wait_recv()

    def fold(z):
        z = z.astype(F32)
        return jnp.sum((z * z).reshape(z.shape[0] // 8, 8, 128), axis=0)

    NR, NS = S["NR"], S["NS"]
    NS[...] = fold(S["ZFO"][...]) + fold(S["ZMO"][...])
    cp_n = [go(copy(("n", r), NS, NR.at[r - 1], {"mp": xor(m, r)})) for r in range(1, 2 * nq)]
    lane_v = lax.broadcasted_iota(jnp.int32, VEC.shape, 1)
    row_v = lax.broadcasted_iota(jnp.int32, VEC.shape, 0)
    vmask = (row_v < 2 * LT) | (lane_v >= 64)
    vsq = fold(jnp.where(vmask, vtot, 0.0))
    for i in range(1, nq):
        cp_fin[i].wait_recv()
        cp_cg[i].wait_recv()
    S["fin"][...] = FR[...]
    S["cgrad"][...] = CR[...]
    S["gf"][...] = S["ZFO"][...]
    S["gm"][...] = S["ZMO"][...]
    for cp in cp_n:
        cp.wait_recv()
    S["sq"][...] = tree_sum([NS[...]] + [NR[r] for r in range(2 * nq - 1)]) + vsq
    for cp in sends:
        if cp is not cp_fo and cp is not cp_att:
            cp.wait_send()


def layer_call(ndp, nmp, args, shapes):
    T, D = shapes["tok"].shape
    nq = nmp // 2
    FH = shapes["w_up"].shape[1]
    nlev = (T - 1).bit_length()
    npair = nq // 2
    nseq = 2 * nq
    lt = D // 128
    zf = 2 * D * FH // 128
    zm = (D * 256 + 64 * D) // 128
    vrows = 2 * lt + nseq
    R = nq - 1
    V = pltpu.VMEM
    scratch = dict(
        XT=V((2, T, D), BF16), XC=V((2 * T, D), BF16),
        Win=V((nq, D, 256), BF16), Wout=V((nq, 64, D), BF16),
        Wup=V((nq, D, FH), BF16), Wdown=V((nq, FH, D), BF16),
        CS=V((nseq, 2, 64, 256), BF16), Cin=V((nq, 2, 2, 64, 256), BF16),
        LV=V((T, T), F32), MK=V((nlev + 1, T, T), BF16), MT=V((nlev + 1, T, T), BF16),
        TRI=V((T, (nlev + 1) * T), BF16), VEC=V((vrows, 128), F32),
        WBH=V((nq, 128, 256), BF16), WBL=V((nq, 128, 256), BF16),
        SZ=V((npair, 2, 256, 512), BF16), NA=V((2 * T, D), BF16),
        PH=V((nq, 2 * T, 512), BF16), TV=V((nq, 2 * T, 128), F32),
        VV=V((npair, 2 * T, 128), F32), KK=V((npair, 2 * T, 128), F32),
        WW=V((npair, 2 * T, 128), F32), PP=V((npair, 2, nlev + 1, T, 128), BF16),
        UU=V((npair, 2, nlev, T, 128), BF16), YY=V((npair, 2, nlev, T, 256), BF16),
        ND=V((npair, 2, T, 256), F32), NDL=V((npair, 2, nlev + 1, T, 256), BF16),
        MX=V((2 * T, 64 * nq), BF16), FS=V((nq, 2, 2, 64, 256), BF16),
        FR=V((nseq, 2, 64, 256), BF16), AP=V((2 * T, D), F32), AQ=V((2 * T, D), F32),
        MID=V((2 * T, D), F32), NF=V((2 * T, D), BF16),
        DN=V((2 * T, D), F32), NFT=V((D, 2 * T), BF16),
        GUo=V((D, FH), F32), GDo=V((FH, D), F32),
        GUs=V((R, D, FH), BF16), GDs=V((R, FH, D), BF16),
        GUr=V((R, D, FH), BF16), GDr=V((R, FH, D), BF16),
        FOR=V((T, D), F32), DNR=V((2 * T, D), F32),
        DA=V((2 * T, D), BF16), DM=V((2 * T, 64 * nq), F32), DMI=V((T, D), F32),
        GOo=V((64, D), F32), GOs=V((R, 64, D), BF16), GOr=V((R, 64, D), BF16),
        XL=V(((nlev + 1) * T, 128), BF16), DPJ=V((nq, 2 * T, 256), BF16),
        CG=V((nq, 2, 2, 64, 256), BF16), CR=V((nseq, 2, 64, 256), BF16),
        GIo=V((D, 256), F32), GIs=V((R, D, 256), BF16), GIr=V((R, D, 256), BF16),
        DXR=V((T, D), F32), ZF=V((zf, 128), BF16), ZM=V((zm, 128), BF16),
        ZFR=V((max(ndp - 1, 1), zf // ndp, 128), BF16),
        ZMR=V((max(ndp - 1, 1), zm // ndp, 128), BF16),
        ZFO=V((zf, 128), BF16), ZMO=V((zm, 128), BF16),
        VR=V((nq + ndp, vrows, 128), F32), VS=V((2, vrows, 128), F32),
        NR=V((2 * nq - 1, 8, 128), F32), NS=V((8, 128), F32),
    )
    nsem = 20 + 9 * R + 5 * ndp + 2 * nq
    scratch["ssem"] = pltpu.SemaphoreType.DMA((nsem,))
    scratch["rsem"] = pltpu.SemaphoreType.DMA((nsem,))
    outs = dict(
        block_out=((T, D), BF16), token_grad=((T, D), F32),
        fin=((nseq, 2, 64, 256), BF16), cgrad=((nseq, 2, 64, 256), BF16),
        gf=((zf, 128), BF16), gm=((zm, 128), BF16),
        vec_sum=((vrows, 128), F32), sq=((8, 128), F32))
    names = list(args) + list(outs) + list(scratch)
    cfg = dict(names=names, ndp=ndp, nq=nq, T=T, D=D, nlev=nlev, FH=FH)
    vm = pl.BlockSpec(memory_space=pltpu.VMEM)
    res = pl.pallas_call(
        functools.partial(layer_kernel, cfg),
        out_shape=[jax.ShapeDtypeStruct(s, d) for s, d in outs.values()],
        in_specs=[vm] * len(args),
        out_specs=[vm] * len(outs),
        scratch_shapes=list(scratch.values()),
        compiler_params=pltpu.CompilerParams(
            collective_id=0, has_side_effects=True, vmem_limit_bytes=62 * 2**20),
        name="layer",
    )(*args.values())
    return dict(zip(outs, res))


def adam(w, g, first, second, rate, decay):
    first_new = B1 * first + (1.0 - B1) * g
    second_new = B2 * second + (1.0 - B2) * g * g
    first_hat = first_new / (1.0 - B1**STEP)
    second_hat = second_new / (1.0 - B2**STEP)
    w_new = w - rate * (first_hat / (jnp.sqrt(second_hat) + ADAM_EPS) + decay * w)
    return first_new, second_new, w_new


def shards(
    tokens, cotangent, carried, frequencies, vectors, vectors_first, vectors_second,
    mix_in, mix_in_first, mix_in_second, mix_out, mix_out_first, mix_out_second,
    ffn_up, ffn_up_first, ffn_up_second, ffn_down, ffn_down_first, ffn_down_second,
    *, ndp, nmp,
):
    T, D = tokens.shape
    heads = frequencies.shape[0]
    hd = D // heads
    FH = ffn_up.shape[1]
    lt = D // 128
    bias = jnp.pad(vectors[2].reshape(heads, hd), ((0, 0), (128 - hd, 0)))
    args = dict(
        tok=tokens, cot=cotangent, carried=carried,
        freq=jnp.swapaxes(frequencies, 1, 2), vec=vectors, bias=bias,
        w_in=mix_in.reshape(2 * D, 128), w_out=mix_out, w_up=ffn_up, w_down=ffn_down)
    res = layer_call(ndp, nmp, args, args)
    gf, gm, vs = res["gf"].astype(F32), res["gm"].astype(F32), res["vec_sum"]
    nu = FH // 128
    g_up = jnp.concatenate([gf[t * D:(t + 1) * D] for t in range(nu)], axis=1)
    base = nu * D
    g_down = jnp.concatenate([gf[base + t * FH:base + (t + 1) * FH] for t in range(lt)], axis=1)
    g_in = jnp.concatenate([gm[t * D:(t + 1) * D] for t in range(2)], axis=1).reshape(mix_in.shape)
    g_out = jnp.concatenate(
        [gm[2 * D + t * 64:2 * D + (t + 1) * 64] for t in range(lt)], axis=1)
    g_vec = jnp.stack([vs[:lt].reshape(D), vs[lt:2 * lt].reshape(D), vs[2 * lt:, 128 - hd:].reshape(D)])
    grad_norm = jnp.sqrt(jnp.sum(res["sq"]))
    factor = CLIP / jnp.maximum(grad_norm, CLIP)
    vn = adam(vectors, g_vec * factor, vectors_first, vectors_second, RATE_VECTOR, 0.0)
    im = adam(mix_in, g_in * factor, mix_in_first, mix_in_second, RATE_MATRIX, DECAY)
    om = adam(mix_out, g_out * factor, mix_out_first, mix_out_second, RATE_MATRIX, DECAY)
    um = adam(ffn_up, g_up * factor, ffn_up_first, ffn_up_second, RATE_MATRIX, DECAY)
    dm = adam(ffn_down, g_down * factor, ffn_down_first, ffn_down_second, RATE_MATRIX, DECAY)
    out = (res["block_out"], res["fin"].astype(F32).reshape(carried.shape), res["token_grad"],
           res["cgrad"].astype(F32).reshape(carried.shape), grad_norm) + vn
    for new in (im, om, um, dm):
        out = out + new + (new[2].astype(BF16),)
    return out


def solution(mesh):
    tok = P(("dp", "mp"), None)
    car = P("dp", "mp", None, None, None)
    head = P(None, "mp", None)
    rowp = P("mp", None)
    colp = P(None, "mp")
    rep = P()
    in_specs = (tok, tok, car, rep, rep, rep, rep) + (head,) * 3 + (rowp,) * 3 + (
        colp,) * 3 + (rowp,) * 3
    out_specs = (tok, car, tok, car, rep, rep, rep, rep) + (head,) * 4 + (rowp,) * 4 + (
        colp,) * 4 + (rowp,) * 4
    body = functools.partial(shards, ndp=mesh.shape["dp"], nmp=mesh.shape["mp"])
    return jax.shard_map(body, mesh=mesh, in_specs=in_specs, out_specs=out_specs, check_vma=False)
```

```python
import functools

import jax
import jax.numpy as jnp
from jax import lax
from jax.experimental import pallas as pl
from jax.experimental.pallas import tpu as pltpu
from jax.sharding import PartitionSpec as P

STEP = 10
NORM_EPS = 1e-06
DEN_FLOOR = 0.25
CLIP = 1.0
B1 = 0.9
B2 = 0.999
ADAM_EPS = 1e-08
DECAY = 0.1
RATE_MATRIX = 0.05
RATE_VECTOR = 0.6
MESH = pl.DeviceIdType.MESH
F32 = jnp.float32
BF16 = jnp.bfloat16

SIN = (9.99999996e-01, -1.66666578e-01, 8.33304727e-03, -1.98087928e-04, 2.60457914e-06)
COS = (1.0, -4.99999993e-01, 4.16666357e-02, -1.38883546e-03, 2.47598090e-05, -2.60452002e-07)
PI_A, PI_B, PI_C = 3.140625, 0.0009675025939941406, 1.5099579897537296e-07


def mm(a, b):
    return jnp.dot(a, b, preferred_element_type=F32)


def mm_nt(a, b):
    return lax.dot_general(a, b, (((1,), (1,)), ((), ())), preferred_element_type=F32)


def mm_tn(a, b):
    return lax.dot_general(a, b, (((0,), (0,)), ((), ())), preferred_element_type=F32)


def horner(coefs, y):
    acc = jnp.full_like(y, coefs[-1])
    for coef in coefs[-2::-1]:
        acc = acc * y + coef
    return acc


def sincos(x):
    turns = jnp.floor(x * 0.3183098861837907 + 0.5)
    r = ((x - turns * PI_A) - turns * PI_B) - turns * PI_C
    sign = 1.0 - 2.0 * (turns - 2.0 * jnp.floor(turns * 0.5))
    y = r * r
    return sign * (r * horner(SIN, y)), sign * horner(COS, y)


def rms_scale(x):
    return lax.rsqrt(jnp.mean(x * x, axis=-1, keepdims=True) + NORM_EPS)


def norm_back(grad, unit, scale, gain):
    e = grad * gain
    return scale * (e - unit * jnp.mean(e * unit, axis=-1, keepdims=True))


def xor(a, bits):
    out = a
    step = 1
    while step <= bits:
        if bits & step:
            out = out + step - 2 * step * (lax.div(a, step) % 2)
        step *= 2
    return out


def tree_sum(terms):
    terms = list(terms)
    if len(terms) == 1:
        return terms[0]
    half = len(terms) // 2
    return tree_sum(terms[:half]) + tree_sum(terms[half:])


def halves(a):
    return a[:, :128], a[:, 128:]


def pair_cat(a):
    return jnp.concatenate([a, a], axis=1)


def layer_kernel(cfg, *refs):
    names = cfg["names"]
    S = dict(zip(names, refs))
    ndp, nq, T, D = cfg["ndp"], cfg["nq"], cfg["T"], cfg["D"]
    nlev = cfg["nlev"]
    FH = cfg["FH"]
    npair = nq // 2
    rows2 = 2 * T
    me_dp = lax.axis_index("dp")
    m = lax.axis_index("mp")
    c = m % 2
    q = lax.div(m, 2)
    sib = {"mp": q * 2 + (1 - c)}
    ssem, rsem = S["ssem"], S["rsem"]
    sem_of = {}

    def sem(key):
        return sem_of.setdefault(key, len(sem_of))

    def peer(i):
        return {"mp": xor(q, i) * 2 + c}

    def dpeer(k):
        return {"dp": xor(me_dp, k)}

    def copy(key, src, dst, dev):
        k = sem(key)
        return pltpu.make_async_remote_copy(
            src_ref=src, dst_ref=dst, send_sem=ssem.at[k], recv_sem=rsem.at[k],
            device_id=dev, device_id_type=MESH)

    XT, XC = S["XT"], S["XC"]
    lsem = S["lsem"]
    own_rows = pl.ds(pl.multiple_of(c * T, T), T)
    plan = [("w_in", S["v_in"]), ("tok", XT.at[c]), ("vec", S["v_vec"]), ("freq", S["v_freq"]),
            ("w_out", S["v_out"]), ("carried", S["v_car"]), ("cot", XC.at[own_rows]),
            ("w_up", S["v_up"]), ("w_down", S["v_down"])]
    loads = {}
    for k, (name, dst) in enumerate(plan):
        loads[name] = pltpu.make_async_copy(S[name], dst, lsem.at[k])
        loads[name].start()

    barrier = pltpu.get_barrier_semaphore()
    count = 0
    for r in range(1, 2 * nq):
        pl.semaphore_signal(barrier, inc=1, device_id={"mp": xor(m, r)}, device_id_type=MESH)
        count += 1
    for k in range(1, ndp):
        pl.semaphore_signal(barrier, inc=1, device_id=dpeer(k), device_id_type=MESH)
        count += 1

    Win, Wout, Wup, Wdown = S["Win"], S["Wout"], S["Wup"], S["Wdown"]
    w_in = S["v_in"]
    loads["w_in"].wait()
    Win[0] = jnp.concatenate(
        [w_in[pl.ds(0, D, 2), :], w_in[pl.ds(1, D, 2), :]], axis=1).astype(BF16)
    loads["w_out"].wait()
    Wout[0] = S["v_out"][...].astype(BF16)
    loads["tok"].wait()
    pl.semaphore_wait(barrier, count)

    sends = []

    def go(cp):
        cp.start()
        sends.append(cp)
        return cp

    side = me_dp % 2

    class Gather:
        def __init__(self, name, W):
            part = W.shape[1] // 4

            def rows(first, n):
                return pl.ds(pl.multiple_of(first * part, 16), n * part)

            def cp(key, i, k, r, dev):
                return copy((name, key, k), W.at[i].at[r], W.at[k].at[r], dev)

            self.direct = {i: cp("d", 0, i, rows(side, 3), peer(i)) for i in (1, 2)}
            self.cross = (cp("x", 2, 3, rows(2 * side, 1), peer(1)),
                          cp("y", 1, 3, rows(2 * side + 1, 1), peer(2)))
            self.swap = {i: cp("z", i, i, rows(3 * side, 1), dpeer(1)) for i in (1, 2)}
            self.swap[3] = cp("z", 3, 3, rows(2 * side, 2), dpeer(1))

        def start(self):
            go(self.direct[1])
            go(self.direct[2])

        def forward(self):
            self.direct[2].wait_recv()
            go(self.cross[0])
            self.direct[1].wait_recv()
            go(self.cross[1])
            go(self.swap[1])
            go(self.swap[2])

        def forward_far(self):
            for cp in self.cross:
                cp.wait_recv()
            go(self.swap[3])

        def finish(self, i):
            self.swap[i].wait_recv()

    g_in, g_out, g_up, g_down = (
        Gather(n, W) for n, W in (("in", Win), ("out", Wout), ("up", Wup), ("down", Wdown)))
    cp_tok = go(copy("tok", XT.at[c], XT.at[c], sib))
    g_in.start()
    g_out.start()
    CS, Cin = S["CS"], S["Cin"]

    loads["vec"].wait()
    loads["freq"].wait()
    vec = S["v_vec"]
    gain_a = vec[0:1, :]
    gain_f = vec[1:2, :]
    row_i = lax.broadcasted_iota(jnp.int32, (T, T), 0)
    col_i = lax.broadcasted_iota(jnp.int32, (T, T), 1)
    gap = row_i ^ col_i
    lower = row_i > col_i
    upper = row_i < col_i
    LV, MK, MT, TRI = S["LV"], S["MK"], S["MT"], S["TRI"]
    code = jnp.where(row_i == col_i, 0.0, -1.0)
    MK[0] = jnp.where(row_i == col_i, 1.0, 0.0).astype(BF16)
    MT[0] = jnp.where(row_i == col_i, 1.0, 0.0).astype(BF16)
    for lv in range(nlev):
        h = 1 << lv
        here = (gap >= h) & (gap < 2 * h)
        code = jnp.where(lower & here, float(lv + 1), code)
        MK[lv + 1] = jnp.where(lower & here, 1.0, 0.0).astype(BF16)
        MT[lv + 1] = jnp.where(upper & here, 1.0, 0.0).astype(BF16)
        bit = (row_i & h) != 0
        same = gap < h
        take = same & ((bit & (col_i >= row_i)) | ((~bit) & (col_i < row_i)))
        TRI[:, lv * T:(lv + 1) * T] = jnp.where(take, 1.0, 0.0).astype(BF16)
    TRI[:, nlev * T:(nlev + 1) * T] = jnp.where(col_i >= row_i, 1.0, 0.0).astype(BF16)
    LV[...] = code
    VEC = S["VEC"]
    VEC[...] = jnp.zeros_like(VEC)
    WBH, WBL = S["WBH"], S["WBL"]
    WBH[...] = jnp.zeros_like(WBH)
    WBL[...] = jnp.zeros_like(WBL)
    for i in range(nq):
        freq = S["v_freq"][2 * xor(q, i) + c]
        high = freq.astype(BF16)
        rest = (freq - high.astype(F32)).astype(BF16)
        WBH[i, 0:64, 0:128] = high
        WBH[i, 64:128, 128:256] = high
        WBL[i, 0:64, 0:128] = rest
        WBL[i, 64:128, 128:256] = rest
    SZ = S["SZ"]
    SZ[...] = jnp.zeros_like(SZ)

    NA = S["NA"]
    cp_tok.wait_recv()
    for s in range(2):
        x = XT[s].astype(F32)
        NA[s * T:(s + 1) * T, :] = (x * rms_scale(x) * gain_a).astype(BF16)

    PH, TV = S["PH"], S["TV"]
    lane_row = lax.broadcasted_iota(jnp.int32, (1, 128), 1)
    cp_car = [None]
    for i in range(nq):
        if i == 1:
            g_in.forward()
            g_out.forward()
            for k in range(1, nq):
                cp_car.append(go(copy(
                    ("car", k), CS.at[pl.ds(2 * xor(q, k), 2)], Cin.at[k], peer(k))))
            g_up.start()
            g_down.start()
        if i == 2:
            g_in.forward_far()
            g_out.forward_far()
        if i > 0:
            g_in.finish(i)
        bias = vec[2:3, pl.ds(pl.multiple_of(xor(q, i) * 128, 128), 128)]
        bias = jnp.where(c == 0, pltpu.roll(bias, 64, 1), bias)
        bias = jnp.where(lane_row >= 64, bias, 0.0)

        def head(s, _, i=i, bias=bias):
            rows = pl.ds(pl.multiple_of(s * T, T), T)
            pr = mm(NA[rows, :], Win[i])
            t0, t1 = halves(pr)
            TV[i, rows, :] = t1 + bias
            high = t0.astype(BF16)
            rest = (t0 - high.astype(F32)).astype(BF16)
            ang = mm(high, WBH[i]) + (mm(rest, WBH[i]) + mm(high, WBL[i]))
            sin, cos = sincos(ang)
            PH[i, rows, 0:128] = sin[:, :128].astype(BF16)
            PH[i, rows, 128:256] = cos[:, :128].astype(BF16)
            PH[i, rows, 256:384] = sin[:, 128:].astype(BF16)
            PH[i, rows, 384:512] = cos[:, 128:].astype(BF16)
            return 0

        lax.fori_loop(0, 2, head, 0)
        if i == 0:
            loads["carried"].wait()
            CS[...] = S["v_car"][:, 0].astype(BF16)
            Cin[0] = CS[pl.ds(2 * q, 2)]
            loads["cot"].wait()
            cp_cot = go(copy("cot", XC.at[own_rows], XC.at[own_rows], sib))
            loads["w_up"].wait()
            Wup[0] = S["v_up"][...].astype(BF16)
            loads["w_down"].wait()
            Wdown[0] = S["v_down"][...].astype(BF16)

    lane = lax.broadcasted_iota(jnp.int32, (T, 128), 1)
    first = lane < 64
    row = lax.broadcasted_iota(jnp.int32, (T, 128), 0)
    lane_b = lax.broadcasted_iota(jnp.int32, (T, 256), 1)
    first_b = (lane_b % 128) < 64
    inv_feat = 1.0 / 128.0
    inv_root = 128.0 ** (-0.5)

    def swap(a, h):
        if h < 8:
            return jnp.where((row & h) != 0, pltpu.roll(a, h, 0), pltpu.roll(a, T - h, 0))
        parts = []
        for b in range(T // (2 * h)):
            parts.append(a[(2 * b + 1) * h:(2 * b + 2) * h])
            parts.append(a[2 * b * h:(2 * b + 1) * h])
        return jnp.concatenate(parts, axis=0)

    VV, KK, WW, PP, UU, YY = S["VV"], S["KK"], S["WW"], S["PP"], S["UU"], S["YY"]
    ND, NDL, MX = S["ND"], S["NDL"], S["MX"]
    FS = S["FS"]

    def split_rows(y):
        z = jnp.zeros_like(y)
        return jnp.concatenate([jnp.where(first_b, y, z), jnp.where(first_b, z, y)], axis=0)

    for j in range(npair):
        i0, i1 = 2 * j, 2 * j + 1
        for i in (i0, i1):
            if i > 0:
                cp_car[i].wait_recv()

        def forward(s, _, i0=i0, i1=i1, j=j):
            rows = pl.ds(pl.multiple_of(s * T, T), T)
            for k, i in enumerate((i0, i1)):
                SZ[j, s, k * 64:k * 64 + 64, k * 256:k * 256 + 256] = Cin[i, s, 0]
                SZ[j, s, 128 + k * 64:192 + k * 64, k * 256:k * 256 + 256] = Cin[i, s, 1]
            ta, tb = TV[i0, rows, :], TV[i1, rows, :]
            value = jnp.where(first, ta, pltpu.roll(tb, 64, 1))
            gate = jnp.where(first, pltpu.roll(ta, 64, 1), tb)
            small = jnp.exp(-jnp.abs(gate))
            big = 1.0 / (1.0 + small)
            rest = small * big
            keep = jnp.where(gate >= 0, big, rest)
            write = jnp.where(gate >= 0, rest, big)
            written = write * value
            VV[j, rows, :] = value
            KK[j, rows, :] = keep
            WW[j, rows, :] = write
            scores = [
                (mm_nt(PH[i, rows, 0:256], PH[i, rows, 256:512]) * inv_feat).astype(BF16)
                for i in (i0, i1)]
            total, pre, suf = keep, keep, jnp.ones_like(keep)
            y = jnp.concatenate([written, write], axis=1).astype(BF16)
            left = jnp.concatenate([sc * MK[0] for sc in scores], axis=1)
            acc = mm(left, split_rows(y))
            for lv in range(nlev):
                h = 1 << lv
                if lv > 0:
                    y = jnp.concatenate([suf * written, suf * write], axis=1).astype(BF16)
                YY[j, s, lv] = y
                PP[j, s, lv] = pre.astype(BF16)
                UU[j, s, lv] = suf.astype(BF16)
                left = jnp.concatenate([sc * MK[lv + 1] for sc in scores], axis=1)
                nd = mm(left, split_rows(y)) * pair_cat(pre)
                acc = acc + nd
                NDL[j, s, lv] = nd.astype(BF16)
                other = swap(total, h)
                upper_half = (row & h) != 0
                pre = jnp.where(upper_half, pre * other, pre)
                suf = jnp.where(upper_half, suf, suf * other)
                total = total * other
            PP[j, s, nlev] = pre.astype(BF16)
            phq = jnp.concatenate([PH[i, rows, 0:256] for i in (i0, i1)], axis=1)
            phk = jnp.concatenate([PH[i, rows, 256:512] for i in (i0, i1)], axis=1)
            nd = mm_nt(phq, SZ[j, s]) * (pair_cat(pre) * inv_root)
            NDL[j, s, nlev] = nd.astype(BF16)
            acc = acc + nd
            ND[j, s] = acc
            num, den = halves(acc)
            MX[rows, j * 128:(j + 1) * 128] = (
                num * lax.rsqrt(den * den + DEN_FLOOR)).astype(BF16)
            y = jnp.concatenate([suf * written, suf * write], axis=1).astype(BF16)
            new = mm_tn(y, phk) * inv_root
            last = jnp.transpose(pre[T - 128:, :], (1, 0))[:, 127:128]
            for k, i in enumerate((i0, i1)):
                kept = last[k * 64:k * 64 + 64, :]
                for z in range(2):
                    block = new[z * 128 + k * 64:z * 128 + k * 64 + 64, k * 256:k * 256 + 256]
                    FS[i, s, z] = (kept * Cin[i, s, z].astype(F32) + block).astype(BF16)
            return 0

        lax.fori_loop(0, 2, forward, 0)

    AP, AQ, MID, NF = S["AP"], S["AQ"], S["MID"], S["NF"]
    g_up.forward()
    for i in range(1, nq):
        g_out.finish(i)
    wout = jnp.concatenate([Wout[i] for i in range(nq)], axis=0)
    AP[...] = mm(MX[...], wout)
    cp_att = go(copy("att", AP, AQ, sib))
    g_down.forward()
    cp_att.wait_recv()
    for s in range(2):
        rows = slice(s * T, (s + 1) * T)
        middle = XT[s].astype(F32) + (AP[rows, :] + AQ[rows, :])
        MID[rows, :] = middle
        NF[rows, :] = (middle * rms_scale(middle) * gain_f).astype(BF16)

    FO, DN = AP, S["DN"]
    cp_att.wait_send()
    cp_cot.wait_recv()
    NFT, CT = S["NFT"], XC
    NFT[...] = jnp.transpose(NF[...], (1, 0))

    class Scatter:
        def __init__(self, name):
            self.name = name
            self.own, self.out, self.mid, self.got = (S[name + k] for k in "ospr")
            self.half = self.own.shape[0] // 2
            self.top, self.bottom = pl.ds(0, self.half), pl.ds(self.half, self.half)

        def send(self, key, src, dst, i):
            cp = go(copy((self.name, key), src, dst, peer(i)))
            setattr(self, key, cp)

        def put(self, i, value):
            if i == 0:
                self.own[...] = value
                return
            out = self.out
            out[i - 1] = value.astype(BF16)
            if i == 1:
                self.send("a1", out.at[0].at[self.top], self.got.at[0].at[self.top], 1)
            elif i == 2:
                self.send("a2", out.at[1].at[self.bottom], self.got.at[1].at[self.bottom], 2)
            else:
                self.send("p1", out.at[2].at[self.top], self.mid.at[0], 1)
                self.send("p2", out.at[2].at[self.bottom], self.mid.at[1], 2)

        def middle(self):
            out, half = self.out, self.half
            self.p1.wait_recv()
            out[1, :half] = (out[1, :half].astype(F32) + self.mid[0].astype(F32)).astype(BF16)
            self.send("b2", out.at[1].at[self.top], self.got.at[1].at[self.top], 2)
            self.p2.wait_recv()
            out[0, half:] = (out[0, half:].astype(F32) + self.mid[1].astype(F32)).astype(BF16)
            self.send("b1", out.at[0].at[self.bottom], self.got.at[0].at[self.bottom], 1)

        def total(self):
            for cp in (self.a1, self.a2, self.b1, self.b2):
                cp.wait_recv()
            return self.own[...] + (self.got[0].astype(F32) + self.got[1].astype(F32))

    sc_up, sc_down, sc_in, sc_out = (Scatter(n) for n in ("gu", "gd", "gi", "go"))
    for i in range(nq):
        if i == 1:
            g_up.forward_far()
            g_down.forward_far()
        if i > 0:
            g_up.finish(i)
            g_down.finish(i)
        up, down = Wup[i], Wdown[i]
        pre = mm(NF[...], up)
        square = pre * pre
        th = jnp.tanh(0.7978845608028654 * (pre + 0.044715 * pre * square))
        hidden = (0.5 * pre * (1.0 + th)).astype(BF16)
        slope = 0.5 * (1.0 + th) + 0.5 * pre * (1.0 - th * th) * (
            0.7978845608028654 * (1.0 + 0.134145 * square))
        d_pre = (mm_nt(CT[...], down) * slope).astype(BF16)
        fo = mm(hidden, down)
        dn = mm_nt(d_pre, up)
        if i == 0:
            FO[...] = fo
            DN[...] = dn
        else:
            FO[...] += fo
            DN[...] += dn
        sc_down.put(i, mm_tn(hidden, CT[...]))
        sc_up.put(i, mm(NFT[...], d_pre))
    FOR, DNR = S["FOR"], S["DNR"]
    cp_dn = go(copy("dn", DN, DNR, sib))
    cp_fo = go(copy("fo", FO.at[pl.ds((1 - c) * T, T)], FOR, sib))
    cp_dn.wait_recv()
    DA, DM, DMI = S["DA"], S["DM"], S["DMI"]
    for s in range(2):
        rows = slice(s * T, (s + 1) * T)
        middle = MID[rows, :]
        scale = rms_scale(middle)
        unit = middle * scale
        grad = DN[rows, :] + DNR[rows, :]
        d_mid = XC[rows, :].astype(F32) + norm_back(grad, unit, scale, gain_f)
        DA[rows, :] = d_mid.astype(BF16)
        gain_grad = jnp.sum(grad * unit, axis=0, keepdims=True)

        @pl.when(c == s)
        def _(gain_grad=gain_grad, d_mid=d_mid):
            DMI[...] = d_mid
            for t in range(D // 128):
                VEC[D // 128 + t:D // 128 + t + 1, :] = gain_grad[:, t * 128:(t + 1) * 128]

    cp_fo.wait_recv()
    S["block_out"][...] = (MID[own_rows, :] + (FO[own_rows, :] + FOR[...])).astype(BF16)
    DM[...] = mm_nt(DA[...], wout)
    go_all = mm_tn(MX[...], DA[...])
    for i in range(nq):
        sc_out.put(i, go_all[64 * i:64 * i + 64])

    XL, DPJ, CG = S["XL"], S["DPJ"], S["CG"]
    ZD, ZU, ZI = S["ZD"], S["ZU"], S["ZI"]
    NS = S["NS"]
    LT = D // 128

    def fold(z):
        return jnp.sum((z * z).reshape(z.shape[0] // 8, 8, 128), axis=0)

    def tiles_of(a):
        return [a[:, t * 128:(t + 1) * 128].astype(BF16) for t in range(a.shape[1] // 128)]

    def lay(Z, parts):
        at = 0
        for part in parts:
            Z[at:at + part.shape[0], :] = part
            at += part.shape[0]

    def reduce_dp(name, Z, R, out):
        piece = Z.shape[0] // ndp
        mine = pl.ds(pl.multiple_of(me_dp * piece, 16), piece)
        scatter = [copy((name, "rs", k), Z.at[pl.ds(xor(me_dp, k) * piece, piece)], R.at[k - 1],
                        dpeer(k)) for k in range(1, ndp)]
        spread = [copy((name, "ag", k), out.at[mine], out.at[mine], dpeer(k))
                  for k in range(1, ndp)]

        def start():
            for cp in scatter:
                go(cp)

        def middle():
            for cp in scatter:
                cp.wait_recv()
            total = tree_sum([Z[mine, :].astype(F32)] + [R[k].astype(F32) for k in range(ndp - 1)])
            total = total.astype(BF16)
            out[mine, :] = total
            for cp in spread:
                go(cp)
            return fold(total.astype(F32))

        def finish():
            for cp in spread:
                cp.wait_recv()
        return start, middle, finish

    zd_start, zd_middle, zd_finish = reduce_dp("zd", ZD, S["ZDR"], S["ZDO"])
    zu_start, zu_middle, zu_finish = reduce_dp("zu", ZU, S["ZUR"], S["ZUO"])
    zi_start, zi_middle, zi_finish = reduce_dp("zi", ZI, S["ZIR"], S["ZIO"])

    def hook_0():
        sc_down.middle()

    def hook_1():
        sc_up.middle()
        sc_out.middle()

    def hook_2():
        lay(ZD, tiles_of(sc_down.total()))
        zd_start()

    def hook_3():
        lay(ZU, tiles_of(sc_up.total()) + tiles_of(sc_out.total()))
        zu_start()

    NAT = NFT
    NAT[...] = jnp.transpose(NA[...], (1, 0))
    for j in (1, 0):
        i0, i1 = 2 * j, 2 * j + 1

        bias_sum = jnp.zeros((1, 128), F32)
        for s in range(2):
            rows = pl.ds(s * T, T)
            if s == 1:
                if j == 1:
                    hook_0()
                else:
                    hook_2()
            dm = DM[rows, j * 128:(j + 1) * 128]
            num, den = halves(ND[j, s])
            r = lax.rsqrt(den * den + DEN_FLOOR)
            d_num = dm * r
            d_den = -(d_num * num) * den * (r * r)
            g = jnp.concatenate([d_num, d_den], axis=1)
            value, keep, write = VV[j, rows, :], KK[j, rows, :], WW[j, rows, :]
            written = write * value
            scores = [
                (mm_nt(PH[i, rows, 256:512], PH[i, rows, 0:256]) * inv_feat).astype(BF16)
                for i in (i0, i1)]
            levels = LV[...]
            z16 = jnp.zeros((T, 256), BF16)
            gb = g.astype(BF16)
            g0, g1 = jnp.where(first_b, gb, z16), jnp.where(first_b, z16, gb)
            left = jnp.concatenate([sc * MT[0] for sc in scores], axis=1)
            ab = mm(left, jnp.concatenate([g0, g1], axis=0))
            y = YY[j, s, 0]
            ds0 = mm_nt(g0, y)
            ds1 = mm_nt(g1, y)
            for lv in range(nlev):
                h = 1 << lv
                pg = (pair_cat(PP[j, s, lv].astype(F32)) * g).astype(BF16)
                g0, g1 = jnp.where(first_b, pg, z16), jnp.where(first_b, z16, pg)
                left = jnp.concatenate([sc * MT[lv + 1] for sc in scores], axis=1)
                part = mm(left, jnp.concatenate([g0, g1], axis=0)) * pair_cat(UU[j, s, lv].astype(F32))
                ab = ab + part
                pa, pb = halves(part)
                from_key = written * pa + write * pb
                oa, ob = halves(g * NDL[j, s, lv].astype(F32))
                XL[lv * T:(lv + 1) * T, :] = jnp.where(
                    (row & h) != 0, oa + ob, from_key).astype(BF16)
                y = YY[j, s, lv]
                hit = levels == float(lv + 1)
                ds0 = jnp.where(hit, mm_nt(g0, y), ds0)
                ds1 = jnp.where(hit, mm_nt(g1, y), ds1)
            causal = levels >= 0.0
            ds0 = jnp.where(causal, ds0, 0.0).astype(BF16)
            ds1 = jnp.where(causal, ds1, 0.0).astype(BF16)
            oa, ob = halves(g * NDL[j, s, nlev].astype(F32))
            XL[nlev * T:, :] = (oa + ob).astype(BF16)
            pg = (pair_cat(PP[j, s, nlev].astype(F32)) * g).astype(BF16)
            phq = jnp.concatenate([PH[i, rows, 0:256] for i in (i0, i1)], axis=1)
            opening = mm(pg, SZ[j, s]) * inv_root
            cg = mm_tn(pg, phq) * inv_root
            for k, i in enumerate((i0, i1)):
                for z in range(2):
                    CG[i, s, z] = cg[z * 128 + k * 64:z * 128 + k * 64 + 64,
                                     k * 256:k * 256 + 256].astype(BF16)
            d_log = mm(TRI[...], XL[...])
            a, b = halves(ab)
            d_value = write * a
            d_write = value * a + b
            d_gate = write * (d_log - keep * d_write)
            tiles = (jnp.where(first, d_value, pltpu.roll(d_gate, 64, 1)),
                     jnp.where(first, pltpu.roll(d_value, 64, 1), d_gate))
            for k, (i, ds) in enumerate(((i0, ds0), (i1, ds1))):
                pq, pk = PH[i, rows, 0:256], PH[i, rows, 256:512]
                dq = mm(ds, pk) * inv_feat + opening[:, k * 256:k * 256 + 256]
                dk = mm_tn(ds, pq) * inv_feat
                pq, pk = pq.astype(F32), pk.astype(F32)
                aq = pq[:, 128:] * dq[:, :128] - pq[:, :128] * dq[:, 128:]
                ak = pk[:, 128:] * dk[:, :128] - pk[:, :128] * dk[:, 128:]
                d_ang = jnp.concatenate([aq, ak], axis=1).astype(BF16)
                DPJ[i, rows, 0:128] = mm_nt(d_ang, WBH[i]).astype(BF16)
                DPJ[i, rows, 128:256] = tiles[k].astype(BF16)
            bias_sum = bias_sum + jnp.sum(d_gate, axis=0, keepdims=True)

        for k, i in enumerate((i0, i1)):
            VEC[pl.ds(2 * D // 128 + 2 * xor(q, i) + c, 1), :] = (
                bias_sum if k else pltpu.roll(bias_sum, 64, 1))

        for i in (i1, i0):
            sc_in.put(i, mm(NAT[...], DPJ[i]))
        if j == 1:
            hook_1()

    sc_in.middle()
    hook_3()
    CR, FR = S["CR"], S["FR"]
    cp_cg = [None] + [
        go(copy(("cg", i), CG.at[i], CR.at[pl.ds(2 * q, 2)], peer(i))) for i in range(1, nq)]
    cp_fin = [None] + [
        go(copy(("fin", i), FS.at[i], FR.at[pl.ds(2 * q, 2)], peer(i))) for i in range(1, nq)]
    CR[pl.ds(2 * q, 2)] = CG[0]
    FR[pl.ds(2 * q, 2)] = FS[0]
    DX = FO
    cp_fo.wait_send()
    DX[...] = mm_nt(DPJ[0], Win[0])
    for i in range(1, nq):
        DX[...] += mm_nt(DPJ[i], Win[i])
    DXR = S["DXR"]
    cp_dx = go(copy("dx", DX.at[pl.ds((1 - c) * T, T)], DXR, sib))
    square = zd_middle()
    cp_dx.wait_recv()
    x = XT[c].astype(F32)
    scale = rms_scale(x)
    unit = x * scale
    grad = DX[own_rows, :] + DXR[...]
    S["token_grad"][...] = DMI[...] + norm_back(grad, unit, scale, gain_a)
    gain_grad = jnp.sum(grad * unit, axis=0, keepdims=True)
    for t in range(LT):
        VEC[t:t + 1, :] = gain_grad[:, t * 128:(t + 1) * 128]
    VR = S["VR"]
    VS = S["VS"]
    cp_v = go(copy("v0", VEC, VR.at[0], sib))

    lay(ZI, tiles_of(sc_in.total()))
    zi_start()
    cp_v.wait_recv()
    VS[0] = VEC[...] + VR[0]
    cp_vs = [go(copy(("v1", i), VS.at[0], VR.at[i], peer(i))) for i in range(1, nq)]
    square = square + zu_middle()
    for cp in cp_vs:
        cp.wait_recv()
    VS[1] = tree_sum([VS[0]] + [VR[i] for i in range(1, nq)])
    cp_vd = [go(copy(("v2", k), VS.at[1], VR.at[nq - 1 + k], dpeer(k))) for k in range(1, ndp)]
    NS[0] = square + zi_middle()
    NR = S["NR"]
    cp_n = [go(copy(("n", r), NS.at[0], NR.at[r - 1], {"mp": xor(m, r)})) for r in range(1, 2 * nq)]
    for cp in cp_vd:
        cp.wait_recv()
    vtot = tree_sum([VS[1]] + [VR[nq - 1 + k] for k in range(1, ndp)])
    g_vec = S["g_vec"]
    for t in range(LT):
        part = slice(t * 128, (t + 1) * 128)
        g_vec[0:1, part] = vtot[t:t + 1, :]
        g_vec[1:2, part] = vtot[LT + t:LT + t + 1, :]
        even = vtot[2 * LT + 2 * t:2 * LT + 2 * t + 1, :]
        odd = vtot[2 * LT + 2 * t + 1:2 * LT + 2 * t + 2, :]
        g_vec[2:3, part] = jnp.where(lane_row < 64, pltpu.roll(even, 64, 1), odd)
    for cp in cp_n:
        cp.wait_recv()
    NS[1] = tree_sum([NS[0]] + [NR[r] for r in range(2 * nq - 1)])
    cp_m = [go(copy(("m", k), NS.at[1], NR.at[2 * nq - 2 + k], dpeer(k))) for k in range(1, ndp)]

    lane_v = lax.broadcasted_iota(jnp.int32, VEC.shape, 1)
    row_v = lax.broadcasted_iota(jnp.int32, VEC.shape, 0)
    vmask = (row_v < 2 * LT) | (lane_v >= 64)
    vsq = fold(jnp.where(vmask, vtot, 0.0))

    def unlay(Z, first, shape):
        n = shape[0]
        return jnp.concatenate(
            [Z[first + t * n:first + (t + 1) * n, :] for t in range(shape[1] // 128)], axis=1)

    zd_finish()
    S["g_down"][...] = unlay(S["ZDO"], 0, (FH, D))
    zu_finish()
    S["g_up"][...] = unlay(S["ZUO"], 0, (D, FH))
    S["g_out"][...] = unlay(S["ZUO"], D * FH // 128, (64, D))
    zi_finish()
    S["g_in"][...] = unlay(S["ZIO"], 0, (D, 256))
    for i in range(1, nq):
        cp_fin[i].wait_recv()
        cp_cg[i].wait_recv()
    S["fin"][...] = FR[...]
    S["cgrad"][...] = CR[...]
    for cp in cp_m:
        cp.wait_recv()
    S["sq"][...] = tree_sum([NS[1]] + [NR[2 * nq - 2 + k] for k in range(1, ndp)]) + vsq
    for cp in sends:
        if cp is not cp_fo and cp is not cp_att:
            cp.wait_send()


def layer_call(ndp, nmp, args, shapes):
    T, D = shapes["tok"].shape
    nq = nmp // 2
    FH = shapes["w_up"].shape[1]
    nlev = (T - 1).bit_length()
    npair = nq // 2
    nseq = 2 * nq
    lt = D // 128
    zd = D * FH // 128
    zu = (D * FH + 64 * D) // 128
    zi = D * 256 // 128
    vrows = 2 * lt + nseq
    R = nq - 1
    V = pltpu.VMEM
    scratch = dict(
        XT=V((2, T, D), BF16), XC=V((2 * T, D), BF16),
        Win=V((nq, D, 256), BF16), Wout=V((nq, 64, D), BF16),
        Wup=V((nq, D, FH), BF16), Wdown=V((nq, FH, D), BF16),
        CS=V((nseq, 2, 64, 256), BF16), Cin=V((nq, 2, 2, 64, 256), BF16),
        LV=V((T, T), F32), MK=V((nlev + 1, T, T), BF16), MT=V((nlev + 1, T, T), BF16),
        TRI=V((T, (nlev + 1) * T), BF16), VEC=V((vrows, 128), F32),
        WBH=V((nq, 128, 256), BF16), WBL=V((nq, 128, 256), BF16),
        SZ=V((npair, 2, 256, 512), BF16), NA=V((2 * T, D), BF16),
        PH=V((nq, 2 * T, 512), BF16), TV=V((nq, 2 * T, 128), F32),
        VV=V((npair, 2 * T, 128), F32), KK=V((npair, 2 * T, 128), F32),
        WW=V((npair, 2 * T, 128), F32), PP=V((npair, 2, nlev + 1, T, 128), BF16),
        UU=V((npair, 2, nlev, T, 128), BF16), YY=V((npair, 2, nlev, T, 256), BF16),
        ND=V((npair, 2, T, 256), F32), NDL=V((npair, 2, nlev + 1, T, 256), BF16),
        MX=V((2 * T, 64 * nq), BF16), FS=V((nq, 2, 2, 64, 256), BF16),
        FR=V((nseq, 2, 64, 256), BF16), AP=V((2 * T, D), F32), AQ=V((2 * T, D), F32),
        MID=V((2 * T, D), F32), NF=V((2 * T, D), BF16),
        DN=V((2 * T, D), F32), NFT=V((D, 2 * T), BF16),
        guo=V((D, FH), F32), gus=V((R, D, FH), BF16),
        gup=V((2, D // 2, FH), BF16), gur=V((2, D, FH), BF16),
        gdo=V((FH, D), F32), gds=V((R, FH, D), BF16),
        gdp=V((2, FH // 2, D), BF16), gdr=V((2, FH, D), BF16),
        gio=V((D, 256), F32), gis=V((R, D, 256), BF16),
        gip=V((2, D // 2, 256), BF16), gir=V((2, D, 256), BF16),
        goo=V((64, D), F32), gos=V((R, 64, D), BF16),
        gop=V((2, 32, D), BF16), gor=V((2, 64, D), BF16),
        FOR=V((T, D), F32), DNR=V((2 * T, D), F32),
        DA=V((2 * T, D), BF16), DM=V((2 * T, 64 * nq), F32), DMI=V((T, D), F32),
        XL=V(((nlev + 1) * T, 128), BF16), DPJ=V((nq, 2 * T, 256), BF16),
        CG=V((nq, 2, 2, 64, 256), BF16), CR=V((nseq, 2, 64, 256), BF16),
        DXR=V((T, D), F32), ZD=V((zd, 128), BF16), ZU=V((zu, 128), BF16),
        ZI=V((zi, 128), BF16),
        ZDR=V((ndp - 1, zd // ndp, 128), BF16), ZUR=V((ndp - 1, zu // ndp, 128), BF16),
        ZIR=V((ndp - 1, zi // ndp, 128), BF16),
        ZDO=V((zd, 128), BF16), ZUO=V((zu, 128), BF16), ZIO=V((zi, 128), BF16),
        VR=V((nq + ndp, vrows, 128), F32), VS=V((2, vrows, 128), F32),
        NR=V((2 * nq - 2 + ndp, 8, 128), F32), NS=V((2, 8, 128), F32),
        v_in=V((2 * D, 128), F32), v_vec=V((3, D), F32), v_freq=V(shapes["freq"].shape, F32),
        v_out=V((64, D), F32), v_car=V(shapes["carried"].shape, F32),
        v_up=V((D, FH), F32), v_down=V((FH, D), F32),
    )
    nsem = 80 + 3 * R + 9 * ndp + 2 * nq
    scratch["lsem"] = pltpu.SemaphoreType.DMA((len(args),))
    scratch["ssem"] = pltpu.SemaphoreType.DMA((nsem,))
    scratch["rsem"] = pltpu.SemaphoreType.DMA((nsem,))
    outs = dict(
        block_out=((T, D), BF16), token_grad=((T, D), F32),
        fin=((nseq, 2, 64, 256), BF16), cgrad=((nseq, 2, 64, 256), BF16),
        g_in=((D, 256), BF16), g_out=((64, D), BF16),
        g_up=((D, FH), BF16), g_down=((FH, D), BF16),
        g_vec=((3, D), F32), sq=((8, 128), F32))
    names = list(args) + list(outs) + list(scratch)
    cfg = dict(names=names, ndp=ndp, nq=nq, T=T, D=D, nlev=nlev, FH=FH)
    vm = pl.BlockSpec(memory_space=pltpu.VMEM)
    res = pl.pallas_call(
        functools.partial(layer_kernel, cfg),
        out_shape=[jax.ShapeDtypeStruct(s, d) for s, d in outs.values()],
        in_specs=[pl.BlockSpec(memory_space=pl.ANY)] * len(args),
        out_specs=[vm] * len(outs),
        scratch_shapes=list(scratch.values()),
        compiler_params=pltpu.CompilerParams(
            collective_id=0, has_side_effects=True, vmem_limit_bytes=62 * 2**20),
        name="layer",
    )(*args.values())
    return dict(zip(outs, res))


def adam(w, g, first, second, rate, decay):
    first_new = B1 * first + (1.0 - B1) * g
    second_new = B2 * second + (1.0 - B2) * g * g
    first_hat = first_new / (1.0 - B1**STEP)
    second_hat = second_new / (1.0 - B2**STEP)
    w_new = w - rate * (first_hat / (jnp.sqrt(second_hat) + ADAM_EPS) + decay * w)
    return first_new, second_new, w_new


def adam_kernel(names, nout, *refs):
    S = dict(zip(names, refs))
    norm = jnp.sqrt(jnp.sum(S["sq"][...]))
    factor = CLIP / jnp.maximum(norm, CLIP)

    @pl.when(pl.program_id(0) == 0)
    def _():
        S["norm"][0, 0] = norm
        g = S["g_v"][...] * factor
        res = adam(S["v0"][...], g, S["v1"][...], S["v2"][...], RATE_VECTOR, 0.0)
        for k in range(3):
            S["nv%d" % k][...] = res[k]

    for key in "oud":
        g = S["g_" + key][...].astype(F32) * factor
        res = adam(S[key + "0"][...], g, S[key + "1"][...], S[key + "2"][...], RATE_MATRIX, DECAY)
        for k in range(3):
            S["n%s%d" % (key, k)][...] = res[k]
        S["n%s3" % key][...] = res[2].astype(BF16)
    count = S["i0"].shape[0] // 2
    for t in range(2):
        rows = pl.ds(t, count, 2)
        lanes = slice(t * 128, (t + 1) * 128)
        g = S["g_i"][:, lanes].astype(F32) * factor
        res = adam(S["i0"][rows, :], g, S["i1"][rows, :], S["i2"][rows, :], RATE_MATRIX, DECAY)
        for k in range(3):
            S["ni%d" % k][rows, :] = res[k]
        S["ni3"][:, lanes] = res[2].astype(BF16)
    S["n_block_out"][...] = S["block_out"][...]
    S["n_token_grad"][...] = S["token_grad"][...]
    S["n_fin"][...] = S["fin"][...].astype(F32)
    S["n_cgrad"][...] = S["cgrad"][...].astype(F32)


def adam_call(res, params):
    steps = 4

    def cut(shape):
        block = (shape[0] // steps,) + tuple(shape[1:])
        return pl.BlockSpec(block, lambda g: (g,) + (0,) * (len(shape) - 1))

    def whole(shape):
        return pl.BlockSpec(tuple(shape), lambda g: (0,) * len(shape))

    ins, in_specs, outs, out_specs, names, onames = [], [], [], [], [], []

    def take(name, a, spec):
        names.append(name)
        ins.append(a)
        in_specs.append(spec(a.shape))

    def give(name, shape, dtype, spec):
        onames.append(name)
        outs.append(jax.ShapeDtypeStruct(shape, dtype))
        out_specs.append(spec(shape))

    take("sq", res["sq"], whole)
    for key, full in zip("vioud", ("g_vec", "g_in", "g_out", "g_up", "g_down")):
        spec = whole if key == "v" else cut
        take("g_" + key, res[full], spec)
        for k, a in enumerate(params[key]):
            take("%s%d" % (key, k), a, spec)
            give("n%s%d" % (key, k), a.shape, F32, spec)
        if key != "v":
            give("n%s3" % key, res[full].shape, BF16, spec)
    for name in ("block_out", "token_grad", "fin", "cgrad"):
        a = res[name]
        take(name, a, cut)
        give("n_" + name, a.shape, F32 if name in ("fin", "cgrad") else a.dtype, cut)
    onames.append("norm")
    outs.append(jax.ShapeDtypeStruct((1, 1), F32))
    out_specs.append(pl.BlockSpec(memory_space=pltpu.SMEM))
    got = pl.pallas_call(
        functools.partial(adam_kernel, names + onames, len(onames)),
        grid=(steps,), out_shape=outs, in_specs=in_specs, out_specs=out_specs,
        compiler_params=pltpu.CompilerParams(vmem_limit_bytes=int(63.9 * 2**20)),
        name="adam",
    )(*ins)
    got = dict(zip(onames, got))
    new = {key: tuple(got["n%s%d" % (key, k)] for k in range(3 if key == "v" else 4))
           for key in "vioud"}
    for name in ("block_out", "token_grad", "fin", "cgrad"):
        new[name] = got["n_" + name]
    new["norm"] = got["norm"]
    return new


def shards(
    tokens, cotangent, carried, frequencies, vectors, vectors_first, vectors_second,
    mix_in, mix_in_first, mix_in_second, mix_out, mix_out_first, mix_out_second,
    ffn_up, ffn_up_first, ffn_up_second, ffn_down, ffn_down_first, ffn_down_second,
    *, ndp, nmp,
):
    D = tokens.shape[1]
    FH = ffn_up.shape[1]
    args = dict(
        tok=tokens, cot=cotangent, carried=carried,
        freq=jnp.swapaxes(frequencies, 1, 2), vec=vectors,
        w_in=mix_in.reshape(2 * D, 128), w_out=mix_out, w_up=ffn_up, w_down=ffn_down)
    res = layer_call(ndp, nmp, args, args)
    flat = (2 * D, 128)
    params = dict(
        v=(vectors, vectors_first, vectors_second),
        i=tuple(a.reshape(flat) for a in (mix_in, mix_in_first, mix_in_second)),
        o=(mix_out, mix_out_first, mix_out_second),
        u=(ffn_up, ffn_up_first, ffn_up_second),
        d=(ffn_down, ffn_down_first, ffn_down_second))
    new = adam_call(res, params)
    shape = mix_in.shape
    return (
        new["block_out"], new["fin"].reshape(carried.shape), new["token_grad"],
        new["cgrad"].reshape(carried.shape), new["norm"][0, 0],
        *new["v"], *(a.reshape(shape) for a in new["i"]), *new["o"], *new["u"], *new["d"])


def solution(mesh):
    tok = P(("dp", "mp"), None)
    car = P("dp", "mp", None, None, None)
    head = P(None, "mp", None)
    rowp = P("mp", None)
    colp = P(None, "mp")
    rep = P()
    in_specs = (tok, tok, car, rep, rep, rep, rep) + (head,) * 3 + (rowp,) * 3 + (
        colp,) * 3 + (rowp,) * 3
    out_specs = (tok, car, tok, car, rep, rep, rep, rep) + (head,) * 4 + (rowp,) * 4 + (
        colp,) * 4 + (rowp,) * 4
    body = functools.partial(shards, ndp=mesh.shape["dp"], nmp=mesh.shape["mp"])
    return jax.shard_map(body, mesh=mesh, in_specs=in_specs, out_specs=out_specs, check_vma=False)
```

```python
import functools

import jax
import jax.numpy as jnp
from jax import lax
from jax.experimental import pallas as pl
from jax.experimental.pallas import tpu as pltpu
from jax.sharding import PartitionSpec as P

STEP = 10
NORM_EPS = 1e-06
DEN_FLOOR = 0.25
CLIP = 1.0
B1 = 0.9
B2 = 0.999
ADAM_EPS = 1e-08
DECAY = 0.1
RATE_MATRIX = 0.05
RATE_VECTOR = 0.6
MESH = pl.DeviceIdType.MESH
F32 = jnp.float32
BF16 = jnp.bfloat16

SIN = (9.99999996e-01, -1.66666578e-01, 8.33304727e-03, -1.98087928e-04, 2.60457914e-06)
COS = (1.0, -4.99999993e-01, 4.16666357e-02, -1.38883546e-03, 2.47598090e-05, -2.60452002e-07)
PI_A, PI_B, PI_C = 3.140625, 0.0009675025939941406, 1.5099579897537296e-07


def mm(a, b):
    return jnp.dot(a, b, preferred_element_type=F32)


def mm_nt(a, b):
    return lax.dot_general(a, b, (((1,), (1,)), ((), ())), preferred_element_type=F32)


def mm_tn(a, b):
    return lax.dot_general(a, b, (((0,), (0,)), ((), ())), preferred_element_type=F32)


def horner(coefs, y):
    acc = jnp.full_like(y, coefs[-1])
    for coef in coefs[-2::-1]:
        acc = acc * y + coef
    return acc


def sincos(x):
    turns = jnp.floor(x * 0.3183098861837907 + 0.5)
    r = ((x - turns * PI_A) - turns * PI_B) - turns * PI_C
    sign = 1.0 - 2.0 * (turns - 2.0 * jnp.floor(turns * 0.5))
    y = r * r
    return sign * (r * horner(SIN, y)), sign * horner(COS, y)


def rms_scale(x):
    return lax.rsqrt(jnp.mean(x * x, axis=-1, keepdims=True) + NORM_EPS)


def norm_back(grad, unit, scale, gain):
    e = grad * gain
    return scale * (e - unit * jnp.mean(e * unit, axis=-1, keepdims=True))


def xor(a, bits):
    out = a
    step = 1
    while step <= bits:
        if bits & step:
            out = out + step - 2 * step * (lax.div(a, step) % 2)
        step *= 2
    return out


def tree_sum(terms):
    terms = list(terms)
    if len(terms) == 1:
        return terms[0]
    half = len(terms) // 2
    return tree_sum(terms[:half]) + tree_sum(terms[half:])


def halves(a):
    return a[:, :128], a[:, 128:]


def pair_cat(a):
    return jnp.concatenate([a, a], axis=1)


def layer_kernel(cfg, *refs):
    names = cfg["names"]
    S = dict(zip(names, refs))
    ndp, nq, T, D = cfg["ndp"], cfg["nq"], cfg["T"], cfg["D"]
    nlev = cfg["nlev"]
    FH = cfg["FH"]
    npair = nq // 2
    rows2 = 2 * T
    me_dp = lax.axis_index("dp")
    m = lax.axis_index("mp")
    c = m % 2
    q = lax.div(m, 2)
    sib = {"mp": q * 2 + (1 - c)}
    ssem, rsem = S["ssem"], S["rsem"]
    sem_of = {}

    def sem(key):
        return sem_of.setdefault(key, len(sem_of))

    def peer(i):
        return {"mp": xor(q, i) * 2 + c}

    def dpeer(k):
        return {"dp": xor(me_dp, k)}

    def copy(key, src, dst, dev):
        k = sem(key)
        return pltpu.make_async_remote_copy(
            src_ref=src, dst_ref=dst, send_sem=ssem.at[k], recv_sem=rsem.at[k],
            device_id=dev, device_id_type=MESH)

    XT, XC = S["XT"], S["XC"]
    lsem = S["lsem"]
    own_rows = pl.ds(pl.multiple_of(c * T, T), T)
    plan = [("w_in", S["v_in"]), ("tok", XT.at[c]), ("vec", S["v_vec"]), ("freq", S["v_freq"]),
            ("w_out", S["v_out"]), ("carried", S["v_car"]), ("cot", XC.at[own_rows]),
            ("w_up", S["v_up"]), ("w_down", S["v_down"])]
    loads = {}
    for k, (name, dst) in enumerate(plan):
        loads[name] = pltpu.make_async_copy(S[name], dst, lsem.at[k])
        loads[name].start()

    barrier = pltpu.get_barrier_semaphore()
    count = 0
    for r in range(1, 2 * nq):
        pl.semaphore_signal(barrier, inc=1, device_id={"mp": xor(m, r)}, device_id_type=MESH)
        count += 1
    for k in range(1, ndp):
        pl.semaphore_signal(barrier, inc=1, device_id=dpeer(k), device_id_type=MESH)
        count += 1

    Win, Wout, Wup, Wdown = S["Win"], S["Wout"], S["Wup"], S["Wdown"]
    w_in = S["v_in"]
    loads["w_in"].wait()
    Win[0] = jnp.concatenate(
        [w_in[pl.ds(0, D, 2), :], w_in[pl.ds(1, D, 2), :]], axis=1).astype(BF16)
    loads["w_out"].wait()
    Wout[0] = S["v_out"][...].astype(BF16)
    loads["tok"].wait()
    pl.semaphore_wait(barrier, count)

    sends = []

    def go(cp):
        cp.start()
        sends.append(cp)
        return cp

    side = me_dp % 2

    class Gather:
        def __init__(self, name, W):
            part = W.shape[1] // 4

            def rows(first, n):
                return pl.ds(pl.multiple_of(first * part, 16), n * part)

            def cp(key, i, k, r, dev):
                return copy((name, key, k), W.at[i].at[r], W.at[k].at[r], dev)

            self.direct = {i: cp("d", 0, i, rows(side, 3), peer(i)) for i in (1, 2)}
            self.cross = (cp("x", 2, 3, rows(2 * side, 1), peer(1)),
                          cp("y", 1, 3, rows(2 * side + 1, 1), peer(2)))
            self.swap = {i: cp("z", i, i, rows(3 * side, 1), dpeer(1)) for i in (1, 2)}
            self.swap[3] = cp("z", 3, 3, rows(2 * side, 2), dpeer(1))

        def start(self):
            go(self.direct[1])
            go(self.direct[2])

        def forward(self):
            self.direct[2].wait_recv()
            go(self.cross[0])
            self.direct[1].wait_recv()
            go(self.cross[1])
            go(self.swap[1])
            go(self.swap[2])

        def forward_far(self):
            for cp in self.cross:
                cp.wait_recv()
            go(self.swap[3])

        def finish(self, i):
            self.swap[i].wait_recv()

    g_in, g_out, g_up, g_down = (
        Gather(n, W) for n, W in (("in", Win), ("out", Wout), ("up", Wup), ("down", Wdown)))
    cp_tok = go(copy("tok", XT.at[c], XT.at[c], sib))
    g_in.start()
    g_out.start()
    CS, Cin = S["CS"], S["Cin"]

    loads["vec"].wait()
    loads["freq"].wait()
    vec = S["v_vec"]
    gain_a = vec[0:1, :]
    gain_f = vec[1:2, :]
    row_i = lax.broadcasted_iota(jnp.int32, (T, T), 0)
    col_i = lax.broadcasted_iota(jnp.int32, (T, T), 1)
    gap = row_i ^ col_i
    lower = row_i > col_i
    upper = row_i < col_i
    LV, MK, MT, TRI = S["LV"], S["MK"], S["MT"], S["TRI"]
    code = jnp.where(row_i == col_i, 0.0, -1.0)
    MK[0] = jnp.where(row_i == col_i, 1.0, 0.0).astype(BF16)
    MT[0] = jnp.where(row_i == col_i, 1.0, 0.0).astype(BF16)
    for lv in range(nlev):
        h = 1 << lv
        here = (gap >= h) & (gap < 2 * h)
        code = jnp.where(lower & here, float(lv + 1), code)
        MK[lv + 1] = jnp.where(lower & here, 1.0, 0.0).astype(BF16)
        MT[lv + 1] = jnp.where(upper & here, 1.0, 0.0).astype(BF16)
        bit = (row_i & h) != 0
        same = gap < h
        take = same & ((bit & (col_i >= row_i)) | ((~bit) & (col_i < row_i)))
        TRI[:, lv * T:(lv + 1) * T] = jnp.where(take, 1.0, 0.0).astype(BF16)
    TRI[:, nlev * T:(nlev + 1) * T] = jnp.where(col_i >= row_i, 1.0, 0.0).astype(BF16)
    LV[...] = code
    VEC = S["VEC"]
    VEC[...] = jnp.zeros_like(VEC)
    WBH, WBL = S["WBH"], S["WBL"]
    WBH[...] = jnp.zeros_like(WBH)
    WBL[...] = jnp.zeros_like(WBL)
    for i in range(nq):
        freq = S["v_freq"][2 * xor(q, i) + c]
        high = freq.astype(BF16)
        rest = (freq - high.astype(F32)).astype(BF16)
        WBH[i, 0:64, 0:128] = high
        WBH[i, 64:128, 128:256] = high
        WBL[i, 0:64, 0:128] = rest
        WBL[i, 64:128, 128:256] = rest
    SZ = S["SZ"]
    SZ[...] = jnp.zeros_like(SZ)

    NA = S["NA"]
    cp_tok.wait_recv()
    for s in range(2):
        x = XT[s].astype(F32)
        NA[s * T:(s + 1) * T, :] = (x * rms_scale(x) * gain_a).astype(BF16)

    PH, TV = S["PH"], S["TV"]
    lane_row = lax.broadcasted_iota(jnp.int32, (1, 128), 1)
    cp_car = [None]
    for i in range(nq):
        if i == 1:
            g_in.forward()
            g_out.forward()
            for k in range(1, nq):
                cp_car.append(go(copy(
                    ("car", k), CS.at[pl.ds(2 * xor(q, k), 2)], Cin.at[k], peer(k))))
            g_up.start()
        if i == 2:
            g_in.forward_far()
            g_out.forward_far()
        if i > 0:
            g_in.finish(i)
        bias = vec[2:3, pl.ds(pl.multiple_of(xor(q, i) * 128, 128), 128)]
        bias = jnp.where(c == 0, pltpu.roll(bias, 64, 1), bias)
        bias = jnp.where(lane_row >= 64, bias, 0.0)

        def head(s, _, i=i, bias=bias):
            rows = pl.ds(pl.multiple_of(s * T, T), T)
            pr = mm(NA[rows, :], Win[i])
            t0, t1 = halves(pr)
            TV[i, rows, :] = t1 + bias
            high = t0.astype(BF16)
            rest = (t0 - high.astype(F32)).astype(BF16)
            ang = mm(high, WBH[i]) + (mm(rest, WBH[i]) + mm(high, WBL[i]))
            sin, cos = sincos(ang)
            PH[i, rows, 0:128] = sin[:, :128].astype(BF16)
            PH[i, rows, 128:256] = cos[:, :128].astype(BF16)
            PH[i, rows, 256:384] = sin[:, 128:].astype(BF16)
            PH[i, rows, 384:512] = cos[:, 128:].astype(BF16)
            return 0

        lax.fori_loop(0, 2, head, 0)
        if i == nq - 1:
            g_down.start()
        if i == 0:
            loads["carried"].wait()
            CS[...] = S["v_car"][:, 0].astype(BF16)
            Cin[0] = CS[pl.ds(2 * q, 2)]
            loads["cot"].wait()
            cp_cot = go(copy("cot", XC.at[own_rows], XC.at[own_rows], sib))
            loads["w_up"].wait()
            Wup[0] = S["v_up"][...].astype(BF16)
            loads["w_down"].wait()
            Wdown[0] = S["v_down"][...].astype(BF16)

    lane = lax.broadcasted_iota(jnp.int32, (T, 128), 1)
    first = lane < 64
    row = lax.broadcasted_iota(jnp.int32, (T, 128), 0)
    lane_b = lax.broadcasted_iota(jnp.int32, (T, 256), 1)
    first_b = (lane_b % 128) < 64
    inv_feat = 1.0 / 128.0
    inv_root = 128.0 ** (-0.5)

    def swap(a, h):
        if h < 8:
            return jnp.where((row & h) != 0, pltpu.roll(a, h, 0), pltpu.roll(a, T - h, 0))
        parts = []
        for b in range(T // (2 * h)):
            parts.append(a[(2 * b + 1) * h:(2 * b + 2) * h])
            parts.append(a[2 * b * h:(2 * b + 1) * h])
        return jnp.concatenate(parts, axis=0)

    VV, KK, WW, PP, UU, YY = S["VV"], S["KK"], S["WW"], S["PP"], S["UU"], S["YY"]
    ND, NDL, MX = S["ND"], S["NDL"], S["MX"]
    FS = S["FS"]

    def split_rows(y):
        z = jnp.zeros_like(y)
        return jnp.concatenate([jnp.where(first_b, y, z), jnp.where(first_b, z, y)], axis=0)

    for j in range(npair):
        i0, i1 = 2 * j, 2 * j + 1
        for i in (i0, i1):
            if i > 0:
                cp_car[i].wait_recv()

        def forward(s, _, i0=i0, i1=i1, j=j):
            rows = pl.ds(pl.multiple_of(s * T, T), T)
            for k, i in enumerate((i0, i1)):
                SZ[j, s, k * 64:k * 64 + 64, k * 256:k * 256 + 256] = Cin[i, s, 0]
                SZ[j, s, 128 + k * 64:192 + k * 64, k * 256:k * 256 + 256] = Cin[i, s, 1]
            ta, tb = TV[i0, rows, :], TV[i1, rows, :]
            value = jnp.where(first, ta, pltpu.roll(tb, 64, 1))
            gate = jnp.where(first, pltpu.roll(ta, 64, 1), tb)
            small = jnp.exp(-jnp.abs(gate))
            big = 1.0 / (1.0 + small)
            rest = small * big
            keep = jnp.where(gate >= 0, big, rest)
            write = jnp.where(gate >= 0, rest, big)
            written = write * value
            VV[j, rows, :] = value
            KK[j, rows, :] = keep
            WW[j, rows, :] = write
            scores = [
                (mm_nt(PH[i, rows, 0:256], PH[i, rows, 256:512]) * inv_feat).astype(BF16)
                for i in (i0, i1)]
            total, pre, suf = keep, keep, jnp.ones_like(keep)
            y = jnp.concatenate([written, write], axis=1).astype(BF16)
            left = jnp.concatenate([sc * MK[0] for sc in scores], axis=1)
            acc = mm(left, split_rows(y))
            for lv in range(nlev):
                h = 1 << lv
                if lv > 0:
                    y = jnp.concatenate([suf * written, suf * write], axis=1).astype(BF16)
                YY[j, s, lv] = y
                PP[j, s, lv] = pre.astype(BF16)
                UU[j, s, lv] = suf.astype(BF16)
                left = jnp.concatenate([sc * MK[lv + 1] for sc in scores], axis=1)
                nd = mm(left, split_rows(y)) * pair_cat(pre)
                acc = acc + nd
                NDL[j, s, lv] = nd.astype(BF16)
                other = swap(total, h)
                upper_half = (row & h) != 0
                pre = jnp.where(upper_half, pre * other, pre)
                suf = jnp.where(upper_half, suf, suf * other)
                total = total * other
            PP[j, s, nlev] = pre.astype(BF16)
            phq = jnp.concatenate([PH[i, rows, 0:256] for i in (i0, i1)], axis=1)
            phk = jnp.concatenate([PH[i, rows, 256:512] for i in (i0, i1)], axis=1)
            nd = mm_nt(phq, SZ[j, s]) * (pair_cat(pre) * inv_root)
            NDL[j, s, nlev] = nd.astype(BF16)
            acc = acc + nd
            ND[j, s] = acc
            num, den = halves(acc)
            MX[rows, j * 128:(j + 1) * 128] = (
                num * lax.rsqrt(den * den + DEN_FLOOR)).astype(BF16)
            y = jnp.concatenate([suf * written, suf * write], axis=1).astype(BF16)
            new = mm_tn(y, phk) * inv_root
            last = jnp.transpose(pre[T - 128:, :], (1, 0))[:, 127:128]
            for k, i in enumerate((i0, i1)):
                kept = last[k * 64:k * 64 + 64, :]
                for z in range(2):
                    block = new[z * 128 + k * 64:z * 128 + k * 64 + 64, k * 256:k * 256 + 256]
                    FS[i, s, z] = (kept * Cin[i, s, z].astype(F32) + block).astype(BF16)
            return 0

        lax.fori_loop(0, 2, forward, 0)

    AP, AQ, MID, NF = S["AP"], S["AQ"], S["MID"], S["NF"]
    g_up.forward()
    for i in range(1, nq):
        g_out.finish(i)
    wout = jnp.concatenate([Wout[i] for i in range(nq)], axis=0)
    AP[...] = mm(MX[...], wout)
    cp_att = go(copy("att", AP, AQ, sib))
    g_down.forward()
    cp_att.wait_recv()
    for s in range(2):
        rows = slice(s * T, (s + 1) * T)
        middle = XT[s].astype(F32) + (AP[rows, :] + AQ[rows, :])
        MID[rows, :] = middle
        NF[rows, :] = (middle * rms_scale(middle) * gain_f).astype(BF16)

    FO, DN = AP, S["DN"]
    cp_att.wait_send()
    cp_cot.wait_recv()
    NFT, CT = S["NFT"], XC
    NFT[...] = jnp.transpose(NF[...], (1, 0))

    class Scatter:
        def __init__(self, name):
            self.name = name
            self.own, self.out, self.mid, self.got = (S[name + k] for k in "ospr")
            self.half = self.own.shape[0] // 2
            self.top, self.bottom = pl.ds(0, self.half), pl.ds(self.half, self.half)

        def send(self, key, src, dst, i):
            cp = go(copy((self.name, key), src, dst, peer(i)))
            setattr(self, key, cp)

        def put(self, i, value):
            if i == 0:
                self.own[...] = value
                return
            out = self.out
            out[i - 1] = value.astype(BF16)
            if i == 1:
                self.send("a1", out.at[0].at[self.top], self.got.at[0].at[self.top], 1)
            elif i == 2:
                self.send("a2", out.at[1].at[self.bottom], self.got.at[1].at[self.bottom], 2)
            else:
                self.send("p1", out.at[2].at[self.top], self.mid.at[0], 1)
                self.send("p2", out.at[2].at[self.bottom], self.mid.at[1], 2)

        def middle(self):
            out, half = self.out, self.half
            self.p1.wait_recv()
            out[1, :half] = (out[1, :half].astype(F32) + self.mid[0].astype(F32)).astype(BF16)
            self.send("b2", out.at[1].at[self.top], self.got.at[1].at[self.top], 2)
            self.p2.wait_recv()
            out[0, half:] = (out[0, half:].astype(F32) + self.mid[1].astype(F32)).astype(BF16)
            self.send("b1", out.at[0].at[self.bottom], self.got.at[0].at[self.bottom], 1)

        def total(self):
            for cp in (self.a1, self.a2, self.b1, self.b2):
                cp.wait_recv()
            return self.own[...] + (self.got[0].astype(F32) + self.got[1].astype(F32))

    sc_up, sc_down, sc_in, sc_out = (Scatter(n) for n in ("gu", "gd", "gi", "go"))
    for i in range(nq):
        if i == 1:
            g_up.forward_far()
            g_down.forward_far()
        if i > 0:
            g_up.finish(i)
            g_down.finish(i)
        up, down = Wup[i], Wdown[i]
        pre = mm(NF[...], up)
        square = pre * pre
        th = jnp.tanh(0.7978845608028654 * (pre + 0.044715 * pre * square))
        hidden = (0.5 * pre * (1.0 + th)).astype(BF16)
        slope = 0.5 * (1.0 + th) + 0.5 * pre * (1.0 - th * th) * (
            0.7978845608028654 * (1.0 + 0.134145 * square))
        d_pre = (mm_nt(CT[...], down) * slope).astype(BF16)
        fo = mm(hidden, down)
        dn = mm_nt(d_pre, up)
        if i == 0:
            FO[...] = fo
            DN[...] = dn
        else:
            FO[...] += fo
            DN[...] += dn
        sc_down.put(i, mm_tn(hidden, CT[...]))
        sc_up.put(i, mm(NFT[...], d_pre))
    FOR, DNR = S["FOR"], S["DNR"]
    cp_dn = go(copy("dn", DN, DNR, sib))
    cp_fo = go(copy("fo", FO.at[pl.ds((1 - c) * T, T)], FOR, sib))
    cp_dn.wait_recv()
    DA, DM, DMI = S["DA"], S["DM"], S["DMI"]
    for s in range(2):
        rows = slice(s * T, (s + 1) * T)
        middle = MID[rows, :]
        scale = rms_scale(middle)
        unit = middle * scale
        grad = DN[rows, :] + DNR[rows, :]
        d_mid = XC[rows, :].astype(F32) + norm_back(grad, unit, scale, gain_f)
        DA[rows, :] = d_mid.astype(BF16)
        gain_grad = jnp.sum(grad * unit, axis=0, keepdims=True)

        @pl.when(c == s)
        def _(gain_grad=gain_grad, d_mid=d_mid):
            DMI[...] = d_mid
            for t in range(D // 128):
                VEC[D // 128 + t:D // 128 + t + 1, :] = gain_grad[:, t * 128:(t + 1) * 128]

    cp_fo.wait_recv()
    S["block_out"][...] = (MID[own_rows, :] + (FO[own_rows, :] + FOR[...])).astype(BF16)
    DM[...] = mm_nt(DA[...], wout)
    go_all = mm_tn(MX[...], DA[...])
    for i in range(nq):
        sc_out.put(i, go_all[64 * i:64 * i + 64])

    XL, DPJ, CG = S["XL"], S["DPJ"], S["CG"]
    ZD, ZU, ZI = S["ZD"], S["ZU"], S["ZI"]
    NS = S["NS"]
    LT = D // 128

    def fold(z):
        return jnp.sum((z * z).reshape(z.shape[0] // 8, 8, 128), axis=0)

    def tiles_of(a):
        return [a[:, t * 128:(t + 1) * 128].astype(BF16) for t in range(a.shape[1] // 128)]

    def lay(Z, parts):
        at = 0
        for part in parts:
            Z[at:at + part.shape[0], :] = part
            at += part.shape[0]

    def reduce_dp(name, Z, R, out):
        piece = Z.shape[0] // ndp
        mine = pl.ds(pl.multiple_of(me_dp * piece, 16), piece)
        scatter = [copy((name, "rs", k), Z.at[pl.ds(xor(me_dp, k) * piece, piece)], R.at[k - 1],
                        dpeer(k)) for k in range(1, ndp)]
        spread = [copy((name, "ag", k), out.at[mine], out.at[mine], dpeer(k))
                  for k in range(1, ndp)]

        def start():
            for cp in scatter:
                go(cp)

        def middle():
            for cp in scatter:
                cp.wait_recv()
            total = tree_sum([Z[mine, :].astype(F32)] + [R[k].astype(F32) for k in range(ndp - 1)])
            total = total.astype(BF16)
            out[mine, :] = total
            for cp in spread:
                go(cp)
            return fold(total.astype(F32))

        def finish():
            for cp in spread:
                cp.wait_recv()
        return start, middle, finish

    nbit = ndp.bit_length() - 1

    class Halving:
        def __init__(self, name, Z, R, out):
            self.Z, self.R, self.out = Z, R, out
            size, first, at = Z.shape[0], 0, 0
            self.rs, self.ag, self.keep, self.land = [], [], [], []
            for b in range(nbit):
                bit = lax.div(me_dp, 1 << b) % 2
                size //= 2
                keep, give = first + bit * size, first + (1 - bit) * size
                land = R.at[pl.ds(at, size)]
                self.keep.append(pl.ds(pl.multiple_of(keep, 16), size))
                self.land.append(pl.ds(at, size))
                self.rs.append(copy((name, "rs", b), Z.at[pl.ds(give, size)], land, dpeer(1 << b)))
                seg = pl.ds(pl.multiple_of(keep, 16), size)
                self.ag.append(copy((name, "ag", b), out.at[seg], out.at[seg], dpeer(1 << b)))
                first, at = keep, at + size
            self.at = 0
            self.square = None

        def start(self):
            go(self.rs[0])

        def step(self):
            for _ in range(max(nbit // 2, 1)):
                k = self.at
                self.at += 1
                if k < nbit:
                    self.rs[k].wait_recv()
                    rows = self.keep[k]
                    total = self.Z[rows, :].astype(F32) + self.R[self.land[k], :].astype(F32)
                    total = total.astype(BF16)
                    if k + 1 < nbit:
                        self.Z[rows, :] = total
                        go(self.rs[k + 1])
                    else:
                        self.out[rows, :] = total
                        go(self.ag[k])
                        self.square = fold(total.astype(F32))
                else:
                    b = 2 * nbit - 1 - k
                    self.ag[b].wait_recv()
                    if b > 0:
                        go(self.ag[b - 1])

    zd = Halving("zd", ZD, S["ZDR"], S["ZDO"])
    zu = Halving("zu", ZU, S["ZUR"], S["ZUO"])
    zi_start, zi_middle, zi_finish = reduce_dp("zi", ZI, S["ZIR"], S["ZIO"])

    def hook_0():
        sc_down.middle()
        sc_up.middle()
        sc_out.middle()

    def hook_1():
        lay(ZD, tiles_of(sc_down.total()))
        zd.start()

    def hook_2():
        zd.step()
        lay(ZU, tiles_of(sc_up.total()) + tiles_of(sc_out.total()))
        zu.start()

    NAT = NFT
    NAT[...] = jnp.transpose(NA[...], (1, 0))
    for j in (1, 0):
        i0, i1 = 2 * j, 2 * j + 1

        bias_sum = jnp.zeros((1, 128), F32)
        for s in range(2):
            rows = pl.ds(s * T, T)
            if s == 1:
                if j == 1:
                    hook_0()
                else:
                    hook_2()
            dm = DM[rows, j * 128:(j + 1) * 128]
            num, den = halves(ND[j, s])
            r = lax.rsqrt(den * den + DEN_FLOOR)
            d_num = dm * r
            d_den = -(d_num * num) * den * (r * r)
            g = jnp.concatenate([d_num, d_den], axis=1)
            value, keep, write = VV[j, rows, :], KK[j, rows, :], WW[j, rows, :]
            written = write * value
            scores = [
                (mm_nt(PH[i, rows, 256:512], PH[i, rows, 0:256]) * inv_feat).astype(BF16)
                for i in (i0, i1)]
            levels = LV[...]
            z16 = jnp.zeros((T, 256), BF16)
            gb = g.astype(BF16)
            g0, g1 = jnp.where(first_b, gb, z16), jnp.where(first_b, z16, gb)
            left = jnp.concatenate([sc * MT[0] for sc in scores], axis=1)
            ab = mm(left, jnp.concatenate([g0, g1], axis=0))
            y = YY[j, s, 0]
            ds0 = mm_nt(g0, y)
            ds1 = mm_nt(g1, y)
            for lv in range(nlev):
                h = 1 << lv
                pg = (pair_cat(PP[j, s, lv].astype(F32)) * g).astype(BF16)
                g0, g1 = jnp.where(first_b, pg, z16), jnp.where(first_b, z16, pg)
                left = jnp.concatenate([sc * MT[lv + 1] for sc in scores], axis=1)
                part = mm(left, jnp.concatenate([g0, g1], axis=0)) * pair_cat(UU[j, s, lv].astype(F32))
                ab = ab + part
                pa, pb = halves(part)
                from_key = written * pa + write * pb
                oa, ob = halves(g * NDL[j, s, lv].astype(F32))
                XL[lv * T:(lv + 1) * T, :] = jnp.where(
                    (row & h) != 0, oa + ob, from_key).astype(BF16)
                y = YY[j, s, lv]
                hit = levels == float(lv + 1)
                ds0 = jnp.where(hit, mm_nt(g0, y), ds0)
                ds1 = jnp.where(hit, mm_nt(g1, y), ds1)
            causal = levels >= 0.0
            ds0 = jnp.where(causal, ds0, 0.0).astype(BF16)
            ds1 = jnp.where(causal, ds1, 0.0).astype(BF16)
            oa, ob = halves(g * NDL[j, s, nlev].astype(F32))
            XL[nlev * T:, :] = (oa + ob).astype(BF16)
            pg = (pair_cat(PP[j, s, nlev].astype(F32)) * g).astype(BF16)
            phq = jnp.concatenate([PH[i, rows, 0:256] for i in (i0, i1)], axis=1)
            opening = mm(pg, SZ[j, s]) * inv_root
            cg = mm_tn(pg, phq) * inv_root
            for k, i in enumerate((i0, i1)):
                for z in range(2):
                    CG[i, s, z] = cg[z * 128 + k * 64:z * 128 + k * 64 + 64,
                                     k * 256:k * 256 + 256].astype(BF16)
            d_log = mm(TRI[...], XL[...])
            a, b = halves(ab)
            d_value = write * a
            d_write = value * a + b
            d_gate = write * (d_log - keep * d_write)
            tiles = (jnp.where(first, d_value, pltpu.roll(d_gate, 64, 1)),
                     jnp.where(first, pltpu.roll(d_value, 64, 1), d_gate))
            for k, (i, ds) in enumerate(((i0, ds0), (i1, ds1))):
                pq, pk = PH[i, rows, 0:256], PH[i, rows, 256:512]
                dq = mm(ds, pk) * inv_feat + opening[:, k * 256:k * 256 + 256]
                dk = mm_tn(ds, pq) * inv_feat
                pq, pk = pq.astype(F32), pk.astype(F32)
                aq = pq[:, 128:] * dq[:, :128] - pq[:, :128] * dq[:, 128:]
                ak = pk[:, 128:] * dk[:, :128] - pk[:, :128] * dk[:, 128:]
                d_ang = jnp.concatenate([aq, ak], axis=1).astype(BF16)
                DPJ[i, rows, 0:128] = mm_nt(d_ang, WBH[i]).astype(BF16)
                DPJ[i, rows, 128:256] = tiles[k].astype(BF16)
            bias_sum = bias_sum + jnp.sum(d_gate, axis=0, keepdims=True)

        for k, i in enumerate((i0, i1)):
            VEC[pl.ds(2 * D // 128 + 2 * xor(q, i) + c, 1), :] = (
                bias_sum if k else pltpu.roll(bias_sum, 64, 1))

        for i in (i1, i0):
            sc_in.put(i, mm(NAT[...], DPJ[i]))
        if j == 1:
            hook_1()

    sc_in.middle()
    zd.step()
    zu.step()
    CR, FR = S["CR"], S["FR"]
    DX = FO
    cp_fo.wait_send()
    DX[...] = mm_nt(DPJ[0], Win[0])
    for i in range(1, nq):
        DX[...] += mm_nt(DPJ[i], Win[i])
    DXR = S["DXR"]
    cp_dx = go(copy("dx", DX.at[pl.ds((1 - c) * T, T)], DXR, sib))
    lay(ZI, tiles_of(sc_in.total()))
    zi_start()
    cp_cg = [None] + [
        go(copy(("cg", i), CG.at[i], CR.at[pl.ds(2 * q, 2)], peer(i))) for i in range(1, nq)]
    cp_fin = [None] + [
        go(copy(("fin", i), FS.at[i], FR.at[pl.ds(2 * q, 2)], peer(i))) for i in range(1, nq)]
    CR[pl.ds(2 * q, 2)] = CG[0]
    FR[pl.ds(2 * q, 2)] = FS[0]
    zd.step()
    zu.step()
    cp_dx.wait_recv()
    x = XT[c].astype(F32)
    scale = rms_scale(x)
    unit = x * scale
    grad = DX[own_rows, :] + DXR[...]
    S["token_grad"][...] = DMI[...] + norm_back(grad, unit, scale, gain_a)
    gain_grad = jnp.sum(grad * unit, axis=0, keepdims=True)
    for t in range(LT):
        VEC[t:t + 1, :] = gain_grad[:, t * 128:(t + 1) * 128]
    VR = S["VR"]
    VS = S["VS"]
    cp_v = go(copy("v0", VEC, VR.at[0], sib))

    zu.step()
    cp_v.wait_recv()
    VS[0] = VEC[...] + VR[0]
    cp_vs = [go(copy(("v1", i), VS.at[0], VR.at[i], peer(i))) for i in range(1, nq)]
    for cp in cp_vs:
        cp.wait_recv()
    VS[1] = tree_sum([VS[0]] + [VR[i] for i in range(1, nq)])
    cp_vd = [go(copy(("v2", k), VS.at[1], VR.at[nq - 1 + k], dpeer(k))) for k in range(1, ndp)]
    NS[0] = zd.square + zu.square + zi_middle()
    zd.step()
    zu.step()
    NR = S["NR"]
    cp_n = [go(copy(("n", r), NS.at[0], NR.at[r - 1], {"mp": xor(m, r)})) for r in range(1, 2 * nq)]
    for cp in cp_vd:
        cp.wait_recv()
    vtot = tree_sum([VS[1]] + [VR[nq - 1 + k] for k in range(1, ndp)])
    g_vec = S["g_vec"]
    for t in range(LT):
        part = slice(t * 128, (t + 1) * 128)
        g_vec[0:1, part] = vtot[t:t + 1, :]
        g_vec[1:2, part] = vtot[LT + t:LT + t + 1, :]
        even = vtot[2 * LT + 2 * t:2 * LT + 2 * t + 1, :]
        odd = vtot[2 * LT + 2 * t + 1:2 * LT + 2 * t + 2, :]
        g_vec[2:3, part] = jnp.where(lane_row < 64, pltpu.roll(even, 64, 1), odd)
    for cp in cp_n:
        cp.wait_recv()
    NS[1] = tree_sum([NS[0]] + [NR[r] for r in range(2 * nq - 1)])
    cp_m = [go(copy(("m", k), NS.at[1], NR.at[2 * nq - 2 + k], dpeer(k))) for k in range(1, ndp)]

    lane_v = lax.broadcasted_iota(jnp.int32, VEC.shape, 1)
    row_v = lax.broadcasted_iota(jnp.int32, VEC.shape, 0)
    vmask = (row_v < 2 * LT) | (lane_v >= 64)
    vsq = fold(jnp.where(vmask, vtot, 0.0))

    def unlay(Z, first, shape):
        n = shape[0]
        return jnp.concatenate(
            [Z[first + t * n:first + (t + 1) * n, :] for t in range(shape[1] // 128)], axis=1)

    S["g_down"][...] = unlay(S["ZDO"], 0, (FH, D))
    S["g_up"][...] = unlay(S["ZUO"], 0, (D, FH))
    S["g_out"][...] = unlay(S["ZUO"], D * FH // 128, (64, D))
    zi_finish()
    S["g_in"][...] = unlay(S["ZIO"], 0, (D, 256))
    for i in range(1, nq):
        cp_fin[i].wait_recv()
        cp_cg[i].wait_recv()
    S["fin"][...] = FR[...]
    S["cgrad"][...] = CR[...]
    for cp in cp_m:
        cp.wait_recv()
    S["sq"][...] = tree_sum([NS[1]] + [NR[2 * nq - 2 + k] for k in range(1, ndp)]) + vsq
    for cp in sends:
        if cp is not cp_fo and cp is not cp_att:
            cp.wait_send()


def layer_call(ndp, nmp, args, shapes):
    T, D = shapes["tok"].shape
    nq = nmp // 2
    FH = shapes["w_up"].shape[1]
    nlev = (T - 1).bit_length()
    npair = nq // 2
    nseq = 2 * nq
    lt = D // 128
    zd = D * FH // 128
    zu = (D * FH + 64 * D) // 128
    zi = D * 256 // 128
    vrows = 2 * lt + nseq
    R = nq - 1
    V = pltpu.VMEM
    scratch = dict(
        XT=V((2, T, D), BF16), XC=V((2 * T, D), BF16),
        Win=V((nq, D, 256), BF16), Wout=V((nq, 64, D), BF16),
        Wup=V((nq, D, FH), BF16), Wdown=V((nq, FH, D), BF16),
        CS=V((nseq, 2, 64, 256), BF16), Cin=V((nq, 2, 2, 64, 256), BF16),
        LV=V((T, T), F32), MK=V((nlev + 1, T, T), BF16), MT=V((nlev + 1, T, T), BF16),
        TRI=V((T, (nlev + 1) * T), BF16), VEC=V((vrows, 128), F32),
        WBH=V((nq, 128, 256), BF16), WBL=V((nq, 128, 256), BF16),
        SZ=V((npair, 2, 256, 512), BF16), NA=V((2 * T, D), BF16),
        PH=V((nq, 2 * T, 512), BF16), TV=V((nq, 2 * T, 128), F32),
        VV=V((npair, 2 * T, 128), F32), KK=V((npair, 2 * T, 128), F32),
        WW=V((npair, 2 * T, 128), F32), PP=V((npair, 2, nlev + 1, T, 128), BF16),
        UU=V((npair, 2, nlev, T, 128), BF16), YY=V((npair, 2, nlev, T, 256), BF16),
        ND=V((npair, 2, T, 256), F32), NDL=V((npair, 2, nlev + 1, T, 256), BF16),
        MX=V((2 * T, 64 * nq), BF16), FS=V((nq, 2, 2, 64, 256), BF16),
        FR=V((nseq, 2, 64, 256), BF16), AP=V((2 * T, D), F32), AQ=V((2 * T, D), F32),
        MID=V((2 * T, D), F32), NF=V((2 * T, D), BF16),
        DN=V((2 * T, D), F32), NFT=V((D, 2 * T), BF16),
        guo=V((D, FH), F32), gus=V((R, D, FH), BF16),
        gup=V((2, D // 2, FH), BF16), gur=V((2, D, FH), BF16),
        gdo=V((FH, D), F32), gds=V((R, FH, D), BF16),
        gdp=V((2, FH // 2, D), BF16), gdr=V((2, FH, D), BF16),
        gio=V((D, 256), F32), gis=V((R, D, 256), BF16),
        gip=V((2, D // 2, 256), BF16), gir=V((2, D, 256), BF16),
        goo=V((64, D), F32), gos=V((R, 64, D), BF16),
        gop=V((2, 32, D), BF16), gor=V((2, 64, D), BF16),
        FOR=V((T, D), F32), DNR=V((2 * T, D), F32),
        DA=V((2 * T, D), BF16), DM=V((2 * T, 64 * nq), F32), DMI=V((T, D), F32),
        XL=V(((nlev + 1) * T, 128), BF16), DPJ=V((nq, 2 * T, 256), BF16),
        CG=V((nq, 2, 2, 64, 256), BF16), CR=V((nseq, 2, 64, 256), BF16),
        DXR=V((T, D), F32), ZD=V((zd, 128), BF16), ZU=V((zu, 128), BF16),
        ZI=V((zi, 128), BF16),
        ZDR=V((zd, 128), BF16), ZUR=V((zu, 128), BF16),
        ZIR=V((ndp - 1, zi // ndp, 128), BF16),
        ZDO=V((zd, 128), BF16), ZUO=V((zu, 128), BF16), ZIO=V((zi, 128), BF16),
        VR=V((nq + ndp, vrows, 128), F32), VS=V((2, vrows, 128), F32),
        NR=V((2 * nq - 2 + ndp, 8, 128), F32), NS=V((2, 8, 128), F32),
        v_in=V((2 * D, 128), F32), v_vec=V((3, D), F32), v_freq=V(shapes["freq"].shape, F32),
        v_out=V((64, D), F32), v_car=V(shapes["carried"].shape, F32),
        v_up=V((D, FH), F32), v_down=V((FH, D), F32),
    )
    nsem = 80 + 3 * R + 9 * ndp + 2 * nq
    scratch["lsem"] = pltpu.SemaphoreType.DMA((len(args),))
    scratch["ssem"] = pltpu.SemaphoreType.DMA((nsem,))
    scratch["rsem"] = pltpu.SemaphoreType.DMA((nsem,))
    outs = dict(
        block_out=((T, D), BF16), token_grad=((T, D), F32),
        fin=((nseq, 2, 64, 256), BF16), cgrad=((nseq, 2, 64, 256), BF16),
        g_in=((D, 256), BF16), g_out=((64, D), BF16),
        g_up=((D, FH), BF16), g_down=((FH, D), BF16),
        g_vec=((3, D), F32), sq=((8, 128), F32))
    names = list(args) + list(outs) + list(scratch)
    cfg = dict(names=names, ndp=ndp, nq=nq, T=T, D=D, nlev=nlev, FH=FH)
    vm = pl.BlockSpec(memory_space=pltpu.VMEM)
    res = pl.pallas_call(
        functools.partial(layer_kernel, cfg),
        out_shape=[jax.ShapeDtypeStruct(s, d) for s, d in outs.values()],
        in_specs=[pl.BlockSpec(memory_space=pl.ANY)] * len(args),
        out_specs=[vm] * len(outs),
        scratch_shapes=list(scratch.values()),
        compiler_params=pltpu.CompilerParams(
            collective_id=0, has_side_effects=True, vmem_limit_bytes=62 * 2**20),
        name="layer",
    )(*args.values())
    return dict(zip(outs, res))


def adam(w, g, first, second, rate, decay):
    first_new = B1 * first + (1.0 - B1) * g
    second_new = B2 * second + (1.0 - B2) * g * g
    first_hat = first_new / (1.0 - B1**STEP)
    second_hat = second_new / (1.0 - B2**STEP)
    w_new = w - rate * (first_hat / (jnp.sqrt(second_hat) + ADAM_EPS) + decay * w)
    return first_new, second_new, w_new


def adam_kernel(names, nout, *refs):
    S = dict(zip(names, refs))
    norm = jnp.sqrt(jnp.sum(S["sq"][...]))
    factor = CLIP / jnp.maximum(norm, CLIP)

    @pl.when(pl.program_id(0) == 0)
    def _():
        S["norm"][0, 0] = norm
        g = S["g_v"][...] * factor
        res = adam(S["v0"][...], g, S["v1"][...], S["v2"][...], RATE_VECTOR, 0.0)
        for k in range(3):
            S["nv%d" % k][...] = res[k]

    for key in "oud":
        g = S["g_" + key][...].astype(F32) * factor
        res = adam(S[key + "0"][...], g, S[key + "1"][...], S[key + "2"][...], RATE_MATRIX, DECAY)
        for k in range(3):
            S["n%s%d" % (key, k)][...] = res[k]
        S["n%s3" % key][...] = res[2].astype(BF16)
    count = S["i0"].shape[0] // 2
    for t in range(2):
        rows = pl.ds(t, count, 2)
        lanes = slice(t * 128, (t + 1) * 128)
        g = S["g_i"][:, lanes].astype(F32) * factor
        res = adam(S["i0"][rows, :], g, S["i1"][rows, :], S["i2"][rows, :], RATE_MATRIX, DECAY)
        for k in range(3):
            S["ni%d" % k][rows, :] = res[k]
        S["ni3"][:, lanes] = res[2].astype(BF16)
    S["n_block_out"][...] = S["block_out"][...]
    S["n_token_grad"][...] = S["token_grad"][...]
    S["n_fin"][...] = S["fin"][...].astype(F32)
    S["n_cgrad"][...] = S["cgrad"][...].astype(F32)


def adam_call(res, params):
    steps = 4

    def cut(shape):
        block = (shape[0] // steps,) + tuple(shape[1:])
        return pl.BlockSpec(block, lambda g: (g,) + (0,) * (len(shape) - 1))

    def whole(shape):
        return pl.BlockSpec(tuple(shape), lambda g: (0,) * len(shape))

    ins, in_specs, outs, out_specs, names, onames = [], [], [], [], [], []

    def take(name, a, spec):
        names.append(name)
        ins.append(a)
        in_specs.append(spec(a.shape))

    def give(name, shape, dtype, spec):
        onames.append(name)
        outs.append(jax.ShapeDtypeStruct(shape, dtype))
        out_specs.append(spec(shape))

    take("sq", res["sq"], whole)
    for key, full in zip("vioud", ("g_vec", "g_in", "g_out", "g_up", "g_down")):
        spec = whole if key == "v" else cut
        take("g_" + key, res[full], spec)
        for k, a in enumerate(params[key]):
            take("%s%d" % (key, k), a, spec)
            give("n%s%d" % (key, k), a.shape, F32, spec)
        if key != "v":
            give("n%s3" % key, res[full].shape, BF16, spec)
    for name in ("block_out", "token_grad", "fin", "cgrad"):
        a = res[name]
        take(name, a, cut)
        give("n_" + name, a.shape, F32 if name in ("fin", "cgrad") else a.dtype, cut)
    onames.append("norm")
    outs.append(jax.ShapeDtypeStruct((1, 1), F32))
    out_specs.append(pl.BlockSpec(memory_space=pltpu.SMEM))
    got = pl.pallas_call(
        functools.partial(adam_kernel, names + onames, len(onames)),
        grid=(steps,), out_shape=outs, in_specs=in_specs, out_specs=out_specs,
        compiler_params=pltpu.CompilerParams(vmem_limit_bytes=int(63.9 * 2**20)),
        name="adam",
    )(*ins)
    got = dict(zip(onames, got))
    new = {key: tuple(got["n%s%d" % (key, k)] for k in range(3 if key == "v" else 4))
           for key in "vioud"}
    for name in ("block_out", "token_grad", "fin", "cgrad"):
        new[name] = got["n_" + name]
    new["norm"] = got["norm"]
    return new


def shards(
    tokens, cotangent, carried, frequencies, vectors, vectors_first, vectors_second,
    mix_in, mix_in_first, mix_in_second, mix_out, mix_out_first, mix_out_second,
    ffn_up, ffn_up_first, ffn_up_second, ffn_down, ffn_down_first, ffn_down_second,
    *, ndp, nmp,
):
    D = tokens.shape[1]
    FH = ffn_up.shape[1]
    args = dict(
        tok=tokens, cot=cotangent, carried=carried,
        freq=jnp.swapaxes(frequencies, 1, 2), vec=vectors,
        w_in=mix_in.reshape(2 * D, 128), w_out=mix_out, w_up=ffn_up, w_down=ffn_down)
    res = layer_call(ndp, nmp, args, args)
    flat = (2 * D, 128)
    params = dict(
        v=(vectors, vectors_first, vectors_second),
        i=tuple(a.reshape(flat) for a in (mix_in, mix_in_first, mix_in_second)),
        o=(mix_out, mix_out_first, mix_out_second),
        u=(ffn_up, ffn_up_first, ffn_up_second),
        d=(ffn_down, ffn_down_first, ffn_down_second))
    new = adam_call(res, params)
    shape = mix_in.shape
    return (
        new["block_out"], new["fin"].reshape(carried.shape), new["token_grad"],
        new["cgrad"].reshape(carried.shape), new["norm"][0, 0],
        *new["v"], *(a.reshape(shape) for a in new["i"]), *new["o"], *new["u"], *new["d"])


def solution(mesh):
    tok = P(("dp", "mp"), None)
    car = P("dp", "mp", None, None, None)
    head = P(None, "mp", None)
    rowp = P("mp", None)
    colp = P(None, "mp")
    rep = P()
    in_specs = (tok, tok, car, rep, rep, rep, rep) + (head,) * 3 + (rowp,) * 3 + (
        colp,) * 3 + (rowp,) * 3
    out_specs = (tok, car, tok, car, rep, rep, rep, rep) + (head,) * 4 + (rowp,) * 4 + (
        colp,) * 4 + (rowp,) * 4
    body = functools.partial(shards, ndp=mesh.shape["dp"], nmp=mesh.shape["mp"])
    return jax.shard_map(body, mesh=mesh, in_specs=in_specs, out_specs=out_specs, check_vma=False)
```

```python
import functools

import jax
import jax.numpy as jnp
from jax import lax
from jax.experimental import pallas as pl
from jax.experimental.pallas import tpu as pltpu
from jax.sharding import PartitionSpec as P

STEP = 10
NORM_EPS = 1e-06
DEN_FLOOR = 0.25
CLIP = 1.0
B1 = 0.9
B2 = 0.999
ADAM_EPS = 1e-08
DECAY = 0.1
RATE_MATRIX = 0.05
RATE_VECTOR = 0.6
MESH = pl.DeviceIdType.MESH
F32 = jnp.float32
BF16 = jnp.bfloat16

SIN = (9.99999996e-01, -1.66666578e-01, 8.33304727e-03, -1.98087928e-04, 2.60457914e-06)
COS = (1.0, -4.99999993e-01, 4.16666357e-02, -1.38883546e-03, 2.47598090e-05, -2.60452002e-07)
PI_A, PI_B, PI_C = 3.140625, 0.0009675025939941406, 1.5099579897537296e-07


def mm(a, b):
    return jnp.dot(a, b, preferred_element_type=F32)


def mm_nt(a, b):
    return lax.dot_general(a, b, (((1,), (1,)), ((), ())), preferred_element_type=F32)


def mm_tn(a, b):
    return lax.dot_general(a, b, (((0,), (0,)), ((), ())), preferred_element_type=F32)


def horner(coefs, y):
    acc = jnp.full_like(y, coefs[-1])
    for coef in coefs[-2::-1]:
        acc = acc * y + coef
    return acc


def sincos(x):
    turns = jnp.floor(x * 0.3183098861837907 + 0.5)
    r = ((x - turns * PI_A) - turns * PI_B) - turns * PI_C
    sign = 1.0 - 2.0 * (turns - 2.0 * jnp.floor(turns * 0.5))
    y = r * r
    return sign * (r * horner(SIN, y)), sign * horner(COS, y)


def rms_scale(x):
    return lax.rsqrt(jnp.mean(x * x, axis=-1, keepdims=True) + NORM_EPS)


def norm_back(grad, unit, scale, gain):
    e = grad * gain
    return scale * (e - unit * jnp.mean(e * unit, axis=-1, keepdims=True))


def xor(a, bits):
    out = a
    step = 1
    while step <= bits:
        if bits & step:
            out = out + step - 2 * step * (lax.div(a, step) % 2)
        step *= 2
    return out


def tree_sum(terms):
    terms = list(terms)
    if len(terms) == 1:
        return terms[0]
    half = len(terms) // 2
    return tree_sum(terms[:half]) + tree_sum(terms[half:])


def halves(a):
    return a[:, :128], a[:, 128:]


def pair_cat(a):
    return jnp.concatenate([a, a], axis=1)


def layer_kernel(cfg, *refs):
    names = cfg["names"]
    S = dict(zip(names, refs))
    ndp, nq, T, D = cfg["ndp"], cfg["nq"], cfg["T"], cfg["D"]
    nlev = cfg["nlev"]
    FH = cfg["FH"]
    npair = nq // 2
    rows2 = 2 * T
    me_dp = lax.axis_index("dp")
    m = lax.axis_index("mp")
    c = m % 2
    q = lax.div(m, 2)
    sib = {"mp": q * 2 + (1 - c)}
    ssem, rsem = S["ssem"], S["rsem"]
    sem_of = {}

    def sem(key):
        return sem_of.setdefault(key, len(sem_of))

    def peer(i):
        return {"mp": xor(q, i) * 2 + c}

    def dpeer(k):
        return {"dp": xor(me_dp, k)}

    def copy(key, src, dst, dev):
        k = sem(key)
        return pltpu.make_async_remote_copy(
            src_ref=src, dst_ref=dst, send_sem=ssem.at[k], recv_sem=rsem.at[k],
            device_id=dev, device_id_type=MESH)

    XT, XC = S["XT"], S["XC"]
    lsem = S["lsem"]
    own_rows = pl.ds(pl.multiple_of(c * T, T), T)
    plan = [("w_in", S["v_in"]), ("tok", XT.at[c]), ("vec", S["v_vec"]), ("freq", S["v_freq"]),
            ("w_out", S["v_out"]), ("carried", S["v_car"]), ("cot", XC.at[own_rows]),
            ("w_up", S["v_up"]), ("w_down", S["v_down"])]
    loads = {}
    for k, (name, dst) in enumerate(plan):
        loads[name] = pltpu.make_async_copy(S[name], dst, lsem.at[k])
        loads[name].start()

    barrier = pltpu.get_barrier_semaphore()
    count = 0
    for r in range(1, 2 * nq):
        pl.semaphore_signal(barrier, inc=1, device_id={"mp": xor(m, r)}, device_id_type=MESH)
        count += 1
    for k in range(1, ndp):
        pl.semaphore_signal(barrier, inc=1, device_id=dpeer(k), device_id_type=MESH)
        count += 1

    Win, Wout, Wup, Wdown = S["Win"], S["Wout"], S["Wup"], S["Wdown"]
    w_in = S["v_in"]
    loads["w_in"].wait()
    Win[0] = jnp.concatenate(
        [w_in[pl.ds(0, D, 2), :], w_in[pl.ds(1, D, 2), :]], axis=1).astype(BF16)
    loads["w_out"].wait()
    Wout[0] = S["v_out"][...].astype(BF16)
    loads["tok"].wait()
    pl.semaphore_wait(barrier, count)

    sends = []
    puts = []

    def put(src, dst):
        cp = pltpu.make_async_copy(src, dst, S["osem"].at[len(puts)])
        cp.start()
        puts.append(cp)

    def go(cp):
        cp.start()
        sends.append(cp)
        return cp

    side = me_dp % 2

    class Gather:
        def __init__(self, name, W):
            part = W.shape[1] // 4

            def rows(first, n):
                return pl.ds(pl.multiple_of(first * part, 16), n * part)

            def cp(key, i, k, r, dev):
                return copy((name, key, k), W.at[i].at[r], W.at[k].at[r], dev)

            self.direct = {i: cp("d", 0, i, rows(side, 3), peer(i)) for i in (1, 2)}
            self.cross = (cp("x", 2, 3, rows(2 * side, 1), peer(1)),
                          cp("y", 1, 3, rows(2 * side + 1, 1), peer(2)))
            self.swap = {i: cp("z", i, i, rows(3 * side, 1), dpeer(1)) for i in (1, 2)}
            self.swap[3] = cp("z", 3, 3, rows(2 * side, 2), dpeer(1))

        def start(self):
            go(self.direct[1])
            go(self.direct[2])

        def forward(self):
            self.direct[2].wait_recv()
            go(self.cross[0])
            self.direct[1].wait_recv()
            go(self.cross[1])
            go(self.swap[1])
            go(self.swap[2])

        def forward_far(self):
            for cp in self.cross:
                cp.wait_recv()
            go(self.swap[3])

        def finish(self, i):
            self.swap[i].wait_recv()

    g_in, g_out, g_up, g_down = (
        Gather(n, W) for n, W in (("in", Win), ("out", Wout), ("up", Wup), ("down", Wdown)))
    cp_tok = go(copy("tok", XT.at[c], XT.at[c], sib))
    g_in.start()
    g_out.start()
    CS, Cin = S["CS"], S["Cin"]

    loads["vec"].wait()
    loads["freq"].wait()
    vec = S["v_vec"]
    gain_a = vec[0:1, :]
    gain_f = vec[1:2, :]
    row_i = lax.broadcasted_iota(jnp.int32, (T, T), 0)
    col_i = lax.broadcasted_iota(jnp.int32, (T, T), 1)
    gap = row_i ^ col_i
    lower = row_i > col_i
    upper = row_i < col_i
    LV, MK, MT, TRI = S["LV"], S["MK"], S["MT"], S["TRI"]
    code = jnp.where(row_i == col_i, 0.0, -1.0)
    MK[0] = jnp.where(row_i == col_i, 1.0, 0.0).astype(BF16)
    MT[0] = jnp.where(row_i == col_i, 1.0, 0.0).astype(BF16)
    for lv in range(nlev):
        h = 1 << lv
        here = (gap >= h) & (gap < 2 * h)
        code = jnp.where(lower & here, float(lv + 1), code)
        MK[lv + 1] = jnp.where(lower & here, 1.0, 0.0).astype(BF16)
        MT[lv + 1] = jnp.where(upper & here, 1.0, 0.0).astype(BF16)
        bit = (row_i & h) != 0
        same = gap < h
        take = same & ((bit & (col_i >= row_i)) | ((~bit) & (col_i < row_i)))
        TRI[:, lv * T:(lv + 1) * T] = jnp.where(take, 1.0, 0.0).astype(BF16)
    TRI[:, nlev * T:(nlev + 1) * T] = jnp.where(col_i >= row_i, 1.0, 0.0).astype(BF16)
    LV[...] = code
    VEC = S["VEC"]
    VEC[...] = jnp.zeros_like(VEC)
    WBH, WBL = S["WBH"], S["WBL"]
    WBH[...] = jnp.zeros_like(WBH)
    WBL[...] = jnp.zeros_like(WBL)
    for i in range(nq):
        freq = S["v_freq"][2 * xor(q, i) + c]
        high = freq.astype(BF16)
        rest = (freq - high.astype(F32)).astype(BF16)
        WBH[i, 0:64, 0:128] = high
        WBH[i, 64:128, 128:256] = high
        WBL[i, 0:64, 0:128] = rest
        WBL[i, 64:128, 128:256] = rest
    SZ = S["SZ"]
    SZ[...] = jnp.zeros_like(SZ)

    NA = S["NA"]
    cp_tok.wait_recv()
    for s in range(2):
        x = XT[s].astype(F32)
        NA[s * T:(s + 1) * T, :] = (x * rms_scale(x) * gain_a).astype(BF16)

    PH, TV = S["PH"], S["TV"]
    lane_row = lax.broadcasted_iota(jnp.int32, (1, 128), 1)
    cp_car = [None]
    for i in range(nq):
        if i == 1:
            g_in.forward()
            g_out.forward()
            for k in range(1, nq):
                cp_car.append(go(copy(
                    ("car", k), CS.at[pl.ds(2 * xor(q, k), 2)], Cin.at[k], peer(k))))
            g_up.start()
        if i == 2:
            g_in.forward_far()
            g_out.forward_far()
        if i > 0:
            g_in.finish(i)
        bias = vec[2:3, pl.ds(pl.multiple_of(xor(q, i) * 128, 128), 128)]
        bias = jnp.where(c == 0, pltpu.roll(bias, 64, 1), bias)
        bias = jnp.where(lane_row >= 64, bias, 0.0)

        def head(s, _, i=i, bias=bias):
            rows = pl.ds(pl.multiple_of(s * T, T), T)
            pr = mm(NA[rows, :], Win[i])
            t0, t1 = halves(pr)
            TV[i, rows, :] = t1 + bias
            high = t0.astype(BF16)
            rest = (t0 - high.astype(F32)).astype(BF16)
            ang = mm(high, WBH[i]) + (mm(rest, WBH[i]) + mm(high, WBL[i]))
            sin, cos = sincos(ang)
            PH[i, rows, 0:128] = sin[:, :128].astype(BF16)
            PH[i, rows, 128:256] = cos[:, :128].astype(BF16)
            PH[i, rows, 256:384] = sin[:, 128:].astype(BF16)
            PH[i, rows, 384:512] = cos[:, 128:].astype(BF16)
            return 0

        lax.fori_loop(0, 2, head, 0)
        if i == nq - 1:
            g_down.start()
        if i == 0:
            loads["carried"].wait()
            CS[...] = S["v_car"][:, 0].astype(BF16)
            Cin[0] = CS[pl.ds(2 * q, 2)]
            loads["cot"].wait()
            cp_cot = go(copy("cot", XC.at[own_rows], XC.at[own_rows], sib))
            loads["w_up"].wait()
            Wup[0] = S["v_up"][...].astype(BF16)
            loads["w_down"].wait()
            Wdown[0] = S["v_down"][...].astype(BF16)

    lane = lax.broadcasted_iota(jnp.int32, (T, 128), 1)
    first = lane < 64
    row = lax.broadcasted_iota(jnp.int32, (T, 128), 0)
    lane_b = lax.broadcasted_iota(jnp.int32, (T, 256), 1)
    first_b = (lane_b % 128) < 64
    inv_feat = 1.0 / 128.0
    inv_root = 128.0 ** (-0.5)

    def swap(a, h):
        if h < 8:
            return jnp.where((row & h) != 0, pltpu.roll(a, h, 0), pltpu.roll(a, T - h, 0))
        parts = []
        for b in range(T // (2 * h)):
            parts.append(a[(2 * b + 1) * h:(2 * b + 2) * h])
            parts.append(a[2 * b * h:(2 * b + 1) * h])
        return jnp.concatenate(parts, axis=0)

    VV, KK, WW, PP, UU, YY = S["VV"], S["KK"], S["WW"], S["PP"], S["UU"], S["YY"]
    ND, NDL, MX = S["ND"], S["NDL"], S["MX"]
    FS = S["FS"]

    def split_rows(y):
        z = jnp.zeros_like(y)
        return jnp.concatenate([jnp.where(first_b, y, z), jnp.where(first_b, z, y)], axis=0)

    for j in range(npair):
        i0, i1 = 2 * j, 2 * j + 1
        for i in (i0, i1):
            if i > 0:
                cp_car[i].wait_recv()

        def forward(s, _, i0=i0, i1=i1, j=j):
            rows = pl.ds(pl.multiple_of(s * T, T), T)
            for k, i in enumerate((i0, i1)):
                SZ[j, s, k * 64:k * 64 + 64, k * 256:k * 256 + 256] = Cin[i, s, 0]
                SZ[j, s, 128 + k * 64:192 + k * 64, k * 256:k * 256 + 256] = Cin[i, s, 1]
            ta, tb = TV[i0, rows, :], TV[i1, rows, :]
            value = jnp.where(first, ta, pltpu.roll(tb, 64, 1))
            gate = jnp.where(first, pltpu.roll(ta, 64, 1), tb)
            small = jnp.exp(-jnp.abs(gate))
            big = 1.0 / (1.0 + small)
            rest = small * big
            keep = jnp.where(gate >= 0, big, rest)
            write = jnp.where(gate >= 0, rest, big)
            written = write * value
            VV[j, rows, :] = value
            KK[j, rows, :] = keep
            WW[j, rows, :] = write
            scores = [
                (mm_nt(PH[i, rows, 0:256], PH[i, rows, 256:512]) * inv_feat).astype(BF16)
                for i in (i0, i1)]
            total, pre, suf = keep, keep, jnp.ones_like(keep)
            y = jnp.concatenate([written, write], axis=1).astype(BF16)
            left = jnp.concatenate([sc * MK[0] for sc in scores], axis=1)
            acc = mm(left, split_rows(y))
            for lv in range(nlev):
                h = 1 << lv
                if lv > 0:
                    y = jnp.concatenate([suf * written, suf * write], axis=1).astype(BF16)
                YY[j, s, lv] = y
                PP[j, s, lv] = pre.astype(BF16)
                UU[j, s, lv] = suf.astype(BF16)
                left = jnp.concatenate([sc * MK[lv + 1] for sc in scores], axis=1)
                nd = mm(left, split_rows(y)) * pair_cat(pre)
                acc = acc + nd
                NDL[j, s, lv] = nd.astype(BF16)
                other = swap(total, h)
                upper_half = (row & h) != 0
                pre = jnp.where(upper_half, pre * other, pre)
                suf = jnp.where(upper_half, suf, suf * other)
                total = total * other
            PP[j, s, nlev] = pre.astype(BF16)
            phq = jnp.concatenate([PH[i, rows, 0:256] for i in (i0, i1)], axis=1)
            phk = jnp.concatenate([PH[i, rows, 256:512] for i in (i0, i1)], axis=1)
            nd = mm_nt(phq, SZ[j, s]) * (pair_cat(pre) * inv_root)
            NDL[j, s, nlev] = nd.astype(BF16)
            acc = acc + nd
            ND[j, s] = acc
            num, den = halves(acc)
            MX[rows, j * 128:(j + 1) * 128] = (
                num * lax.rsqrt(den * den + DEN_FLOOR)).astype(BF16)
            y = jnp.concatenate([suf * written, suf * write], axis=1).astype(BF16)
            new = mm_tn(y, phk) * inv_root
            last = jnp.transpose(pre[T - 128:, :], (1, 0))[:, 127:128]
            for k, i in enumerate((i0, i1)):
                kept = last[k * 64:k * 64 + 64, :]
                for z in range(2):
                    block = new[z * 128 + k * 64:z * 128 + k * 64 + 64, k * 256:k * 256 + 256]
                    FS[i, s, z] = (kept * Cin[i, s, z].astype(F32) + block).astype(BF16)
            return 0

        lax.fori_loop(0, 2, forward, 0)

    AP, AQ, MID, NF = S["AP"], S["AQ"], S["MID"], S["NF"]
    g_up.forward()
    for i in range(1, nq):
        g_out.finish(i)
    wout = jnp.concatenate([Wout[i] for i in range(nq)], axis=0)
    AP[...] = mm(MX[...], wout)
    cp_att = go(copy("att", AP, AQ, sib))
    g_down.forward()
    cp_att.wait_recv()
    for s in range(2):
        rows = slice(s * T, (s + 1) * T)
        middle = XT[s].astype(F32) + (AP[rows, :] + AQ[rows, :])
        MID[rows, :] = middle
        NF[rows, :] = (middle * rms_scale(middle) * gain_f).astype(BF16)

    FO, DN = AP, S["DN"]
    cp_att.wait_send()
    cp_cot.wait_recv()
    NFT, CT = S["NFT"], XC
    NFT[...] = jnp.transpose(NF[...], (1, 0))

    class Scatter:
        def __init__(self, name):
            self.name = name
            self.own, self.out, self.mid, self.got = (S[name + k] for k in "ospr")
            self.half = self.own.shape[0] // 2
            self.top, self.bottom = pl.ds(0, self.half), pl.ds(self.half, self.half)

        def send(self, key, src, dst, i):
            cp = go(copy((self.name, key), src, dst, peer(i)))
            setattr(self, key, cp)

        def put(self, i, value):
            if i == 0:
                self.own[...] = value
                return
            out = self.out
            out[i - 1] = value.astype(BF16)
            if i == 1:
                self.send("a1", out.at[0].at[self.top], self.got.at[0].at[self.top], 1)
            elif i == 2:
                self.send("a2", out.at[1].at[self.bottom], self.got.at[1].at[self.bottom], 2)
            else:
                self.send("p1", out.at[2].at[self.top], self.mid.at[0], 1)
                self.send("p2", out.at[2].at[self.bottom], self.mid.at[1], 2)

        def middle(self):
            out, half = self.out, self.half
            self.p1.wait_recv()
            out[1, :half] = (out[1, :half].astype(F32) + self.mid[0].astype(F32)).astype(BF16)
            self.send("b2", out.at[1].at[self.top], self.got.at[1].at[self.top], 2)
            self.p2.wait_recv()
            out[0, half:] = (out[0, half:].astype(F32) + self.mid[1].astype(F32)).astype(BF16)
            self.send("b1", out.at[0].at[self.bottom], self.got.at[0].at[self.bottom], 1)

        def total(self):
            for cp in (self.a1, self.a2, self.b1, self.b2):
                cp.wait_recv()
            return self.own[...] + (self.got[0].astype(F32) + self.got[1].astype(F32))

    sc_up, sc_down, sc_in, sc_out = (Scatter(n) for n in ("gu", "gd", "gi", "go"))
    for i in range(nq):
        if i == 1:
            g_up.forward_far()
            g_down.forward_far()
        if i > 0:
            g_up.finish(i)
            g_down.finish(i)
        up, down = Wup[i], Wdown[i]
        pre = mm(NF[...], up)
        square = pre * pre
        th = jnp.tanh(0.7978845608028654 * (pre + 0.044715 * pre * square))
        hidden = (0.5 * pre * (1.0 + th)).astype(BF16)
        slope = 0.5 * (1.0 + th) + 0.5 * pre * (1.0 - th * th) * (
            0.7978845608028654 * (1.0 + 0.134145 * square))
        d_pre = (mm_nt(CT[...], down) * slope).astype(BF16)
        fo = mm(hidden, down)
        dn = mm_nt(d_pre, up)
        if i == 0:
            FO[...] = fo
            DN[...] = dn
        else:
            FO[...] += fo
            DN[...] += dn
        sc_down.put(i, mm_tn(hidden, CT[...]))
        sc_up.put(i, mm(NFT[...], d_pre))
    FOR, DNR = S["FOR"], S["DNR"]
    cp_dn = go(copy("dn", DN, DNR, sib))
    cp_fo = go(copy("fo", FO.at[pl.ds((1 - c) * T, T)], FOR, sib))
    cp_dn.wait_recv()
    DA, DM, DMI = S["DA"], S["DM"], S["DMI"]
    for s in range(2):
        rows = slice(s * T, (s + 1) * T)
        middle = MID[rows, :]
        scale = rms_scale(middle)
        unit = middle * scale
        grad = DN[rows, :] + DNR[rows, :]
        d_mid = XC[rows, :].astype(F32) + norm_back(grad, unit, scale, gain_f)
        DA[rows, :] = d_mid.astype(BF16)
        gain_grad = jnp.sum(grad * unit, axis=0, keepdims=True)

        @pl.when(c == s)
        def _(gain_grad=gain_grad, d_mid=d_mid):
            DMI[...] = d_mid
            for t in range(D // 128):
                VEC[D // 128 + t:D // 128 + t + 1, :] = gain_grad[:, t * 128:(t + 1) * 128]

    cp_fo.wait_recv()
    S["BO"][...] = (MID[own_rows, :] + (FO[own_rows, :] + FOR[...])).astype(BF16)
    put(S["BO"], S["block_out"])
    DM[...] = mm_nt(DA[...], wout)
    go_all = mm_tn(MX[...], DA[...])
    for i in range(nq):
        sc_out.put(i, go_all[64 * i:64 * i + 64])

    XL, DPJ, CG = S["XL"], S["DPJ"], S["CG"]
    ZD, ZU, ZI = S["ZD"], S["ZU"], S["ZI"]
    NS = S["NS"]
    LT = D // 128

    def fold(z):
        return jnp.sum((z * z).reshape(z.shape[0] // 8, 8, 128), axis=0)

    def tiles_of(a):
        return [a[:, t * 128:(t + 1) * 128].astype(BF16) for t in range(a.shape[1] // 128)]

    def lay(Z, parts):
        at = 0
        for part in parts:
            Z[at:at + part.shape[0], :] = part
            at += part.shape[0]

    def reduce_dp(name, Z, R, out):
        piece = Z.shape[0] // ndp
        mine = pl.ds(pl.multiple_of(me_dp * piece, 16), piece)
        scatter = [copy((name, "rs", k), Z.at[pl.ds(xor(me_dp, k) * piece, piece)], R.at[k - 1],
                        dpeer(k)) for k in range(1, ndp)]
        spread = [copy((name, "ag", k), out.at[mine], out.at[mine], dpeer(k))
                  for k in range(1, ndp)]

        def start():
            for cp in scatter:
                go(cp)

        def middle():
            for cp in scatter:
                cp.wait_recv()
            total = tree_sum([Z[mine, :].astype(F32)] + [R[k].astype(F32) for k in range(ndp - 1)])
            total = total.astype(BF16)
            out[mine, :] = total
            for cp in spread:
                go(cp)
            return fold(total.astype(F32))

        def finish():
            for cp in spread:
                cp.wait_recv()
        return start, middle, finish

    nbit = ndp.bit_length() - 1

    class Halving:
        def __init__(self, name, Z, R, out):
            self.Z, self.R, self.out = Z, R, out
            size, first, at = Z.shape[0], 0, 0
            self.rs, self.ag, self.keep, self.land = [], [], [], []
            for b in range(nbit):
                bit = lax.div(me_dp, 1 << b) % 2
                size //= 2
                keep, give = first + bit * size, first + (1 - bit) * size
                land = R.at[pl.ds(at, size)]
                self.keep.append(pl.ds(pl.multiple_of(keep, 16), size))
                self.land.append(pl.ds(at, size))
                self.rs.append(copy((name, "rs", b), Z.at[pl.ds(give, size)], land, dpeer(1 << b)))
                seg = pl.ds(pl.multiple_of(keep, 16), size)
                self.ag.append(copy((name, "ag", b), out.at[seg], out.at[seg], dpeer(1 << b)))
                first, at = keep, at + size
            self.at = 0
            self.square = None

        def start(self):
            go(self.rs[0])

        def step(self):
            for _ in range(max(nbit // 2, 1)):
                k = self.at
                self.at += 1
                if k < nbit:
                    self.rs[k].wait_recv()
                    rows = self.keep[k]
                    total = self.Z[rows, :].astype(F32) + self.R[self.land[k], :].astype(F32)
                    total = total.astype(BF16)
                    if k + 1 < nbit:
                        self.Z[rows, :] = total
                        go(self.rs[k + 1])
                    else:
                        self.out[rows, :] = total
                        go(self.ag[k])
                        self.square = fold(total.astype(F32))
                else:
                    b = 2 * nbit - 1 - k
                    self.ag[b].wait_recv()
                    if b > 0:
                        go(self.ag[b - 1])

    zd = Halving("zd", ZD, S["ZDR"], S["ZDO"])
    zu = Halving("zu", ZU, S["ZUR"], S["ZUO"])
    zi = Halving("zi", ZI, S["ZIR"], S["ZIO"])

    def hook_0():
        sc_down.middle()
        sc_up.middle()
        sc_out.middle()

    def hook_1():
        lay(ZD, tiles_of(sc_down.total()))
        zd.start()

    def hook_2():
        zd.step()
        lay(ZU, tiles_of(sc_up.total()) + tiles_of(sc_out.total()))
        zu.start()

    NAT = NFT
    NAT[...] = jnp.transpose(NA[...], (1, 0))
    for j in (1, 0):
        i0, i1 = 2 * j, 2 * j + 1

        bias_sum = jnp.zeros((1, 128), F32)
        for s in range(2):
            rows = pl.ds(s * T, T)
            if s == 1:
                if j == 1:
                    hook_0()
                else:
                    hook_2()
            dm = DM[rows, j * 128:(j + 1) * 128]
            num, den = halves(ND[j, s])
            r = lax.rsqrt(den * den + DEN_FLOOR)
            d_num = dm * r
            d_den = -(d_num * num) * den * (r * r)
            g = jnp.concatenate([d_num, d_den], axis=1)
            value, keep, write = VV[j, rows, :], KK[j, rows, :], WW[j, rows, :]
            written = write * value
            scores = [
                (mm_nt(PH[i, rows, 256:512], PH[i, rows, 0:256]) * inv_feat).astype(BF16)
                for i in (i0, i1)]
            levels = LV[...]
            z16 = jnp.zeros((T, 256), BF16)
            gb = g.astype(BF16)
            g0, g1 = jnp.where(first_b, gb, z16), jnp.where(first_b, z16, gb)
            left = jnp.concatenate([sc * MT[0] for sc in scores], axis=1)
            ab = mm(left, jnp.concatenate([g0, g1], axis=0))
            y = YY[j, s, 0]
            ds0 = mm_nt(g0, y)
            ds1 = mm_nt(g1, y)
            for lv in range(nlev):
                h = 1 << lv
                pg = (pair_cat(PP[j, s, lv].astype(F32)) * g).astype(BF16)
                g0, g1 = jnp.where(first_b, pg, z16), jnp.where(first_b, z16, pg)
                left = jnp.concatenate([sc * MT[lv + 1] for sc in scores], axis=1)
                part = mm(left, jnp.concatenate([g0, g1], axis=0)) * pair_cat(UU[j, s, lv].astype(F32))
                ab = ab + part
                pa, pb = halves(part)
                from_key = written * pa + write * pb
                oa, ob = halves(g * NDL[j, s, lv].astype(F32))
                XL[lv * T:(lv + 1) * T, :] = jnp.where(
                    (row & h) != 0, oa + ob, from_key).astype(BF16)
                y = YY[j, s, lv]
                hit = levels == float(lv + 1)
                ds0 = jnp.where(hit, mm_nt(g0, y), ds0)
                ds1 = jnp.where(hit, mm_nt(g1, y), ds1)
            causal = levels >= 0.0
            ds0 = jnp.where(causal, ds0, 0.0).astype(BF16)
            ds1 = jnp.where(causal, ds1, 0.0).astype(BF16)
            oa, ob = halves(g * NDL[j, s, nlev].astype(F32))
            XL[nlev * T:, :] = (oa + ob).astype(BF16)
            pg = (pair_cat(PP[j, s, nlev].astype(F32)) * g).astype(BF16)
            phq = jnp.concatenate([PH[i, rows, 0:256] for i in (i0, i1)], axis=1)
            opening = mm(pg, SZ[j, s]) * inv_root
            cg = mm_tn(pg, phq) * inv_root
            for k, i in enumerate((i0, i1)):
                for z in range(2):
                    CG[i, s, z] = cg[z * 128 + k * 64:z * 128 + k * 64 + 64,
                                     k * 256:k * 256 + 256].astype(BF16)
            d_log = mm(TRI[...], XL[...])
            a, b = halves(ab)
            d_value = write * a
            d_write = value * a + b
            d_gate = write * (d_log - keep * d_write)
            tiles = (jnp.where(first, d_value, pltpu.roll(d_gate, 64, 1)),
                     jnp.where(first, pltpu.roll(d_value, 64, 1), d_gate))
            for k, (i, ds) in enumerate(((i0, ds0), (i1, ds1))):
                pq, pk = PH[i, rows, 0:256], PH[i, rows, 256:512]
                dq = mm(ds, pk) * inv_feat + opening[:, k * 256:k * 256 + 256]
                dk = mm_tn(ds, pq) * inv_feat
                pq, pk = pq.astype(F32), pk.astype(F32)
                aq = pq[:, 128:] * dq[:, :128] - pq[:, :128] * dq[:, 128:]
                ak = pk[:, 128:] * dk[:, :128] - pk[:, :128] * dk[:, 128:]
                d_ang = jnp.concatenate([aq, ak], axis=1).astype(BF16)
                DPJ[i, rows, 0:128] = mm_nt(d_ang, WBH[i]).astype(BF16)
                DPJ[i, rows, 128:256] = tiles[k].astype(BF16)
            bias_sum = bias_sum + jnp.sum(d_gate, axis=0, keepdims=True)

        for k, i in enumerate((i0, i1)):
            VEC[pl.ds(2 * D // 128 + 2 * xor(q, i) + c, 1), :] = (
                bias_sum if k else pltpu.roll(bias_sum, 64, 1))

        for i in (i1, i0):
            sc_in.put(i, mm(NAT[...], DPJ[i]))
        if j == 1:
            hook_1()

    sc_in.middle()
    zd.step()
    zu.step()
    CR, FR = S["CR"], S["FR"]
    DX = FO
    cp_fo.wait_send()
    DX[...] = mm_nt(DPJ[0], Win[0])
    for i in range(1, nq):
        DX[...] += mm_nt(DPJ[i], Win[i])
    DXR = S["DXR"]
    cp_dx = go(copy("dx", DX.at[pl.ds((1 - c) * T, T)], DXR, sib))
    lay(ZI, tiles_of(sc_in.total()))
    zi.start()
    cp_cg = [None] + [
        go(copy(("cg", i), CG.at[i], CR.at[pl.ds(2 * q, 2)], peer(i))) for i in range(1, nq)]
    cp_fin = [None] + [
        go(copy(("fin", i), FS.at[i], FR.at[pl.ds(2 * q, 2)], peer(i))) for i in range(1, nq)]
    CR[pl.ds(2 * q, 2)] = CG[0]
    FR[pl.ds(2 * q, 2)] = FS[0]
    zd.step()
    zu.step()
    cp_dx.wait_recv()
    zi.step()
    x = XT[c].astype(F32)
    scale = rms_scale(x)
    unit = x * scale
    grad = DX[own_rows, :] + DXR[...]
    S["TG"][...] = DMI[...] + norm_back(grad, unit, scale, gain_a)
    put(S["TG"], S["token_grad"])
    gain_grad = jnp.sum(grad * unit, axis=0, keepdims=True)
    for t in range(LT):
        VEC[t:t + 1, :] = gain_grad[:, t * 128:(t + 1) * 128]
    VR = S["VR"]
    VS = S["VS"]
    cp_v = go(copy("v0", VEC, VR.at[0], sib))

    zu.step()
    zi.step()
    NS[0] = zd.square + zu.square + zi.square
    NR = S["NR"]
    cp_n = [go(copy(("n", r), NS.at[0], NR.at[r - 1], {"mp": xor(m, r)})) for r in range(1, 2 * nq)]
    cp_v.wait_recv()
    VS[0] = VEC[...] + VR[0]
    cp_vs = [go(copy(("v1", i), VS.at[0], VR.at[i], peer(i))) for i in range(1, nq)]

    def put_tiles(Z, first, name, n, count):
        for t in range(count):
            put(Z.at[pl.ds(first + t * n, n)], S[name].at[:, pl.ds(t * 128, 128)])

    zi.step()
    zd.step()
    put_tiles(S["ZDO"], 0, "g_down", FH, LT)
    for cp in cp_n:
        cp.wait_recv()
    NS[1] = tree_sum([NS[0]] + [NR[r] for r in range(2 * nq - 1)])
    cp_m = [go(copy(("m", k), NS.at[1], NR.at[2 * nq - 2 + k], dpeer(k))) for k in range(1, ndp)]
    for cp in cp_vs:
        cp.wait_recv()
    VS[1] = tree_sum([VS[0]] + [VR[i] for i in range(1, nq)])
    cp_vd = [go(copy(("v2", k), VS.at[1], VR.at[nq - 1 + k], dpeer(k))) for k in range(1, ndp)]
    zu.step()
    put_tiles(S["ZUO"], 0, "g_up", D, FH // 128)
    put_tiles(S["ZUO"], D * FH // 128, "g_out", 64, LT)

    for i in range(1, nq):
        cp_cg[i].wait_recv()
    put(CR, S["cgrad"])
    for i in range(1, nq):
        cp_fin[i].wait_recv()
    put(FR, S["fin"])
    for cp in cp_vd:
        cp.wait_recv()
    vtot = tree_sum([VS[1]] + [VR[nq - 1 + k] for k in range(1, ndp)])
    g_vec = S["g_vec"]
    for t in range(LT):
        part = slice(t * 128, (t + 1) * 128)
        g_vec[0:1, part] = vtot[t:t + 1, :]
        g_vec[1:2, part] = vtot[LT + t:LT + t + 1, :]
        even = vtot[2 * LT + 2 * t:2 * LT + 2 * t + 1, :]
        odd = vtot[2 * LT + 2 * t + 1:2 * LT + 2 * t + 2, :]
        g_vec[2:3, part] = jnp.where(lane_row < 64, pltpu.roll(even, 64, 1), odd)
    lane_v = lax.broadcasted_iota(jnp.int32, VEC.shape, 1)
    row_v = lax.broadcasted_iota(jnp.int32, VEC.shape, 0)
    vmask = (row_v < 2 * LT) | (lane_v >= 64)
    vsq = fold(jnp.where(vmask, vtot, 0.0))
    for cp in cp_m:
        cp.wait_recv()
    S["sq"][...] = tree_sum([NS[1]] + [NR[2 * nq - 2 + k] for k in range(1, ndp)]) + vsq
    zi.step()
    put_tiles(S["ZIO"], 0, "g_in", D, 2)
    for cp in puts:
        cp.wait()
    for cp in sends:
        if cp is not cp_fo and cp is not cp_att:
            cp.wait_send()


def layer_call(ndp, nmp, args, shapes):
    T, D = shapes["tok"].shape
    nq = nmp // 2
    FH = shapes["w_up"].shape[1]
    nlev = (T - 1).bit_length()
    npair = nq // 2
    nseq = 2 * nq
    lt = D // 128
    zd = D * FH // 128
    zu = (D * FH + 64 * D) // 128
    zi = D * 256 // 128
    vrows = 2 * lt + nseq
    R = nq - 1
    V = pltpu.VMEM
    scratch = dict(
        XT=V((2, T, D), BF16), XC=V((2 * T, D), BF16),
        Win=V((nq, D, 256), BF16), Wout=V((nq, 64, D), BF16),
        Wup=V((nq, D, FH), BF16), Wdown=V((nq, FH, D), BF16),
        CS=V((nseq, 2, 64, 256), BF16), Cin=V((nq, 2, 2, 64, 256), BF16),
        LV=V((T, T), F32), MK=V((nlev + 1, T, T), BF16), MT=V((nlev + 1, T, T), BF16),
        TRI=V((T, (nlev + 1) * T), BF16), VEC=V((vrows, 128), F32),
        WBH=V((nq, 128, 256), BF16), WBL=V((nq, 128, 256), BF16),
        SZ=V((npair, 2, 256, 512), BF16), NA=V((2 * T, D), BF16),
        PH=V((nq, 2 * T, 512), BF16), TV=V((nq, 2 * T, 128), F32),
        VV=V((npair, 2 * T, 128), F32), KK=V((npair, 2 * T, 128), F32),
        WW=V((npair, 2 * T, 128), F32), PP=V((npair, 2, nlev + 1, T, 128), BF16),
        UU=V((npair, 2, nlev, T, 128), BF16), YY=V((npair, 2, nlev, T, 256), BF16),
        ND=V((npair, 2, T, 256), F32), NDL=V((npair, 2, nlev + 1, T, 256), BF16),
        MX=V((2 * T, 64 * nq), BF16), FS=V((nq, 2, 2, 64, 256), BF16),
        FR=V((nseq, 2, 64, 256), BF16), AP=V((2 * T, D), F32), AQ=V((2 * T, D), F32),
        MID=V((2 * T, D), F32), NF=V((2 * T, D), BF16),
        DN=V((2 * T, D), F32), NFT=V((D, 2 * T), BF16),
        guo=V((D, FH), F32), gus=V((R, D, FH), BF16),
        gup=V((2, D // 2, FH), BF16), gur=V((2, D, FH), BF16),
        gdo=V((FH, D), F32), gds=V((R, FH, D), BF16),
        gdp=V((2, FH // 2, D), BF16), gdr=V((2, FH, D), BF16),
        gio=V((D, 256), F32), gis=V((R, D, 256), BF16),
        gip=V((2, D // 2, 256), BF16), gir=V((2, D, 256), BF16),
        goo=V((64, D), F32), gos=V((R, 64, D), BF16),
        gop=V((2, 32, D), BF16), gor=V((2, 64, D), BF16),
        FOR=V((T, D), F32), DNR=V((2 * T, D), F32),
        DA=V((2 * T, D), BF16), DM=V((2 * T, 64 * nq), F32), DMI=V((T, D), F32),
        XL=V(((nlev + 1) * T, 128), BF16), DPJ=V((nq, 2 * T, 256), BF16),
        CG=V((nq, 2, 2, 64, 256), BF16), CR=V((nseq, 2, 64, 256), BF16),
        BO=V((T, D), BF16), TG=V((T, D), F32), DXR=V((T, D), F32), ZD=V((zd, 128), BF16), ZU=V((zu, 128), BF16),
        ZI=V((zi, 128), BF16),
        ZDR=V((zd, 128), BF16), ZUR=V((zu, 128), BF16),
        ZIR=V((zi, 128), BF16),
        ZDO=V((zd, 128), BF16), ZUO=V((zu, 128), BF16), ZIO=V((zi, 128), BF16),
        VR=V((nq + ndp, vrows, 128), F32), VS=V((2, vrows, 128), F32),
        NR=V((2 * nq - 2 + ndp, 8, 128), F32), NS=V((2, 8, 128), F32),
        v_in=V((2 * D, 128), F32), v_vec=V((3, D), F32), v_freq=V(shapes["freq"].shape, F32),
        v_out=V((64, D), F32), v_car=V(shapes["carried"].shape, F32),
        v_up=V((D, FH), F32), v_down=V((FH, D), F32),
    )
    nsem = 80 + 3 * R + 9 * ndp + 2 * nq
    scratch["osem"] = pltpu.SemaphoreType.DMA((16 + 2 * lt,))
    scratch["lsem"] = pltpu.SemaphoreType.DMA((len(args),))
    scratch["ssem"] = pltpu.SemaphoreType.DMA((nsem,))
    scratch["rsem"] = pltpu.SemaphoreType.DMA((nsem,))
    outs = dict(
        block_out=((T, D), BF16), token_grad=((T, D), F32),
        fin=((nseq, 2, 64, 256), BF16), cgrad=((nseq, 2, 64, 256), BF16),
        g_in=((D, 256), BF16), g_out=((64, D), BF16),
        g_up=((D, FH), BF16), g_down=((FH, D), BF16),
        g_vec=((3, D), F32), sq=((8, 128), F32))
    names = list(args) + list(outs) + list(scratch)
    cfg = dict(names=names, ndp=ndp, nq=nq, T=T, D=D, nlev=nlev, FH=FH)
    vm = pl.BlockSpec(memory_space=pltpu.VMEM)
    res = pl.pallas_call(
        functools.partial(layer_kernel, cfg),
        out_shape=[jax.ShapeDtypeStruct(s, d) for s, d in outs.values()],
        in_specs=[pl.BlockSpec(memory_space=pl.ANY)] * len(args),
        out_specs=[vm if n in ("g_vec", "sq") else pl.BlockSpec(memory_space=pl.ANY) for n in outs],
        scratch_shapes=list(scratch.values()),
        compiler_params=pltpu.CompilerParams(
            collective_id=0, has_side_effects=True, vmem_limit_bytes=62 * 2**20),
        name="layer",
    )(*args.values())
    return dict(zip(outs, res))


def adam(w, g, first, second, rate, decay):
    first_new = B1 * first + (1.0 - B1) * g
    second_new = B2 * second + (1.0 - B2) * g * g
    first_hat = first_new / (1.0 - B1**STEP)
    second_hat = second_new / (1.0 - B2**STEP)
    w_new = w - rate * (first_hat / (jnp.sqrt(second_hat) + ADAM_EPS) + decay * w)
    return first_new, second_new, w_new


def adam_kernel(names, nout, *refs):
    S = dict(zip(names, refs))
    norm = jnp.sqrt(jnp.sum(S["sq"][...]))
    factor = CLIP / jnp.maximum(norm, CLIP)

    def matrix(key):
        g = S["g_" + key][...].astype(F32) * factor
        res = adam(S[key + "0"][...], g, S[key + "1"][...], S[key + "2"][...], RATE_MATRIX, DECAY)
        for k in range(3):
            S["n%s%d" % (key, k)][...] = res[k]
        S["n%s3" % key][...] = res[2].astype(BF16)

    @pl.when(pl.program_id(0) == 0)
    def _():
        S["norm"][0, 0] = norm
        g = S["g_v"][...] * factor
        res = adam(S["v0"][...], g, S["v1"][...], S["v2"][...], RATE_VECTOR, 0.0)
        for k in range(3):
            S["nv%d" % k][...] = res[k]
        matrix("o")

    for key in "ud":
        matrix(key)
    count = S["i0"].shape[0] // 2
    for t in range(2):
        rows = pl.ds(t, count, 2)
        lanes = slice(t * 128, (t + 1) * 128)
        g = S["g_i"][:, lanes].astype(F32) * factor
        res = adam(S["i0"][rows, :], g, S["i1"][rows, :], S["i2"][rows, :], RATE_MATRIX, DECAY)
        for k in range(3):
            S["ni%d" % k][rows, :] = res[k]
        S["ni3"][:, lanes] = res[2].astype(BF16)
    S["n_block_out"][...] = S["block_out"][...]
    S["n_token_grad"][...] = S["token_grad"][...]
    S["n_fin"][...] = S["fin"][...].astype(F32)
    S["n_cgrad"][...] = S["cgrad"][...].astype(F32)


def adam_call(res, params):
    steps = 2

    def cut(shape):
        block = (shape[0] // steps,) + tuple(shape[1:])
        return pl.BlockSpec(block, lambda g: (g,) + (0,) * (len(shape) - 1))

    def whole(shape):
        return pl.BlockSpec(tuple(shape), lambda g: (0,) * len(shape))

    ins, in_specs, outs, out_specs, names, onames = [], [], [], [], [], []

    def take(name, a, spec):
        names.append(name)
        ins.append(a)
        in_specs.append(spec(a.shape))

    def give(name, shape, dtype, spec):
        onames.append(name)
        outs.append(jax.ShapeDtypeStruct(shape, dtype))
        out_specs.append(spec(shape))

    take("sq", res["sq"], whole)
    for key, full in zip("vioud", ("g_vec", "g_in", "g_out", "g_up", "g_down")):
        spec = whole if key in "vo" else cut
        take("g_" + key, res[full], spec)
        for k, a in enumerate(params[key]):
            take("%s%d" % (key, k), a, spec)
            give("n%s%d" % (key, k), a.shape, F32, spec)
        if key != "v":
            give("n%s3" % key, res[full].shape, BF16, spec)
    for name in ("block_out", "token_grad", "fin", "cgrad"):
        a = res[name]
        take(name, a, cut)
        give("n_" + name, a.shape, F32 if name in ("fin", "cgrad") else a.dtype, cut)
    onames.append("norm")
    outs.append(jax.ShapeDtypeStruct((1, 1), F32))
    out_specs.append(pl.BlockSpec(memory_space=pltpu.SMEM))
    got = pl.pallas_call(
        functools.partial(adam_kernel, names + onames, len(onames)),
        grid=(steps,), out_shape=outs, in_specs=in_specs, out_specs=out_specs,
        compiler_params=pltpu.CompilerParams(vmem_limit_bytes=int(63.9 * 2**20)),
        name="adam",
    )(*ins)
    got = dict(zip(onames, got))
    new = {key: tuple(got["n%s%d" % (key, k)] for k in range(3 if key == "v" else 4))
           for key in "vioud"}
    for name in ("block_out", "token_grad", "fin", "cgrad"):
        new[name] = got["n_" + name]
    new["norm"] = got["norm"]
    return new


def shards(
    tokens, cotangent, carried, frequencies, vectors, vectors_first, vectors_second,
    mix_in, mix_in_first, mix_in_second, mix_out, mix_out_first, mix_out_second,
    ffn_up, ffn_up_first, ffn_up_second, ffn_down, ffn_down_first, ffn_down_second,
    *, ndp, nmp,
):
    D = tokens.shape[1]
    FH = ffn_up.shape[1]
    args = dict(
        tok=tokens, cot=cotangent, carried=carried,
        freq=jnp.swapaxes(frequencies, 1, 2), vec=vectors,
        w_in=mix_in.reshape(2 * D, 128), w_out=mix_out, w_up=ffn_up, w_down=ffn_down)
    res = layer_call(ndp, nmp, args, args)
    flat = (2 * D, 128)
    params = dict(
        v=(vectors, vectors_first, vectors_second),
        i=tuple(a.reshape(flat) for a in (mix_in, mix_in_first, mix_in_second)),
        o=(mix_out, mix_out_first, mix_out_second),
        u=(ffn_up, ffn_up_first, ffn_up_second),
        d=(ffn_down, ffn_down_first, ffn_down_second))
    new = adam_call(res, params)
    shape = mix_in.shape
    return (
        new["block_out"], new["fin"].reshape(carried.shape), new["token_grad"],
        new["cgrad"].reshape(carried.shape), new["norm"][0, 0],
        *new["v"], *(a.reshape(shape) for a in new["i"]), *new["o"], *new["u"], *new["d"])


def solution(mesh):
    tok = P(("dp", "mp"), None)
    car = P("dp", "mp", None, None, None)
    head = P(None, "mp", None)
    rowp = P("mp", None)
    colp = P(None, "mp")
    rep = P()
    in_specs = (tok, tok, car, rep, rep, rep, rep) + (head,) * 3 + (rowp,) * 3 + (
        colp,) * 3 + (rowp,) * 3
    out_specs = (tok, car, tok, car, rep, rep, rep, rep) + (head,) * 4 + (rowp,) * 4 + (
        colp,) * 4 + (rowp,) * 4
    body = functools.partial(shards, ndp=mesh.shape["dp"], nmp=mesh.shape["mp"])
    return jax.shard_map(body, mesh=mesh, in_specs=in_specs, out_specs=out_specs, check_vma=False)
```

```python
import functools

import jax
import jax.numpy as jnp
from jax import lax
from jax.experimental import pallas as pl
from jax.experimental.pallas import tpu as pltpu
from jax.sharding import PartitionSpec as P

STEP = 10
NORM_EPS = 1e-06
DEN_FLOOR = 0.25
CLIP = 1.0
B1 = 0.9
B2 = 0.999
ADAM_EPS = 1e-08
DECAY = 0.1
RATE_MATRIX = 0.05
RATE_VECTOR = 0.6
MESH = pl.DeviceIdType.MESH
F32 = jnp.float32
BF16 = jnp.bfloat16

SIN = (9.99999996e-01, -1.66666578e-01, 8.33304727e-03, -1.98087928e-04, 2.60457914e-06)
COS = (1.0, -4.99999993e-01, 4.16666357e-02, -1.38883546e-03, 2.47598090e-05, -2.60452002e-07)
PI_A, PI_B, PI_C = 3.140625, 0.0009675025939941406, 1.5099579897537296e-07


def mm(a, b):
    return jnp.dot(a, b, preferred_element_type=F32)


def mm_nt(a, b):
    return lax.dot_general(a, b, (((1,), (1,)), ((), ())), preferred_element_type=F32)


def mm_tn(a, b):
    return lax.dot_general(a, b, (((0,), (0,)), ((), ())), preferred_element_type=F32)


def horner(coefs, y):
    acc = jnp.full_like(y, coefs[-1])
    for coef in coefs[-2::-1]:
        acc = acc * y + coef
    return acc


def sincos(x):
    turns = jnp.floor(x * 0.3183098861837907 + 0.5)
    r = ((x - turns * PI_A) - turns * PI_B) - turns * PI_C
    sign = 1.0 - 2.0 * (turns - 2.0 * jnp.floor(turns * 0.5))
    y = r * r
    return sign * (r * horner(SIN, y)), sign * horner(COS, y)


def rms_scale(x):
    return lax.rsqrt(jnp.mean(x * x, axis=-1, keepdims=True) + NORM_EPS)


def norm_back(grad, unit, scale, gain):
    e = grad * gain
    return scale * (e - unit * jnp.mean(e * unit, axis=-1, keepdims=True))


def xor(a, bits):
    out = a
    step = 1
    while step <= bits:
        if bits & step:
            out = out + step - 2 * step * (lax.div(a, step) % 2)
        step *= 2
    return out


def tree_sum(terms):
    terms = list(terms)
    if len(terms) == 1:
        return terms[0]
    half = len(terms) // 2
    return tree_sum(terms[:half]) + tree_sum(terms[half:])


def halves(a):
    return a[:, :128], a[:, 128:]


def pair_cat(a):
    return jnp.concatenate([a, a], axis=1)


def layer_kernel(cfg, *refs):
    names = cfg["names"]
    S = dict(zip(names, refs))
    ndp, nq, T, D = cfg["ndp"], cfg["nq"], cfg["T"], cfg["D"]
    nlev = cfg["nlev"]
    FH = cfg["FH"]
    npair = nq // 2
    rows2 = 2 * T
    me_dp = lax.axis_index("dp")
    m = lax.axis_index("mp")
    c = m % 2
    q = lax.div(m, 2)
    sib = {"mp": q * 2 + (1 - c)}
    ssem, rsem = S["ssem"], S["rsem"]
    sem_of = {}

    def sem(key):
        return sem_of.setdefault(key, len(sem_of))

    def peer(i):
        return {"mp": xor(q, i) * 2 + c}

    def dpeer(k):
        return {"dp": xor(me_dp, k)}

    def copy(key, src, dst, dev):
        k = sem(key)
        return pltpu.make_async_remote_copy(
            src_ref=src, dst_ref=dst, send_sem=ssem.at[k], recv_sem=rsem.at[k],
            device_id=dev, device_id_type=MESH)

    XT, XC = S["XT"], S["XC"]
    lsem = S["lsem"]
    own_rows = pl.ds(pl.multiple_of(c * T, T), T)
    plan = [("w_in", S["v_in"]), ("tok", XT.at[c]), ("vec", S["v_vec"]), ("freq", S["v_freq"]),
            ("w_out", S["v_out"]), ("carried", S["v_car"]), ("cot", XC.at[own_rows]),
            ("w_up", S["v_up"]), ("w_down", S["v_down"])]
    loads = {}
    for k, (name, dst) in enumerate(plan):
        loads[name] = pltpu.make_async_copy(S[name], dst, lsem.at[k])
        loads[name].start()

    barrier = pltpu.get_barrier_semaphore()
    count = 0
    for r in range(1, 2 * nq):
        pl.semaphore_signal(barrier, inc=1, device_id={"mp": xor(m, r)}, device_id_type=MESH)
        count += 1
    for k in range(1, ndp):
        pl.semaphore_signal(barrier, inc=1, device_id=dpeer(k), device_id_type=MESH)
        count += 1

    Win, Wout, Wup, Wdown = S["Win"], S["Wout"], S["Wup"], S["Wdown"]
    w_in = S["v_in"]
    loads["w_in"].wait()
    Win[0] = jnp.concatenate(
        [w_in[pl.ds(0, D, 2), :], w_in[pl.ds(1, D, 2), :]], axis=1).astype(BF16)
    loads["w_out"].wait()
    Wout[0] = S["v_out"][...].astype(BF16)
    loads["tok"].wait()
    pl.semaphore_wait(barrier, count)

    sends = []
    puts = []

    def put(src, dst):
        cp = pltpu.make_async_copy(src, dst, S["osem"].at[len(puts)])
        cp.start()
        puts.append(cp)

    def go(cp):
        cp.start()
        sends.append(cp)
        return cp

    side = me_dp % 2

    class Gather:
        def __init__(self, name, W):
            part = W.shape[1] // 4

            def rows(first, n):
                return pl.ds(pl.multiple_of(first * part, 16), n * part)

            def cp(key, i, k, r, dev):
                return copy((name, key, k), W.at[i].at[r], W.at[k].at[r], dev)

            self.direct = {i: cp("d", 0, i, rows(side, 3), peer(i)) for i in (1, 2)}
            self.cross = (cp("x", 2, 3, rows(2 * side, 1), peer(1)),
                          cp("y", 1, 3, rows(2 * side + 1, 1), peer(2)))
            self.swap = {i: cp("z", i, i, rows(3 * side, 1), dpeer(1)) for i in (1, 2)}
            self.swap[3] = cp("z", 3, 3, rows(2 * side, 2), dpeer(1))

        def start(self):
            go(self.direct[1])
            go(self.direct[2])

        def forward(self):
            self.direct[2].wait_recv()
            go(self.cross[0])
            self.direct[1].wait_recv()
            go(self.cross[1])
            go(self.swap[1])
            go(self.swap[2])

        def forward_far(self):
            for cp in self.cross:
                cp.wait_recv()
            go(self.swap[3])

        def finish(self, i):
            self.swap[i].wait_recv()

    g_in, g_out, g_up, g_down = (
        Gather(n, W) for n, W in (("in", Win), ("out", Wout), ("up", Wup), ("down", Wdown)))
    cp_tok = go(copy("tok", XT.at[c], XT.at[c], sib))
    g_in.start()
    g_out.start()
    CS, Cin = S["CS"], S["Cin"]

    loads["vec"].wait()
    loads["freq"].wait()
    vec = S["v_vec"]
    gain_a = vec[0:1, :]
    gain_f = vec[1:2, :]
    row_i = lax.broadcasted_iota(jnp.int32, (T, T), 0)
    col_i = lax.broadcasted_iota(jnp.int32, (T, T), 1)
    gap = row_i ^ col_i
    lower = row_i > col_i
    upper = row_i < col_i
    LV, MK, MT, TRI = S["LV"], S["MK"], S["MT"], S["TRI"]
    code = jnp.where(row_i == col_i, 0.0, -1.0)
    MK[0] = jnp.where(row_i == col_i, 1.0, 0.0).astype(BF16)
    MT[0] = jnp.where(row_i == col_i, 1.0, 0.0).astype(BF16)
    for lv in range(nlev):
        h = 1 << lv
        here = (gap >= h) & (gap < 2 * h)
        code = jnp.where(lower & here, float(lv + 1), code)
        MK[lv + 1] = jnp.where(lower & here, 1.0, 0.0).astype(BF16)
        MT[lv + 1] = jnp.where(upper & here, 1.0, 0.0).astype(BF16)
        bit = (row_i & h) != 0
        same = gap < h
        take = same & ((bit & (col_i >= row_i)) | ((~bit) & (col_i < row_i)))
        TRI[:, lv * T:(lv + 1) * T] = jnp.where(take, 1.0, 0.0).astype(BF16)
    TRI[:, nlev * T:(nlev + 1) * T] = jnp.where(col_i >= row_i, 1.0, 0.0).astype(BF16)
    LV[...] = code
    VEC = S["VEC"]
    VEC[...] = jnp.zeros_like(VEC)
    WBH, WBL = S["WBH"], S["WBL"]
    WBH[...] = jnp.zeros_like(WBH)
    WBL[...] = jnp.zeros_like(WBL)
    for i in range(nq):
        freq = S["v_freq"][2 * xor(q, i) + c]
        high = freq.astype(BF16)
        rest = (freq - high.astype(F32)).astype(BF16)
        WBH[i, 0:64, 0:128] = high
        WBH[i, 64:128, 128:256] = high
        WBL[i, 0:64, 0:128] = rest
        WBL[i, 64:128, 128:256] = rest
    SZ = S["SZ"]
    SZ[...] = jnp.zeros_like(SZ)

    NA = S["NA"]
    cp_tok.wait_recv()
    for s in range(2):
        x = XT[s].astype(F32)
        NA[s * T:(s + 1) * T, :] = (x * rms_scale(x) * gain_a).astype(BF16)

    PH, TV = S["PH"], S["TV"]
    lane_row = lax.broadcasted_iota(jnp.int32, (1, 128), 1)
    cp_car = [None]
    for i in range(nq):
        if i == 1:
            g_in.forward()
            g_out.forward()
            for k in range(1, nq):
                cp_car.append(go(copy(
                    ("car", k), CS.at[pl.ds(2 * xor(q, k), 2)], Cin.at[k], peer(k))))
            g_up.start()
        if i == 2:
            g_in.forward_far()
            g_out.forward_far()
        if i > 0:
            g_in.finish(i)
        bias = vec[2:3, pl.ds(pl.multiple_of(xor(q, i) * 128, 128), 128)]
        bias = jnp.where(c == 0, pltpu.roll(bias, 64, 1), bias)
        bias = jnp.where(lane_row >= 64, bias, 0.0)

        def head(s, _, i=i, bias=bias):
            rows = pl.ds(pl.multiple_of(s * T, T), T)
            pr = mm(NA[rows, :], Win[i])
            t0, t1 = halves(pr)
            TV[i, rows, :] = t1 + bias
            high = t0.astype(BF16)
            rest = (t0 - high.astype(F32)).astype(BF16)
            ang = mm(high, WBH[i]) + (mm(rest, WBH[i]) + mm(high, WBL[i]))
            sin, cos = sincos(ang)
            PH[i, rows, 0:128] = sin[:, :128].astype(BF16)
            PH[i, rows, 128:256] = cos[:, :128].astype(BF16)
            PH[i, rows, 256:384] = sin[:, 128:].astype(BF16)
            PH[i, rows, 384:512] = cos[:, 128:].astype(BF16)
            return 0

        lax.fori_loop(0, 2, head, 0)
        if i == nq - 1:
            g_down.start()
        if i == 0:
            loads["carried"].wait()
            CS[...] = S["v_car"][:, 0].astype(BF16)
            Cin[0] = CS[pl.ds(2 * q, 2)]
            loads["cot"].wait()
            cp_cot = go(copy("cot", XC.at[own_rows], XC.at[own_rows], sib))
            loads["w_up"].wait()
            Wup[0] = S["v_up"][...].astype(BF16)
            loads["w_down"].wait()
            Wdown[0] = S["v_down"][...].astype(BF16)

    lane = lax.broadcasted_iota(jnp.int32, (T, 128), 1)
    first = lane < 64
    row = lax.broadcasted_iota(jnp.int32, (T, 128), 0)
    lane_b = lax.broadcasted_iota(jnp.int32, (T, 256), 1)
    first_b = (lane_b % 128) < 64
    inv_feat = 1.0 / 128.0
    inv_root = 128.0 ** (-0.5)

    def swap(a, h):
        if h < 8:
            return jnp.where((row & h) != 0, pltpu.roll(a, h, 0), pltpu.roll(a, T - h, 0))
        parts = []
        for b in range(T // (2 * h)):
            parts.append(a[(2 * b + 1) * h:(2 * b + 2) * h])
            parts.append(a[2 * b * h:(2 * b + 1) * h])
        return jnp.concatenate(parts, axis=0)

    VV, KK, WW, PP, UU, YY = S["VV"], S["KK"], S["WW"], S["PP"], S["UU"], S["YY"]
    ND, NDL, MX = S["ND"], S["NDL"], S["MX"]
    FS = S["FS"]

    def split_rows(y):
        z = jnp.zeros_like(y)
        mask = first_b[:y.shape[0]]
        return jnp.concatenate([jnp.where(mask, y, z), jnp.where(mask, z, y)], axis=0)

    for j in range(npair):
        i0, i1 = 2 * j, 2 * j + 1
        for i in (i0, i1):
            if i > 0:
                cp_car[i].wait_recv()

        def forward(s, _, i0=i0, i1=i1, j=j):
            rows = pl.ds(pl.multiple_of(s * T, T), T)
            for k, i in enumerate((i0, i1)):
                SZ[j, s, k * 64:k * 64 + 64, k * 256:k * 256 + 256] = Cin[i, s, 0]
                SZ[j, s, 128 + k * 64:192 + k * 64, k * 256:k * 256 + 256] = Cin[i, s, 1]
            ta, tb = TV[i0, rows, :], TV[i1, rows, :]
            value = jnp.where(first, ta, pltpu.roll(tb, 64, 1))
            gate = jnp.where(first, pltpu.roll(ta, 64, 1), tb)
            small = jnp.exp(-jnp.abs(gate))
            big = 1.0 / (1.0 + small)
            rest = small * big
            keep = jnp.where(gate >= 0, big, rest)
            write = jnp.where(gate >= 0, rest, big)
            written = write * value
            VV[j, rows, :] = value
            KK[j, rows, :] = keep
            WW[j, rows, :] = write
            scores = [
                (mm_nt(PH[i, rows, 0:256], PH[i, rows, 256:512]) * inv_feat).astype(BF16)
                for i in (i0, i1)]
            total, pre, suf = keep, keep, jnp.ones_like(keep)
            y = jnp.concatenate([written, write], axis=1).astype(BF16)
            left = jnp.concatenate([sc * MK[0] for sc in scores], axis=1)
            acc = mm(left, split_rows(y))
            for lv in range(nlev):
                h = 1 << lv
                if lv > 0:
                    y = jnp.concatenate([suf * written, suf * write], axis=1).astype(BF16)
                YY[j, s, lv] = y
                PP[j, s, lv] = pre.astype(BF16)
                UU[j, s, lv] = suf.astype(BF16)
                if 2 * h == T:
                    left = jnp.concatenate([sc[h:, :h] for sc in scores], axis=1)
                    nd = mm(left, split_rows(y[:h])) * pair_cat(pre[h:])
                    nd = jnp.concatenate([jnp.zeros_like(nd), nd], axis=0)
                else:
                    left = jnp.concatenate([sc * MK[lv + 1] for sc in scores], axis=1)
                    nd = mm(left, split_rows(y)) * pair_cat(pre)
                acc = acc + nd
                NDL[j, s, lv] = nd.astype(BF16)
                other = swap(total, h)
                upper_half = (row & h) != 0
                pre = jnp.where(upper_half, pre * other, pre)
                suf = jnp.where(upper_half, suf, suf * other)
                total = total * other
            PP[j, s, nlev] = pre.astype(BF16)
            phq = jnp.concatenate([PH[i, rows, 0:256] for i in (i0, i1)], axis=1)
            nd = mm_nt(phq, SZ[j, s]) * (pair_cat(pre) * inv_root)
            NDL[j, s, nlev] = nd.astype(BF16)
            acc = acc + nd
            ND[j, s] = acc
            num, den = halves(acc)
            MX[rows, j * 128:(j + 1) * 128] = (
                num * lax.rsqrt(den * den + DEN_FLOOR)).astype(BF16)
            YY[j, s, nlev] = jnp.concatenate([suf * written, suf * write], axis=1).astype(BF16)
            return 0

        lax.fori_loop(0, 2, forward, 0)

    AP, AQ, MID, NF = S["AP"], S["AQ"], S["MID"], S["NF"]
    g_up.forward()
    for i in range(1, nq):
        g_out.finish(i)
    wout = jnp.concatenate([Wout[i] for i in range(nq)], axis=0)
    cp_att = []
    for s in range(2):
        rows = pl.ds(s * T, T)
        AP[rows, :] = mm(MX[rows, :], wout)
        cp_att.append(go(copy(("att", s), AP.at[rows], AQ.at[rows], sib)))
    g_down.forward()
    for s in range(2):
        cp_att[s].wait_recv()
        rows = slice(s * T, (s + 1) * T)
        middle = XT[s].astype(F32) + (AP[rows, :] + AQ[rows, :])
        MID[rows, :] = middle
        NF[rows, :] = (middle * rms_scale(middle) * gain_f).astype(BF16)

    FO, DN = AP, S["DN"]
    for cp in cp_att:
        cp.wait_send()
    cp_cot.wait_recv()
    NFT, CT = S["NFT"], XC
    NFT[...] = jnp.transpose(NF[...], (1, 0))

    class Scatter:
        def __init__(self, name):
            self.name = name
            self.own, self.out, self.mid, self.got = (S[name + k] for k in "ospr")
            self.half = self.own.shape[0] // 2
            self.top, self.bottom = pl.ds(0, self.half), pl.ds(self.half, self.half)

        def send(self, key, src, dst, i):
            cp = go(copy((self.name, key), src, dst, peer(i)))
            setattr(self, key, cp)

        def put(self, i, value):
            if i == 0:
                self.own[...] = value
                return
            out = self.out
            out[i - 1] = value.astype(BF16)
            if i == 1:
                self.send("a1", out.at[0].at[self.top], self.got.at[0].at[self.top], 1)
            elif i == 2:
                self.send("a2", out.at[1].at[self.bottom], self.got.at[1].at[self.bottom], 2)
            else:
                self.send("p1", out.at[2].at[self.top], self.mid.at[0], 1)
                self.send("p2", out.at[2].at[self.bottom], self.mid.at[1], 2)

        def middle(self):
            out, half = self.out, self.half
            self.p1.wait_recv()
            out[1, :half] = (out[1, :half].astype(F32) + self.mid[0].astype(F32)).astype(BF16)
            self.send("b2", out.at[1].at[self.top], self.got.at[1].at[self.top], 2)
            self.p2.wait_recv()
            out[0, half:] = (out[0, half:].astype(F32) + self.mid[1].astype(F32)).astype(BF16)
            self.send("b1", out.at[0].at[self.bottom], self.got.at[0].at[self.bottom], 1)

        def total(self):
            for cp in (self.a1, self.a2, self.b1, self.b2):
                cp.wait_recv()
            return self.own[...] + (self.got[0].astype(F32) + self.got[1].astype(F32))

    sc_up, sc_down, sc_in, sc_out = (Scatter(n) for n in ("gu", "gd", "gi", "go"))
    for i in range(nq):
        if i == 1:
            g_up.forward_far()
            g_down.forward_far()
        if i > 0:
            g_up.finish(i)
            g_down.finish(i)
        up, down = Wup[i], Wdown[i]
        pre = mm(NF[...], up)
        square = pre * pre
        th = jnp.tanh(0.7978845608028654 * (pre + 0.044715 * pre * square))
        hidden = (0.5 * pre * (1.0 + th)).astype(BF16)
        slope = 0.5 * (1.0 + th) + 0.5 * pre * (1.0 - th * th) * (
            0.7978845608028654 * (1.0 + 0.134145 * square))
        d_pre = (mm_nt(CT[...], down) * slope).astype(BF16)
        fo = mm(hidden, down)
        dn = mm_nt(d_pre, up)
        if i == 0:
            FO[...] = fo
            DN[...] = dn
        else:
            FO[...] += fo
            DN[...] += dn
        sc_down.put(i, mm_tn(hidden, CT[...]))
        sc_up.put(i, mm(NFT[...], d_pre))
    FOR, DNR = S["FOR"], S["DNR"]
    cp_dn = [go(copy(("dn", s), DN.at[pl.ds(s * T, T)], DNR.at[pl.ds(s * T, T)], sib))
             for s in range(2)]
    cp_fo = go(copy("fo", FO.at[pl.ds((1 - c) * T, T)], FOR, sib))
    DA, DM, DMI = S["DA"], S["DM"], S["DMI"]
    for s in range(2):
        cp_dn[s].wait_recv()
        rows = slice(s * T, (s + 1) * T)
        middle = MID[rows, :]
        scale = rms_scale(middle)
        unit = middle * scale
        grad = DN[rows, :] + DNR[rows, :]
        d_mid = XC[rows, :].astype(F32) + norm_back(grad, unit, scale, gain_f)
        DA[rows, :] = d_mid.astype(BF16)
        gain_grad = jnp.sum(grad * unit, axis=0, keepdims=True)

        @pl.when(c == s)
        def _(gain_grad=gain_grad, d_mid=d_mid):
            DMI[...] = d_mid
            for t in range(D // 128):
                VEC[D // 128 + t:D // 128 + t + 1, :] = gain_grad[:, t * 128:(t + 1) * 128]

    cp_fo.wait_recv()
    S["BO"][...] = (MID[own_rows, :] + (FO[own_rows, :] + FOR[...])).astype(BF16)
    put(S["BO"], S["block_out"])
    DM[...] = mm_nt(DA[...], wout)
    go_all = mm_tn(MX[...], DA[...])
    for i in range(nq):
        sc_out.put(i, go_all[64 * i:64 * i + 64])

    def mixed_back(dm, nd):
        num, den = halves(nd)
        r = lax.rsqrt(den * den + DEN_FLOOR)
        d_num = dm * r
        return d_num, -(d_num * num) * den * (r * r)

    XL, DPJ, CG = S["XL"], S["DPJ"], S["CG"]
    ZD, ZU, ZI = S["ZD"], S["ZU"], S["ZI"]
    NS = S["NS"]
    LT = D // 128

    def fold(z):
        return jnp.sum((z * z).reshape(z.shape[0] // 8, 8, 128), axis=0)

    def tiles_of(a):
        return [a[:, t * 128:(t + 1) * 128].astype(BF16) for t in range(a.shape[1] // 128)]

    def lay(Z, parts):
        at = 0
        for part in parts:
            Z[at:at + part.shape[0], :] = part
            at += part.shape[0]

    def reduce_dp(name, Z, R, out):
        piece = Z.shape[0] // ndp
        mine = pl.ds(pl.multiple_of(me_dp * piece, 16), piece)
        scatter = [copy((name, "rs", k), Z.at[pl.ds(xor(me_dp, k) * piece, piece)], R.at[k - 1],
                        dpeer(k)) for k in range(1, ndp)]
        spread = [copy((name, "ag", k), out.at[mine], out.at[mine], dpeer(k))
                  for k in range(1, ndp)]

        def start():
            for cp in scatter:
                go(cp)

        def middle():
            for cp in scatter:
                cp.wait_recv()
            total = tree_sum([Z[mine, :].astype(F32)] + [R[k].astype(F32) for k in range(ndp - 1)])
            total = total.astype(BF16)
            out[mine, :] = total
            for cp in spread:
                go(cp)
            return fold(total.astype(F32))

        def finish():
            for cp in spread:
                cp.wait_recv()
        return start, middle, finish

    nbit = ndp.bit_length() - 1

    class Halving:
        def __init__(self, name, Z, R, out):
            self.Z, self.R, self.out = Z, R, out
            size, first, at = Z.shape[0], 0, 0
            self.rs, self.ag, self.keep, self.land = [], [], [], []
            for b in range(nbit):
                bit = lax.div(me_dp, 1 << b) % 2
                size //= 2
                keep, give = first + bit * size, first + (1 - bit) * size
                land = R.at[pl.ds(at, size)]
                self.keep.append(pl.ds(pl.multiple_of(keep, 16), size))
                self.land.append(pl.ds(at, size))
                self.rs.append(copy((name, "rs", b), Z.at[pl.ds(give, size)], land, dpeer(1 << b)))
                seg = pl.ds(pl.multiple_of(keep, 16), size)
                self.ag.append(copy((name, "ag", b), out.at[seg], out.at[seg], dpeer(1 << b)))
                first, at = keep, at + size
            self.at = 0
            self.square = None

        def start(self):
            go(self.rs[0])

        def step(self):
            for _ in range(max(nbit // 2, 1)):
                k = self.at
                self.at += 1
                if k < nbit:
                    self.rs[k].wait_recv()
                    rows = self.keep[k]
                    total = self.Z[rows, :].astype(F32) + self.R[self.land[k], :].astype(F32)
                    total = total.astype(BF16)
                    if k + 1 < nbit:
                        self.Z[rows, :] = total
                        go(self.rs[k + 1])
                    else:
                        self.out[rows, :] = total
                        go(self.ag[k])
                        self.square = fold(total.astype(F32))
                else:
                    b = 2 * nbit - 1 - k
                    self.ag[b].wait_recv()
                    if b > 0:
                        go(self.ag[b - 1])

    zd = Halving("zd", ZD, S["ZDR"], S["ZDO"])
    zu = Halving("zu", ZU, S["ZUR"], S["ZUO"])
    zi = Halving("zi", ZI, S["ZIR"], S["ZIO"])

    def hook_0():
        sc_down.middle()
        sc_up.middle()
        sc_out.middle()

    def hook_1():
        lay(ZD, tiles_of(sc_down.total()))
        zd.start()

    def hook_2():
        zd.step()
        lay(ZU, tiles_of(sc_up.total()) + tiles_of(sc_out.total()))
        zu.start()

    NAT = NFT
    NAT[...] = jnp.transpose(NA[...], (1, 0))
    for j in (1, 0):
        i0, i1 = 2 * j, 2 * j + 1

        bias_sum = jnp.zeros((1, 128), F32)
        for s in range(2):
            rows = pl.ds(s * T, T)
            if s == 1:
                if j == 1:
                    hook_0()
                else:
                    hook_2()
            dm = DM[rows, j * 128:(j + 1) * 128]
            d_num, d_den = mixed_back(dm, ND[j, s])
            g = jnp.concatenate([d_num, d_den], axis=1)
            value, keep, write = VV[j, rows, :], KK[j, rows, :], WW[j, rows, :]
            written = write * value
            scores = [
                (mm_nt(PH[i, rows, 256:512], PH[i, rows, 0:256]) * inv_feat).astype(BF16)
                for i in (i0, i1)]
            levels = LV[...]
            z16 = jnp.zeros((T, 256), BF16)
            gb = g.astype(BF16)
            g0, g1 = jnp.where(first_b, gb, z16), jnp.where(first_b, z16, gb)
            left = jnp.concatenate([sc * MT[0] for sc in scores], axis=1)
            ab = mm(left, jnp.concatenate([g0, g1], axis=0))
            y = YY[j, s, 0]
            ds0 = mm_nt(g0, y)
            ds1 = mm_nt(g1, y)
            for lv in range(nlev - 1):
                h = 1 << lv
                pg = (pair_cat(PP[j, s, lv].astype(F32)) * g).astype(BF16)
                g0, g1 = jnp.where(first_b, pg, z16), jnp.where(first_b, z16, pg)
                left = jnp.concatenate([sc * MT[lv + 1] for sc in scores], axis=1)
                part = mm(left, jnp.concatenate([g0, g1], axis=0)) * pair_cat(UU[j, s, lv].astype(F32))
                ab = ab + part
                pa, pb = halves(part)
                from_key = written * pa + write * pb
                oa, ob = halves(g * NDL[j, s, lv].astype(F32))
                XL[lv * T:(lv + 1) * T, :] = jnp.where(
                    (row & h) != 0, oa + ob, from_key).astype(BF16)
                y = YY[j, s, lv]
                hit = levels == float(lv + 1)
                ds0 = jnp.where(hit, mm_nt(g0, y), ds0)
                ds1 = jnp.where(hit, mm_nt(g1, y), ds1)
            causal = levels >= 0.0
            h = T // 2
            pg = (pair_cat(PP[j, s, nlev - 1, h:].astype(F32)) * g[h:]).astype(BF16)
            both = split_rows(pg)
            left = jnp.concatenate([sc[:h, h:] for sc in scores], axis=1)
            part = mm(left, both) * pair_cat(UU[j, s, nlev - 1, :h].astype(F32))
            ab = jnp.concatenate([ab[:h] + part, ab[h:]], axis=0)
            pa, pb = halves(part)
            oa, ob = halves(g[h:] * NDL[j, s, nlev - 1, h:].astype(F32))
            XL[(nlev - 1) * T:(nlev - 1) * T + h, :] = (
                written[:h] * pa + write[:h] * pb).astype(BF16)
            XL[(nlev - 1) * T + h:nlev * T, :] = (oa + ob).astype(BF16)
            y = YY[j, s, nlev - 1, :h]

            def place(ds, rows):
                low = jnp.concatenate([mm_nt(rows, y), ds[h:, h:]], axis=1)
                return jnp.concatenate([ds[:h], low], axis=0)

            ds0, ds1 = place(ds0, both[:h]), place(ds1, both[h:])
            ds0 = jnp.where(causal, ds0, 0.0).astype(BF16)
            ds1 = jnp.where(causal, ds1, 0.0).astype(BF16)
            oa, ob = halves(g * NDL[j, s, nlev].astype(F32))
            XL[nlev * T:, :] = (oa + ob).astype(BF16)
            pg = (pair_cat(PP[j, s, nlev].astype(F32)) * g).astype(BF16)
            opening = mm(pg, SZ[j, s]) * inv_root
            d_log = mm(TRI[...], XL[...])
            a, b = halves(ab)
            d_value = write * a
            d_write = value * a + b
            d_gate = write * (d_log - keep * d_write)
            tiles = (jnp.where(first, d_value, pltpu.roll(d_gate, 64, 1)),
                     jnp.where(first, pltpu.roll(d_value, 64, 1), d_gate))
            for k, (i, ds) in enumerate(((i0, ds0), (i1, ds1))):
                pq, pk = PH[i, rows, 0:256], PH[i, rows, 256:512]
                dq = mm(ds, pk) * inv_feat + opening[:, k * 256:k * 256 + 256]
                dk = mm_tn(ds, pq) * inv_feat
                pq, pk = pq.astype(F32), pk.astype(F32)
                aq = pq[:, 128:] * dq[:, :128] - pq[:, :128] * dq[:, 128:]
                ak = pk[:, 128:] * dk[:, :128] - pk[:, :128] * dk[:, 128:]
                d_ang = jnp.concatenate([aq, ak], axis=1).astype(BF16)
                DPJ[i, rows, 0:128] = mm_nt(d_ang, WBH[i]).astype(BF16)
                DPJ[i, rows, 128:256] = tiles[k].astype(BF16)
            bias_sum = bias_sum + jnp.sum(d_gate, axis=0, keepdims=True)

        for k, i in enumerate((i0, i1)):
            VEC[pl.ds(2 * D // 128 + 2 * xor(q, i) + c, 1), :] = (
                bias_sum if k else pltpu.roll(bias_sum, 64, 1))

        for i in (i1, i0):
            sc_in.put(i, mm(NAT[...], DPJ[i]))
        if j == 1:
            hook_1()

    sc_in.middle()
    zd.step()
    zu.step()
    CR, FR = S["CR"], S["FR"]
    DX = FO
    cp_fo.wait_send()
    DX[...] = mm_nt(DPJ[0], Win[0])
    for i in range(1, nq):
        DX[...] += mm_nt(DPJ[i], Win[i])
    DXR = S["DXR"]
    cp_dx = go(copy("dx", DX.at[pl.ds((1 - c) * T, T)], DXR, sib))
    lay(ZI, tiles_of(sc_in.total()))
    zi.start()
    for j in range(npair):
        i0, i1 = 2 * j, 2 * j + 1

        def states(s, _, i0=i0, i1=i1, j=j):
            rows = pl.ds(pl.multiple_of(s * T, T), T)
            d_num, d_den = mixed_back(DM[rows, j * 128:(j + 1) * 128], ND[j, s])
            pre = PP[j, s, nlev].astype(F32)
            pg = (pair_cat(pre) * jnp.concatenate([d_num, d_den], axis=1)).astype(BF16)
            phq = jnp.concatenate([PH[i, rows, 0:256] for i in (i0, i1)], axis=1)
            phk = jnp.concatenate([PH[i, rows, 256:512] for i in (i0, i1)], axis=1)
            cg = mm_tn(pg, phq) * inv_root
            new = mm_tn(YY[j, s, nlev], phk) * inv_root
            last = jnp.transpose(pre[T - 128:, :], (1, 0))[:, 127:128]
            for k, i in enumerate((i0, i1)):
                kept = last[k * 64:k * 64 + 64, :]
                for z in range(2):
                    block = (slice(z * 128 + k * 64, z * 128 + k * 64 + 64),
                             slice(k * 256, k * 256 + 256))
                    CG[i, s, z] = cg[block].astype(BF16)
                    FS[i, s, z] = (kept * Cin[i, s, z].astype(F32) + new[block]).astype(BF16)
            return 0

        lax.fori_loop(0, 2, states, 0)
    cp_cg = [None] + [
        go(copy(("cg", i), CG.at[i], CR.at[pl.ds(2 * q, 2)], peer(i))) for i in range(1, nq)]
    cp_fin = [None] + [
        go(copy(("fin", i), FS.at[i], FR.at[pl.ds(2 * q, 2)], peer(i))) for i in range(1, nq)]
    CR[pl.ds(2 * q, 2)] = CG[0]
    FR[pl.ds(2 * q, 2)] = FS[0]
    zd.step()
    zu.step()
    cp_dx.wait_recv()
    zi.step()
    x = XT[c].astype(F32)
    scale = rms_scale(x)
    unit = x * scale
    grad = DX[own_rows, :] + DXR[...]
    S["TG"][...] = DMI[...] + norm_back(grad, unit, scale, gain_a)
    put(S["TG"], S["token_grad"])
    gain_grad = jnp.sum(grad * unit, axis=0, keepdims=True)
    for t in range(LT):
        VEC[t:t + 1, :] = gain_grad[:, t * 128:(t + 1) * 128]
    VR = S["VR"]
    VS = S["VS"]
    cp_v = go(copy("v0", VEC, VR.at[0], sib))

    zu.step()
    zi.step()
    NS[0] = zd.square + zu.square + zi.square
    NR = S["NR"]
    cp_n = [go(copy(("n", r), NS.at[0], NR.at[r - 1], {"mp": xor(m, r)})) for r in range(1, 2 * nq)]
    cp_v.wait_recv()
    VS[0] = VEC[...] + VR[0]
    cp_vs = [go(copy(("v1", i), VS.at[0], VR.at[i], peer(i))) for i in range(1, nq)]

    def put_tiles(Z, first, name, n, count):
        for t in range(count):
            put(Z.at[pl.ds(first + t * n, n)], S[name].at[:, pl.ds(t * 128, 128)])

    zi.step()
    zd.step()
    put_tiles(S["ZDO"], 0, "g_down", FH, LT)
    for cp in cp_n:
        cp.wait_recv()
    NS[1] = tree_sum([NS[0]] + [NR[r] for r in range(2 * nq - 1)])
    cp_m = [go(copy(("m", k), NS.at[1], NR.at[2 * nq - 2 + k], dpeer(k))) for k in range(1, ndp)]
    for cp in cp_vs:
        cp.wait_recv()
    VS[1] = tree_sum([VS[0]] + [VR[i] for i in range(1, nq)])
    cp_vd = [go(copy(("v2", k), VS.at[1], VR.at[nq - 1 + k], dpeer(k))) for k in range(1, ndp)]
    zu.step()
    put_tiles(S["ZUO"], 0, "g_up", D, FH // 128)
    put_tiles(S["ZUO"], D * FH // 128, "g_out", 64, LT)

    for i in range(1, nq):
        cp_cg[i].wait_recv()
    put(CR, S["cgrad"])
    for i in range(1, nq):
        cp_fin[i].wait_recv()
    put(FR, S["fin"])
    for cp in cp_vd:
        cp.wait_recv()
    vtot = tree_sum([VS[1]] + [VR[nq - 1 + k] for k in range(1, ndp)])
    g_vec = S["g_vec"]
    for t in range(LT):
        part = slice(t * 128, (t + 1) * 128)
        g_vec[0:1, part] = vtot[t:t + 1, :]
        g_vec[1:2, part] = vtot[LT + t:LT + t + 1, :]
        even = vtot[2 * LT + 2 * t:2 * LT + 2 * t + 1, :]
        odd = vtot[2 * LT + 2 * t + 1:2 * LT + 2 * t + 2, :]
        g_vec[2:3, part] = jnp.where(lane_row < 64, pltpu.roll(even, 64, 1), odd)
    lane_v = lax.broadcasted_iota(jnp.int32, VEC.shape, 1)
    row_v = lax.broadcasted_iota(jnp.int32, VEC.shape, 0)
    vmask = (row_v < 2 * LT) | (lane_v >= 64)
    vsq = fold(jnp.where(vmask, vtot, 0.0))
    for cp in cp_m:
        cp.wait_recv()
    S["sq"][...] = tree_sum([NS[1]] + [NR[2 * nq - 2 + k] for k in range(1, ndp)]) + vsq
    zi.step()
    put_tiles(S["ZIO"], 0, "g_in", D, 2)
    for cp in puts:
        cp.wait()
    for cp in sends:
        if cp is not cp_fo and all(cp is not a for a in cp_att):
            cp.wait_send()


def layer_call(ndp, nmp, args, shapes):
    T, D = shapes["tok"].shape
    nq = nmp // 2
    FH = shapes["w_up"].shape[1]
    nlev = (T - 1).bit_length()
    npair = nq // 2
    nseq = 2 * nq
    lt = D // 128
    zd = D * FH // 128
    zu = (D * FH + 64 * D) // 128
    zi = D * 256 // 128
    vrows = 2 * lt + nseq
    R = nq - 1
    V = pltpu.VMEM
    scratch = dict(
        XT=V((2, T, D), BF16), XC=V((2 * T, D), BF16),
        Win=V((nq, D, 256), BF16), Wout=V((nq, 64, D), BF16),
        Wup=V((nq, D, FH), BF16), Wdown=V((nq, FH, D), BF16),
        CS=V((nseq, 2, 64, 256), BF16), Cin=V((nq, 2, 2, 64, 256), BF16),
        LV=V((T, T), F32), MK=V((nlev + 1, T, T), BF16), MT=V((nlev + 1, T, T), BF16),
        TRI=V((T, (nlev + 1) * T), BF16), VEC=V((vrows, 128), F32),
        WBH=V((nq, 128, 256), BF16), WBL=V((nq, 128, 256), BF16),
        SZ=V((npair, 2, 256, 512), BF16), NA=V((2 * T, D), BF16),
        PH=V((nq, 2 * T, 512), BF16), TV=V((nq, 2 * T, 128), F32),
        VV=V((npair, 2 * T, 128), F32), KK=V((npair, 2 * T, 128), F32),
        WW=V((npair, 2 * T, 128), F32), PP=V((npair, 2, nlev + 1, T, 128), BF16),
        UU=V((npair, 2, nlev, T, 128), BF16), YY=V((npair, 2, nlev + 1, T, 256), BF16),
        ND=V((npair, 2, T, 256), F32), NDL=V((npair, 2, nlev + 1, T, 256), BF16),
        MX=V((2 * T, 64 * nq), BF16), FS=V((nq, 2, 2, 64, 256), BF16),
        FR=V((nseq, 2, 64, 256), BF16), AP=V((2 * T, D), F32), AQ=V((2 * T, D), F32),
        MID=V((2 * T, D), F32), NF=V((2 * T, D), BF16),
        DN=V((2 * T, D), F32), NFT=V((D, 2 * T), BF16),
        guo=V((D, FH), F32), gus=V((R, D, FH), BF16),
        gup=V((2, D // 2, FH), BF16), gur=V((2, D, FH), BF16),
        gdo=V((FH, D), F32), gds=V((R, FH, D), BF16),
        gdp=V((2, FH // 2, D), BF16), gdr=V((2, FH, D), BF16),
        gio=V((D, 256), F32), gis=V((R, D, 256), BF16),
        gip=V((2, D // 2, 256), BF16), gir=V((2, D, 256), BF16),
        goo=V((64, D), F32), gos=V((R, 64, D), BF16),
        gop=V((2, 32, D), BF16), gor=V((2, 64, D), BF16),
        FOR=V((T, D), F32), DNR=V((2 * T, D), F32),
        DA=V((2 * T, D), BF16), DM=V((2 * T, 64 * nq), F32), DMI=V((T, D), F32),
        XL=V(((nlev + 1) * T, 128), BF16), DPJ=V((nq, 2 * T, 256), BF16),
        CG=V((nq, 2, 2, 64, 256), BF16), CR=V((nseq, 2, 64, 256), BF16),
        BO=V((T, D), BF16), TG=V((T, D), F32), DXR=V((T, D), F32), ZD=V((zd, 128), BF16), ZU=V((zu, 128), BF16),
        ZI=V((zi, 128), BF16),
        ZDR=V((zd, 128), BF16), ZUR=V((zu, 128), BF16),
        ZIR=V((zi, 128), BF16),
        ZDO=V((zd, 128), BF16), ZUO=V((zu, 128), BF16), ZIO=V((zi, 128), BF16),
        VR=V((nq + ndp, vrows, 128), F32), VS=V((2, vrows, 128), F32),
        NR=V((2 * nq - 2 + ndp, 8, 128), F32), NS=V((2, 8, 128), F32),
        v_in=V((2 * D, 128), F32), v_vec=V((3, D), F32), v_freq=V(shapes["freq"].shape, F32),
        v_out=V((64, D), F32), v_car=V(shapes["carried"].shape, F32),
        v_up=V((D, FH), F32), v_down=V((FH, D), F32),
    )
    nsem = 80 + 3 * R + 9 * ndp + 2 * nq
    scratch["osem"] = pltpu.SemaphoreType.DMA((16 + 2 * lt,))
    scratch["lsem"] = pltpu.SemaphoreType.DMA((len(args),))
    scratch["ssem"] = pltpu.SemaphoreType.DMA((nsem,))
    scratch["rsem"] = pltpu.SemaphoreType.DMA((nsem,))
    outs = dict(
        block_out=((T, D), BF16), token_grad=((T, D), F32),
        fin=((nseq, 2, 64, 256), BF16), cgrad=((nseq, 2, 64, 256), BF16),
        g_in=((D, 256), BF16), g_out=((64, D), BF16),
        g_up=((D, FH), BF16), g_down=((FH, D), BF16),
        g_vec=((3, D), F32), sq=((8, 128), F32))
    names = list(args) + list(outs) + list(scratch)
    cfg = dict(names=names, ndp=ndp, nq=nq, T=T, D=D, nlev=nlev, FH=FH)
    vm = pl.BlockSpec(memory_space=pltpu.VMEM)
    res = pl.pallas_call(
        functools.partial(layer_kernel, cfg),
        out_shape=[jax.ShapeDtypeStruct(s, d) for s, d in outs.values()],
        in_specs=[pl.BlockSpec(memory_space=pl.ANY)] * len(args),
        out_specs=[vm if n in ("g_vec", "sq") else pl.BlockSpec(memory_space=pl.ANY) for n in outs],
        scratch_shapes=list(scratch.values()),
        compiler_params=pltpu.CompilerParams(
            collective_id=0, has_side_effects=True, vmem_limit_bytes=62 * 2**20),
        name="layer",
    )(*args.values())
    return dict(zip(outs, res))


def adam(w, g, first, second, rate, decay):
    first_new = B1 * first + (1.0 - B1) * g
    second_new = B2 * second + (1.0 - B2) * g * g
    first_hat = first_new / (1.0 - B1**STEP)
    second_hat = second_new / (1.0 - B2**STEP)
    w_new = w - rate * (first_hat / (jnp.sqrt(second_hat) + ADAM_EPS) + decay * w)
    return first_new, second_new, w_new


def adam_kernel(names, nout, *refs):
    S = dict(zip(names, refs))
    norm = jnp.sqrt(jnp.sum(S["sq"][...]))
    factor = CLIP / jnp.maximum(norm, CLIP)

    def matrix(key):
        g = S["g_" + key][...].astype(F32) * factor
        res = adam(S[key + "0"][...], g, S[key + "1"][...], S[key + "2"][...], RATE_MATRIX, DECAY)
        for k in range(3):
            S["n%s%d" % (key, k)][...] = res[k]
        S["n%s3" % key][...] = res[2].astype(BF16)

    @pl.when(pl.program_id(0) == 0)
    def _():
        S["norm"][0, 0] = norm
        g = S["g_v"][...] * factor
        res = adam(S["v0"][...], g, S["v1"][...], S["v2"][...], RATE_VECTOR, 0.0)
        for k in range(3):
            S["nv%d" % k][...] = res[k]
        matrix("o")

    for key in "ud":
        matrix(key)
    count = S["i0"].shape[0] // 2
    for t in range(2):
        rows = pl.ds(t, count, 2)
        lanes = slice(t * 128, (t + 1) * 128)
        g = S["g_i"][:, lanes].astype(F32) * factor
        res = adam(S["i0"][rows, :], g, S["i1"][rows, :], S["i2"][rows, :], RATE_MATRIX, DECAY)
        for k in range(3):
            S["ni%d" % k][rows, :] = res[k]
        S["ni3"][:, lanes] = res[2].astype(BF16)
    S["n_block_out"][...] = S["block_out"][...]
    S["n_token_grad"][...] = S["token_grad"][...]
    S["n_fin"][...] = S["fin"][...].astype(F32)
    S["n_cgrad"][...] = S["cgrad"][...].astype(F32)


def adam_call(res, params):
    steps = 2

    def cut(shape):
        block = (shape[0] // steps,) + tuple(shape[1:])
        return pl.BlockSpec(block, lambda g: (g,) + (0,) * (len(shape) - 1))

    def whole(shape):
        return pl.BlockSpec(tuple(shape), lambda g: (0,) * len(shape))

    ins, in_specs, outs, out_specs, names, onames = [], [], [], [], [], []

    def take(name, a, spec):
        names.append(name)
        ins.append(a)
        in_specs.append(spec(a.shape))

    def give(name, shape, dtype, spec):
        onames.append(name)
        outs.append(jax.ShapeDtypeStruct(shape, dtype))
        out_specs.append(spec(shape))

    take("sq", res["sq"], whole)
    for key, full in zip("vioud", ("g_vec", "g_in", "g_out", "g_up", "g_down")):
        spec = whole if key in "vo" else cut
        take("g_" + key, res[full], spec)
        for k, a in enumerate(params[key]):
            take("%s%d" % (key, k), a, spec)
            give("n%s%d" % (key, k), a.shape, F32, spec)
        if key != "v":
            give("n%s3" % key, res[full].shape, BF16, spec)
    for name in ("block_out", "token_grad", "fin", "cgrad"):
        a = res[name]
        take(name, a, cut)
        give("n_" + name, a.shape, F32 if name in ("fin", "cgrad") else a.dtype, cut)
    onames.append("norm")
    outs.append(jax.ShapeDtypeStruct((1, 1), F32))
    out_specs.append(pl.BlockSpec(memory_space=pltpu.SMEM))
    got = pl.pallas_call(
        functools.partial(adam_kernel, names + onames, len(onames)),
        grid=(steps,), out_shape=outs, in_specs=in_specs, out_specs=out_specs,
        compiler_params=pltpu.CompilerParams(vmem_limit_bytes=int(63.9 * 2**20)),
        name="adam",
    )(*ins)
    got = dict(zip(onames, got))
    new = {key: tuple(got["n%s%d" % (key, k)] for k in range(3 if key == "v" else 4))
           for key in "vioud"}
    for name in ("block_out", "token_grad", "fin", "cgrad"):
        new[name] = got["n_" + name]
    new["norm"] = got["norm"]
    return new


def shards(
    tokens, cotangent, carried, frequencies, vectors, vectors_first, vectors_second,
    mix_in, mix_in_first, mix_in_second, mix_out, mix_out_first, mix_out_second,
    ffn_up, ffn_up_first, ffn_up_second, ffn_down, ffn_down_first, ffn_down_second,
    *, ndp, nmp,
):
    D = tokens.shape[1]
    FH = ffn_up.shape[1]
    args = dict(
        tok=tokens, cot=cotangent, carried=carried,
        freq=jnp.swapaxes(frequencies, 1, 2), vec=vectors,
        w_in=mix_in.reshape(2 * D, 128), w_out=mix_out, w_up=ffn_up, w_down=ffn_down)
    res = layer_call(ndp, nmp, args, args)
    flat = (2 * D, 128)
    params = dict(
        v=(vectors, vectors_first, vectors_second),
        i=tuple(a.reshape(flat) for a in (mix_in, mix_in_first, mix_in_second)),
        o=(mix_out, mix_out_first, mix_out_second),
        u=(ffn_up, ffn_up_first, ffn_up_second),
        d=(ffn_down, ffn_down_first, ffn_down_second))
    new = adam_call(res, params)
    shape = mix_in.shape
    return (
        new["block_out"], new["fin"].reshape(carried.shape), new["token_grad"],
        new["cgrad"].reshape(carried.shape), new["norm"][0, 0],
        *new["v"], *(a.reshape(shape) for a in new["i"]), *new["o"], *new["u"], *new["d"])


def solution(mesh):
    tok = P(("dp", "mp"), None)
    car = P("dp", "mp", None, None, None)
    head = P(None, "mp", None)
    rowp = P("mp", None)
    colp = P(None, "mp")
    rep = P()
    in_specs = (tok, tok, car, rep, rep, rep, rep) + (head,) * 3 + (rowp,) * 3 + (
        colp,) * 3 + (rowp,) * 3
    out_specs = (tok, car, tok, car, rep, rep, rep, rep) + (head,) * 4 + (rowp,) * 4 + (
        colp,) * 4 + (rowp,) * 4
    body = functools.partial(shards, ndp=mesh.shape["dp"], nmp=mesh.shape["mp"])
    return jax.shard_map(body, mesh=mesh, in_specs=in_specs, out_specs=out_specs, check_vma=False)
```
